32 devices in a mesh: psg: 4 (over x, core), batch: 8 (over z, y).
Axes of the slice: x: 2, y: 2, z: 4, core: 2. Of those that a mesh axis runs over, the one named last changes fastest.
Arguments:
- decoder_in: bfloat16 [8, 128, 768], P('batch'), may hold values from -6 to 6
- encoded: bfloat16 [8, 3840, 768], P('batch', 'psg'), may hold values from -6 to 6
- cotangent: bfloat16 [8, 128, 768], P('batch'), may hold values from -6 to 6
- task_ids: int32 [8], P('batch'), may hold values from 0 to 2
- task_embed: bfloat16 [3, 768], P(None, ('psg', 'batch')), may hold values from -6 to 6
- gain_self: bfloat16 [768], P(('psg', 'batch')), may hold values from 0.5 to 1.5
- self_query: bfloat16 [768, 768], P(('psg', 'batch')), may hold values from -0.21875 to 0.21875
- self_key: bfloat16 [768, 768], P(('psg', 'batch')), may hold values from -0.21875 to 0.21875
- self_value: bfloat16 [768, 768], P(('psg', 'batch')), may hold values from -0.21875 to 0.21875
- self_output: bfloat16 [768, 768], P(('psg', 'batch')), may hold values from -0.875 to 0.875
- gain_cross: bfloat16 [768], P(('psg', 'batch')), may hold values from 0.5 to 1.5
- cross_query: bfloat16 [768, 768], P(('psg', 'batch')), may hold values from -0.21875 to 0.21875
- cross_key: bfloat16 [768, 768], P(('psg', 'batch')), may hold values from -0.21875 to 0.21875
- cross_value: bfloat16 [768, 768], P(('psg', 'batch')), may hold values from -0.21875 to 0.21875
- cross_output: bfloat16 [768, 768], P(('psg', 'batch')), may hold values from -6 to 6
- gain_hidden: bfloat16 [768], P(('psg', 'batch')), may hold values from 0.5 to 1.5
- hidden_in: bfloat16 [768, 3072], P('batch', 'psg'), may hold values from -0.21875 to 0.21875
- hidden_out: bfloat16 [3072, 768], P('psg', 'batch'), may hold values from -0.109375 to 0.109375
Outputs:
- block_out: bfloat16 [8, 128, 768], P('batch')
- grad_decoder: float32 [8, 128, 768], P('batch')
- grad_encoded: float32 [8, 3840, 768], P('batch', 'psg')
- grad_task_embed: float32 [3, 768], P(None, ('psg', 'batch'))
- grad_gain_self: float32 [768], P(('psg', 'batch'))
- grad_self_query: float32 [768, 768], P(('psg', 'batch'))
- grad_self_key: float32 [768, 768], P(('psg', 'batch'))
- grad_self_value: float32 [768, 768], P(('psg', 'batch'))
- grad_self_output: float32 [768, 768], P(('psg', 'batch'))
- grad_gain_cross: float32 [768], P(('psg', 'batch'))
- grad_cross_query: float32 [768, 768], P(('psg', 'batch'))
- grad_cross_key: float32 [768, 768], P(('psg', 'batch'))
- grad_cross_value: float32 [768, 768], P(('psg', 'batch'))
- grad_cross_output: float32 [768, 768], P(('psg', 'batch'))
- grad_gain_hidden: float32 [768], P(('psg', 'batch'))
- grad_hidden_in: float32 [768, 3072], P('batch', 'psg')
- grad_hidden_out: float32 [3072, 768], P('psg', 'batch')
The draws below stay inside these ranges and needn't reach their ends.
All inputs are finite; a program needn't handle non-finite values.
Results may differ from the reference program's by a relative error of at most 0.023.
Values may be sent and summed in bfloat16 or wider, within the bound.
A program may use at most 192 MiB of HBM per device.

```python
import jax
import jax.numpy as jnp
from jax import lax

D = 768
HEADS = 12
HEAD = 64
FF = 3072
GROUPS = 3
DEC = 128
PASS_LEN = 192
PASSAGES = 20
QUESTIONS = 8


def with_ends(values, key, low, high):
    spot = [jax.random.randint(jax.random.fold_in(key, axis), (), 0, length) for axis, length in enumerate(values.shape)]
    main_axis = values.shape.index(max(values.shape))
    next_to = spot[:main_axis] + [(spot[main_axis] + 1) % values.shape[main_axis]] + spot[main_axis + 1:]
    return values.at[tuple(spot)].set(low).at[tuple(next_to)].set(high)


def level_of(own_key, shape, shards, low, top_value):
    loudness = 1.0
    for position, blocks in shards:
        steps = jax.random.uniform(jax.random.fold_in(jax.random.fold_in(own_key, 6), position), (blocks,), jnp.float32, low / len(shards), top_value / len(shards))
        loudness = loudness * jnp.repeat(jnp.exp(steps), shape[position] // blocks).reshape((-1,) + (1,) * (len(shape) - 1 - position))
    return loudness


def normal_values(rng, dims, spread, most, cuts=(), held_as=jnp.bfloat16):
    values = jax.random.normal(rng, dims, jnp.float32) * spread
    if len(cuts) > 0:
        values = level_of(rng, dims, cuts, -0.22, 0.18) * values
    return jnp.clip(values, min=-most, max=most).astype(held_as)


def setup_inputs(seed: int = 0) -> dict:
    arg_keys = jax.random.split(jax.random.key(seed), 19)
    return {
        "decoder_in": normal_values(arg_keys[0], (QUESTIONS, DEC, D), 1.0, 6.0, ((0, 8),)),
        "encoded": normal_values(arg_keys[1], (QUESTIONS, PASSAGES * PASS_LEN, D), 1.0, 6.0, ((0, 8), (1, 4))),
        "cotangent": normal_values(arg_keys[2], (QUESTIONS, DEC, D), 1.0, 6.0, ((0, 8),)),
        "task_ids": with_ends(jax.random.randint(arg_keys[3], (QUESTIONS,), 0, GROUPS), jax.random.fold_in(arg_keys[3], 1), 0, GROUPS - 1).astype(jnp.int32),
        "task_embed": normal_values(arg_keys[4], (GROUPS, D), 1.0, 6.0, ((1, 32),)),
        "gain_self": jnp.clip(1.0 + 0.1 * jax.random.normal(arg_keys[5], (D,), jnp.float32), 0.5, 1.5).astype(jnp.bfloat16),
        "self_query": normal_values(arg_keys[6], (D, D), D ** -0.5, 0.21875, ((0, 32),)),
        "self_key": normal_values(arg_keys[7], (D, D), D ** -0.5, 0.21875, ((0, 32),)),
        "self_value": normal_values(arg_keys[8], (D, D), D ** -0.5, 0.21875, ((0, 32),)),
        "self_output": normal_values(arg_keys[9], (D, D), (max(1, D // 16)) ** -0.5, 0.875, ((0, 32),)),
        "gain_cross": jnp.clip(1.0 + 0.1 * jax.random.normal(arg_keys[10], (D,), jnp.float32), 0.5, 1.5).astype(jnp.bfloat16),
        "cross_query": normal_values(arg_keys[11], (D, D), D ** -0.5, 0.21875, ((0, 32),)),
        "cross_key": normal_values(arg_keys[12], (D, D), D ** -0.5, 0.21875, ((0, 32),)),
        "cross_value": normal_values(arg_keys[13], (D, D), D ** -0.5, 0.21875, ((0, 32),)),
        "cross_output": normal_values(arg_keys[14], (D, D), (max(1, 3 * D // (PASSAGES * PASS_LEN))) ** -0.5, 6.0, ((0, 32),)),
        "gain_hidden": jnp.clip(1.0 + 0.1 * jax.random.normal(arg_keys[15], (D,), jnp.float32), 0.5, 1.5).astype(jnp.bfloat16),
        "hidden_in": normal_values(arg_keys[16], (D, FF), D ** -0.5, 0.21875, ((0, 8), (1, 4))),
        "hidden_out": normal_values(arg_keys[17], (FF, D), FF ** -0.5, 0.109375, ((0, 4), (1, 8))),
    }


@jax.custom_vjp
def low(v):
    return lax.optimization_barrier(v.astype(jnp.bfloat16)).astype(jnp.float32)

@jax.custom_vjp
def low_back(v):
    return v

def low_keep(v):
    return (low(v), None)

def low_pass(kept, grad):
    return (grad,)

def back_keep(v):
    return (v, None)

def back_low(kept, grad):
    return (low(grad),)
low.defvjp(low_keep, low_pass)
low_back.defvjp(back_keep, back_low)

def rounded(values):
    return low_back(low(values))

def matmul(former, latter):
    return jnp.dot(former, latter, precision=lax.Precision.HIGHEST)

def rms_norm(values, scales):
    return values * lax.rsqrt(lax.optimization_barrier(jnp.mean(values * values, -1, keepdims=True)) + 1e-06) * scales

def attend(queries, keys, values, causal):
    length = queries.shape[0]
    span = keys.shape[0]
    query_heads = queries.reshape(length, HEADS, HEAD)
    key_heads = keys.reshape(span, HEADS, HEAD)
    value_heads = values.reshape(span, HEADS, HEAD)
    scores = jnp.einsum('qhe,khe->hqk', query_heads, key_heads, precision=lax.Precision.HIGHEST)
    scores = low_back(scores * HEAD ** (-0.5))
    if causal:
        allowed = jnp.arange(length)[:, None] >= jnp.arange(span)[None, :]
        scores = jnp.where(allowed[None], scores, -1000000000.0)
    highest = lax.optimization_barrier(jnp.max(scores, -1, keepdims=True))
    expo = jnp.exp(scores - highest)
    chances = expo / lax.optimization_barrier(jnp.sum(expo, -1, keepdims=True))
    mixed = jnp.einsum('hqk,khe->qhe', low(chances), value_heads, precision=lax.Precision.HIGHEST)
    return mixed.reshape(length, HEADS * HEAD)

def forward(decoder, encoder, onehot, weights):
    table, gain_one, wq_self, wk_self, wv_self, wo_self, gain_two, wq_cross, wk_cross, wv_cross, wo_cross, gain_three, weight_in, weight_out = weights
    residual_in = decoder + lax.optimization_barrier(jnp.sum(onehot[:, None] * table, 0))[None, :]
    normed_self = low(rms_norm(residual_in, gain_one))
    query_self = rounded(matmul(normed_self, wq_self))
    key_self = rounded(matmul(normed_self, wk_self))
    value_self = rounded(matmul(normed_self, wv_self))
    mixed_self = rounded(attend(query_self, key_self, value_self, True))
    after_self = residual_in + low_back(matmul(mixed_self, wo_self))
    normed_cross = low(rms_norm(after_self, gain_two))
    query_cross = rounded(matmul(normed_cross, wq_cross))
    key_cross = rounded(matmul(encoder, wk_cross))
    value_cross = rounded(matmul(encoder, wv_cross))
    mixed_cross = rounded(attend(query_cross, key_cross, value_cross, False))
    after_cross = after_self + low_back(matmul(mixed_cross, wo_cross))
    normed_hidden = low(rms_norm(after_cross, gain_three))
    pre_act = low_back(matmul(normed_hidden, weight_in))
    activation = low(jax.nn.gelu(pre_act, approximate=True))
    return after_cross + matmul(activation, weight_out)

def reference(decoder_in, encoded, cotangent, task_ids, task_embed, gain_self, self_query, self_key, self_value, self_output, gain_cross, cross_query, cross_key, cross_value, cross_output, gain_hidden, hidden_in, hidden_out):
    weights = tuple((item.astype(jnp.float32) for item in (task_embed, gain_self, self_query, self_key, self_value, self_output, gain_cross, cross_query, cross_key, cross_value, cross_output, gain_hidden, hidden_in, hidden_out)))
    groups = task_embed.shape[0]

    def per_question(running, items):
        decoder, encoder, grad_top, ident = items
        onehot = (jnp.arange(groups, dtype=jnp.int32) == ident).astype(jnp.float32)

        def closed(dec_value, enc_value, params):
            return forward(dec_value, enc_value, onehot, params)
        result, pullback = jax.vjp(closed, decoder.astype(jnp.float32), encoder.astype(jnp.float32), weights)
        grad_dec, grad_enc, grad_params = pullback(grad_top.astype(jnp.float32))
        running = jax.tree.map(lambda former, latter: former + latter, running, grad_params)
        return (running, (result.astype(jnp.bfloat16), grad_dec, grad_enc))
    zeros = jax.tree.map(jnp.zeros_like, weights)
    totals, stacked = lax.scan(per_question, zeros, (decoder_in, encoded, cotangent, task_ids))
    return (stacked[0], stacked[1], stacked[2], totals[0], totals[1], totals[2], totals[3], totals[4], totals[5], totals[6], totals[7], totals[8], totals[9], totals[10], totals[11], totals[12], totals[13])
```

```python
import functools

import jax
import jax.numpy as jnp
from jax import lax
from jax.experimental import pallas as pl
from jax.experimental.pallas import tpu as pltpu
from jax.sharding import PartitionSpec as P

HEADS = 12
EPSILON = 1e-06
MASKED = -1000000000.0
LANES = 128
SMALL_ROWS = 16
MAX_BLOCKS = 32
MIB = 2**20

F32 = jnp.float32
BF16 = jnp.bfloat16
ID = pl.DeviceIdType.MESH
VMEM = pl.BlockSpec(memory_space=pltpu.VMEM)
ANY = pl.BlockSpec(memory_space=pl.ANY)


def nn(former, latter):
    return jnp.dot(former, latter, preferred_element_type=F32)


def nt(former, latter):
    return lax.dot_general(former, latter, (((1,), (1,)), ((), ())), preferred_element_type=F32)


def rms_factor(values):
    return lax.rsqrt(jnp.mean(values * values, -1, keepdims=True) + EPSILON)


def rms_back(values, factor, scales, grad_out):
    scaled = grad_out * scales
    cubed = factor * factor * factor
    return factor * scaled - values * cubed * jnp.mean(scaled * values, -1, keepdims=True)


def lane_is_low():
    return lax.broadcasted_iota(jnp.int32, (1, LANES), 1) < LANES // 2


def stack_heads(pair):
    low = lane_is_low()
    zero = jnp.zeros_like(pair)
    return jnp.concatenate([jnp.where(low, pair, zero), jnp.where(low, zero, pair)], 0)


def merge_heads(stacked):
    half = stacked.shape[0] // 2
    return jnp.where(lane_is_low(), stacked[:half], stacked[half:])


def stack_stat(stats, pair):
    return jnp.concatenate([stats[:, 2 * pair : 2 * pair + 1], stats[:, 2 * pair + 1 : 2 * pair + 2]], 0)


def spread_stat(stats, pair):
    return jnp.where(
        lane_is_low(), stats[:, 2 * pair : 2 * pair + 1], stats[:, 2 * pair + 1 : 2 * pair + 2]
    )


def remote(src, dst, send, recv, device):
    return pltpu.make_async_remote_copy(
        src_ref=src, dst_ref=dst, send_sem=send, recv_sem=recv, device_id=device, device_id_type=ID
    )


def place():
    index, question = lax.axis_index("psg"), lax.axis_index("batch")
    return index, question


def line_barrier(spans, extra):
    index, question = place()
    far, near = question // 2, question % 2
    barrier = pltpu.get_barrier_semaphore()

    @pl.when(far < spans - 1)
    def _():
        pl.semaphore_signal(barrier, inc=1, device_id=(index, question + 2), device_id_type=ID)

    @pl.when(far > 0)
    def _():
        pl.semaphore_signal(barrier, inc=1, device_id=(index, question - 2), device_id_type=ID)

    others = [(index, far * 2 + 1 - near)] + extra
    for other in others:
        pl.semaphore_signal(barrier, inc=1, device_id=other, device_id_type=ID)
    line = jnp.where(far < spans - 1, 1, 0) + jnp.where(far > 0, 1, 0)
    pl.semaphore_wait(barrier, line + len(others))


def gather_kernel(spans, a_ref, f_ref, s_ref, a_out, f_out, s_out, own_sem, *sems):
    a_recv, a_up, a_down, a_y, a_x, a_c, s_recv, s_up, s_down, s_y, s_x, s_c, f_recv, f_up, f_down, f_y = sems
    index, question = place()
    far, near = question // 2, question % 2
    side, core = index // 2, index % 2
    count = spans * 2
    x_peer = (1 - side) * 2 + core
    c_peer = side * 2 + 1 - core
    line_barrier(spans, [(x_peer, question), (c_peer, question)])

    own = [
        pltpu.make_async_copy(a_ref, a_out.at[index, question], own_sem.at[0]),
        pltpu.make_async_copy(s_ref, s_out.at[index, question], own_sem.at[1]),
        pltpu.make_async_copy(f_ref, f_out.at[question], own_sem.at[2]),
    ]
    for copy in own:
        copy.start()

    def ways(block, mine, up, down, across, wide):
        z = block // 2
        kinds = (
            (a_ref, a_out.at[index, block], a_recv.at[index * count + block], a_up, a_down, a_y),
            (s_ref, s_out.at[index, block], s_recv.at[index * count + block], s_up, s_down, s_y),
            (f_ref, f_out.at[block], f_recv.at[block], f_up, f_down, f_y),
        )
        out = []
        for own_ref, spot, recv, sem_up, sem_down, sem_y in kinds:
            src = own_ref if mine else spot
            if up:
                out.append((far < spans - 1, remote(src, spot, sem_up.at[z], recv, (index, question + 2))))
            if down:
                out.append((far > 0, remote(src, spot, sem_down.at[z], recv, (index, question - 2))))
            if across:
                out.append((None, remote(src, spot, sem_y.at[z], recv, (index, far * 2 + 1 - near))))
        return out

    def wides(owner, block, mine, to_x, to_core):
        kinds = (
            (a_ref, a_out.at[owner, block], a_recv.at[owner * count + block], a_x, a_c),
            (s_ref, s_out.at[owner, block], s_recv.at[owner * count + block], s_x, s_c),
        )
        out = []
        for own_ref, spot, recv, sem_x, sem_c in kinds:
            src = own_ref if mine else spot
            if to_x:
                out.append((None, remote(src, spot, sem_x.at[block], recv, (x_peer, question))))
            if to_core:
                out.append((None, remote(src, spot, sem_c.at[(owner // 2) * count + block], recv, (c_peer, question))))
        return out

    def each(copies, act):
        for when, copy in copies:
            if when is None:
                act(copy)
            else:
                pl.when(when)(functools.partial(act, copy))

    def start(copies):
        each(copies, lambda copy: copy.start())

    def arrived(owner, block, with_f):
        spot = a_out.at[owner, block]
        remote(spot, spot, a_c.at[0], a_recv.at[owner * count + block], (c_peer, question)).wait_recv()
        spot = s_out.at[owner, block]
        remote(spot, spot, s_c.at[0], s_recv.at[owner * count + block], (c_peer, question)).wait_recv()
        if with_f:
            spot = f_out.at[block]
            remote(spot, spot, f_y.at[0], f_recv.at[block], (c_peer, question)).wait_recv()

    start(ways(question, True, True, True, True, True))
    start(wides(index, question, True, True, True))

    def from_y(z):
        block = z * 2 + 1 - near
        arrived(index, block, True)
        start(wides(index, block, False, True, True))

    def from_x(block):
        arrived(x_peer, block, False)
        start(wides(x_peer, block, False, False, True))

    from_y(far)
    from_x(question)
    for step in range(1, spans):
        for sign in (-1, 1):
            z = far + sign * step
            block = z * 2 + near

            @pl.when((z >= 0) & (z < spans))
            def _(z=z, block=block, sign=sign):
                arrived(index, block, True)
                start(ways(block, False, sign < 0, sign > 0, True, True))
                start(wides(index, block, False, True, True))

        for sign in (-1, 1):
            z = far + sign * step

            @pl.when((z >= 0) & (z < spans))
            def _(z=z):
                from_y(z)

        if step == 1:
            from_x(far * 2 + 1 - near)
        for sign in (-1, 1):
            z = far + sign * step

            @pl.when((z >= 0) & (z < spans))
            def _(z=z):
                from_x(z * 2 + near)

    for step in range(1, spans):
        for sign in (-1, 1):
            z = far + sign * step

            @pl.when((z >= 0) & (z < spans))
            def _(z=z):
                from_x(z * 2 + 1 - near)

    for block in range(count):
        arrived(c_peer, block, False)
        arrived((1 - side) * 2 + 1 - core, block, False)

    for copy in own:
        copy.wait()

    def done(copies):
        each(copies, lambda copy: copy.wait_send())

    done(ways(question, True, True, True, True, True))
    done(wides(index, question, True, True, True))
    for step in range(1, spans):
        for sign in (-1, 1):
            z = far + sign * step

            @pl.when((z >= 0) & (z < spans))
            def _(z=z, sign=sign):
                done(ways(z * 2 + near, False, sign < 0, sign > 0, True, True))
                done(wides(index, z * 2 + near, False, True, True))

    for z in range(spans):
        done(wides(index, z * 2 + 1 - near, False, True, True))
    for block in range(count):
        done(wides(x_peer, block, False, False, True))


def gather_all(attn, hidden, small, psg, batch):
    if not regular(attn.shape[0] // 8, psg, batch):
        return (
            lax.all_gather(lax.all_gather(attn, "batch"), "psg"),
            lax.all_gather(hidden, "batch"),
            lax.all_gather(lax.all_gather(small, "batch"), "psg"),
        )
    spans = batch // 2
    dma = pltpu.SemaphoreType.DMA
    wide = [dma((psg * batch,))] + [dma((spans,))] * 3 + [dma((batch,)), dma((2 * batch,))]
    return pl.pallas_call(
        functools.partial(gather_kernel, spans),
        out_shape=(
            jax.ShapeDtypeStruct((psg, batch) + attn.shape, attn.dtype),
            jax.ShapeDtypeStruct((batch,) + hidden.shape, hidden.dtype),
            jax.ShapeDtypeStruct((psg, batch) + small.shape, small.dtype),
        ),
        in_specs=[ANY] * 3,
        out_specs=[ANY] * 3,
        scratch_shapes=[dma((3,))] + wide + wide + [dma((batch,))] + [dma((spans,))] * 3,
        compiler_params=pltpu.CompilerParams(collective_id=0, has_side_effects=True),
        name="gather_weights",
    )(attn, hidden, small)


def regular(owned, psg, batch):
    return psg == 4 and batch % 2 == 0 and psg * batch <= MAX_BLOCKS and owned % 8 == 0


def psg_start(psg, parts, send, recv):
    me, question = place()
    for hop in range(1, psg):
        peer = lax.rem(me + hop, psg)
        for row, (src, dst, scatter) in enumerate(parts):
            source = src.at[peer] if scatter else src
            remote(source, dst.at[me], send.at[row, hop], recv.at[row, me], (peer, question)).start()


def psg_wait(psg, parts, send, recv):
    me, question = place()
    for hop in range(1, psg):
        peer = lax.rem(me + hop, psg)
        for row, (src, dst, scatter) in enumerate(parts):
            source = src.at[peer] if scatter else src
            remote(source, dst.at[peer], send.at[row, hop], recv.at[row, peer], (peer, question)).wait_recv()
    for hop in range(1, psg):
        peer = lax.rem(me + hop, psg)
        for row, (src, dst, scatter) in enumerate(parts):
            source = src.at[peer] if scatter else src
            remote(source, dst.at[me], send.at[row, hop], recv.at[row, me], (peer, question)).wait_send()


def psg_barrier(psg):
    me, question = place()
    barrier = pltpu.get_barrier_semaphore()
    for hop in range(1, psg):
        pl.semaphore_signal(
            barrier, inc=1, device_id=(lax.rem(me + hop, psg), question), device_id_type=ID
        )
    pl.semaphore_wait(barrier, psg - 1)


def reduce_kernel(spans, kv_ref, a_ref, f_ref, s_ref, kv_out, a_out, f_out, s_out,
                  kv_core, kv_x, kv_mid, kv_acc, s_buf, s_recv, x_sem, s_sem, *rest):
    names = ("from_y", "acc", "from_up", "from_down", "y_send", "y_recv", "line_send", "up_recv", "down_recv")
    kv_kit, a_kit, f_kit = [dict(zip(names, rest[i * len(names) :])) for i in range(3)]
    index, question = place()
    far, near = question // 2, question % 2
    side, core = index // 2, index % 2
    x_peer = (1 - side) * 2 + core
    c_peer = side * 2 + 1 - core
    y_peer = far * 2 + 1 - near
    barrier = pltpu.get_barrier_semaphore()
    column = [(index, lax.rem(far + hop, spans) * 2 + near) for hop in range(1, spans)]
    greeted = column + [(index, y_peer), (x_peer, question), (c_peer, question)]
    for other in greeted:
        pl.semaphore_signal(barrier, inc=1, device_id=other, device_id_type=ID)
    pl.semaphore_wait(barrier, len(greeted))

    def y_copy(src, kit, z):
        return remote(
            src.at[z * 2 + 1 - near], kit["from_y"].at[z], kit["y_send"].at[z], kit["y_recv"].at[z], (index, y_peer)
        )

    def line(kit, z, up):
        slot, recv = (kit["from_up"], kit["up_recv"]) if up else (kit["from_down"], kit["down_recv"])
        return remote(
            kit["acc"].at[z], slot.at[z], kit["line_send"].at[z], recv.at[z],
            (index, question + 2 if up else question - 2),
        )

    def own_sum(src, kit, z):
        y_copy(src, kit, z).wait_recv()
        return src[z * 2 + near].astype(F32) + kit["from_y"][z].astype(F32)

    def along(src, kit):
        for step in range(spans):
            for up, z in ((False, step), (True, spans - 1 - step)):
                behind = far > 0 if up else far < spans - 1

                @pl.when(z > far if up else z < far)
                def _(z=z, up=up, behind=behind):
                    total = own_sum(src, kit, z)

                    @pl.when(behind)
                    def _():
                        line(kit, z, up).wait_recv()
                        slot = kit["from_up"] if up else kit["from_down"]
                        kit["acc"][z] = (total + slot[z].astype(F32)).astype(BF16)

                    @pl.when(jnp.logical_not(behind))
                    def _():
                        kit["acc"][z] = total.astype(BF16)

                    line(kit, z, up).start()

    def finish(src, kit, out):
        out[...] = own_sum(src, kit, far)

        @pl.when(far < spans - 1)
        def _():
            line(kit, far, False).wait_recv()
            out[...] = out[...] + kit["from_down"][far].astype(F32)

        @pl.when(far > 0)
        def _():
            line(kit, far, True).wait_recv()
            out[...] = out[...] + kit["from_up"][far].astype(F32)

    def sent(src, kit):
        for z in range(spans):
            y_copy(src, kit, z).wait_send()
            pl.when(z < far)(lambda z=z: line(kit, z, False).wait_send())
            pl.when(z > far)(lambda z=z: line(kit, z, True).wait_send())

    order = [z for step in range((spans + 1) // 2) for z in sorted({step, spans - 1 - step})]

    def y_start(src, kit):
        for z in order:
            y_copy(src, kit, z).start()

    def pair(slot, device):
        return remote(s_buf.at[slot], s_recv.at[slot], s_sem.at[0, slot], s_sem.at[1, slot], device)

    def small(z, mine):
        return remote(s_buf.at[3], s_recv.at[3 + mine], s_sem.at[2, z], s_sem.at[3, mine], (index, z * 2 + near))

    s_core, s_x, s_y = pair(0, (c_peer, question)), pair(1, (x_peer, question)), pair(2, (index, y_peer))
    core_copy = remote(kv_ref.at[1 - core], kv_core, x_sem.at[0], x_sem.at[1], (c_peer, question))
    core_copy.start()
    s_buf[0] = s_ref[...]
    s_core.start()
    y_start(f_ref, f_kit)
    y_start(a_ref, a_kit)

    core_copy.wait()
    kv_mid[...] = (kv_ref[core, 1 - side].astype(F32) + kv_core[1 - side].astype(F32)).astype(BF16)
    x_copy = remote(kv_mid, kv_x, x_sem.at[2], x_sem.at[3], (x_peer, question))
    x_copy.start()
    s_core.wait()
    s_buf[1] = s_buf[0] + s_recv[0]
    s_x.start()
    x_copy.wait()
    kv_acc[...] = (
        kv_ref[core, side].astype(F32) + kv_core[side].astype(F32) + kv_x[...].astype(F32)
    ).astype(BF16)
    y_start(kv_acc, kv_kit)
    s_x.wait()
    s_buf[2] = s_buf[1] + s_recv[1]
    s_y.start()

    along(f_ref, f_kit)
    s_y.wait()
    s_buf[3] = s_buf[2] + s_recv[2]
    for hop in range(1, spans):
        small(lax.rem(far + hop, spans), far).start()
    along(a_ref, a_kit)
    along(kv_acc, kv_kit)
    finish(f_ref, f_kit, f_out)
    finish(a_ref, a_kit, a_out)
    finish(kv_acc, kv_kit, kv_out)
    s_out[...] = s_buf[3]
    for hop in range(1, spans):
        z = lax.rem(far + hop, spans)
        small(z, z).wait_recv()
        s_out[...] = s_out[...] + s_recv[3 + z]
    for hop in range(1, spans):
        small(lax.rem(far + hop, spans), far).wait_send()
    for src, kit in ((f_ref, f_kit), (a_ref, a_kit), (kv_acc, kv_kit)):
        sent(src, kit)


def reduce_all(kv, attn, hidden, small, psg, batch):
    width = attn.shape[-1]
    if not regular(attn.shape[1] // 6, psg, batch):
        both = ("psg", "batch")
        return (
            lax.psum_scatter(kv.reshape((-1,) + kv.shape[2:]).astype(F32), both, tiled=True)[0],
            lax.psum_scatter(attn.astype(F32), "batch", tiled=True)[0],
            lax.psum_scatter(hidden.astype(F32), "batch", tiled=True)[0],
            lax.psum(small, both),
        )
    spans = batch // 2
    dma = pltpu.SemaphoreType.DMA

    def kit(rows):
        return [pltpu.VMEM((spans, rows, width), BF16)] * 4 + [dma((spans,))] * 5

    rows = [value.shape[-2] for value in (kv, attn, hidden)]
    block = (batch, rows[0], width)
    cored = jnp.swapaxes(kv.reshape((psg // 2, 2) + block), 0, 1)
    return pl.pallas_call(
        functools.partial(reduce_kernel, spans),
        out_shape=tuple(jax.ShapeDtypeStruct((n, width), F32) for n in rows + [small.shape[0]]),
        in_specs=[VMEM] * 4,
        out_specs=[VMEM] * 4,
        scratch_shapes=[
            pltpu.VMEM((2,) + block, BF16),
            pltpu.VMEM(block, BF16),
            pltpu.VMEM(block, BF16),
            pltpu.VMEM(block, BF16),
            pltpu.VMEM((4,) + small.shape, F32),
            pltpu.VMEM((3 + spans,) + small.shape, F32),
            dma((4,)),
            dma((4, max(spans, 3))),
        ] + kit(rows[0]) + kit(rows[1]) + kit(rows[2]),
        compiler_params=pltpu.CompilerParams(collective_id=1, has_side_effects=True, vmem_limit_bytes=48 * MIB),
        name="reduce_grads",
    )(cored, attn, hidden, small)


def self_forward(dec, row, g1, wq, wk, wv, wo, g2, wcq, res, n1, q, k, v, probs, mix, after, n2, qc):
    x = dec[...].astype(F32) + row[...]
    res[...] = x
    normed = (x * rms_factor(x) * g1[...]).astype(BF16)
    n1[...] = normed
    q[...] = nn(normed, wq[...]).astype(BF16)
    k[...] = nn(normed, wk[...]).astype(BF16)
    v[...] = nn(normed, wv[...]).astype(BF16)
    tokens, width = x.shape
    scale = (width // HEADS) ** (-0.5)
    rows = lax.broadcasted_iota(jnp.int32, (2 * tokens, tokens), 0) % tokens
    causal = rows >= lax.broadcasted_iota(jnp.int32, (2 * tokens, tokens), 1)
    for pair in range(HEADS // 2):
        cols = slice(pair * LANES, (pair + 1) * LANES)
        scores = jnp.where(causal, nt(stack_heads(q[:, cols]), k[:, cols]) * scale, MASKED)
        expo = jnp.exp(scores - jnp.max(scores, -1, keepdims=True))
        chances = expo * (1.0 / jnp.sum(expo, -1, keepdims=True))
        probs[pair] = chances
        mix[:, cols] = merge_heads(nn(chances.astype(BF16), v[:, cols])).astype(BF16)
    y = x + nn(mix[...], wo[...])
    after[...] = y
    crossed = (y * rms_factor(y) * g2[...]).astype(BF16)
    n2[...] = crossed
    qc[...] = nn(crossed, wcq[...]).astype(BF16)


def cross_forward(enc, wk, wv, qc, key, val, probs, out, stat):
    tokens, width = qc.shape
    length = enc.shape[0]
    scale = (width // HEADS) ** (-0.5)
    step = 256
    for first in range(0, width, step):
        cols = slice(first, first + step)
        key[:, cols] = nn(enc[...], wk[:, cols]).astype(BF16)
        val[:, cols] = nn(enc[...], wv[:, cols]).astype(BF16)
    lane = lax.broadcasted_iota(jnp.int32, (tokens, LANES), 1)
    tops = jnp.zeros((tokens, LANES), F32)
    sums = jnp.ones((tokens, LANES), F32)
    for pair in range(HEADS // 2):
        cols = slice(pair * LANES, (pair + 1) * LANES)
        scores = nt(stack_heads(qc[:, cols]), key[:, cols]) * scale
        top = jnp.max(scores, -1, keepdims=True)
        expo = jnp.exp(scores - top)
        total = jnp.sum(expo, -1, keepdims=True)
        low = expo.astype(BF16)
        probs[pair] = low
        mixed = nn(low, val[:, cols]) * (1.0 / total)
        out[:, cols] = merge_heads(mixed).astype(BF16)
        for half in range(2):
            part = slice(half * tokens, (half + 1) * tokens)
            here = lane == 2 * pair + half
            tops = jnp.where(here, top[part], tops)
            sums = jnp.where(here, total[part], sums)
    stat[:, :LANES] = tops
    stat[:, LANES:] = sums


def cross_combine(psg, out, stat, after, wo, g3, both, log_total, mixed_rows, after_rows,
                  r_out, r_stat, buf, send, recv):
    me, question = place()
    psg_barrier(psg)
    parts = [(out, r_out, True), (stat, r_stat, True)]
    psg_start(psg, parts, send, recv)
    r_out[me] = out[me]
    r_stat[me] = stat[me]
    psg_wait(psg, parts, send, recv)
    tops = [r_stat[p, :, :LANES] for p in range(psg)]
    top = functools.reduce(jnp.maximum, tops)
    shares = [jnp.exp(tops[p] - top) * r_stat[p, :, LANES:] for p in range(psg)]
    total = functools.reduce(jnp.add, shares)
    log_total[me] = top + jnp.log(total)
    inverse = 1.0 / total
    shares = [share * inverse for share in shares]
    width = out.shape[-1]
    for pair in range(HEADS // 2):
        cols = slice(pair * LANES, (pair + 1) * LANES)
        mixed = jnp.zeros(shares[0].shape, F32)
        for p in range(psg):
            mixed = mixed + spread_stat(shares[p], pair) * r_out[p, :, cols].astype(F32)
        mixed_rows[:, cols] = mixed
        both[me, :, width + pair * LANES : width + (pair + 1) * LANES] = mixed.astype(BF16)
    y = after[me] + nn(mixed_rows[...].astype(BF16), wo[...])
    after_rows[...] = y
    both[me, :, :width] = (y * rms_factor(y) * g3[...]).astype(BF16)
    buf[...] = both[me]
    parts = [(buf, both, False), (log_total.at[me], log_total, False)]
    psg_start(psg, parts, send.at[2:4], recv.at[2:4])
    psg_wait(psg, parts, send.at[2:4], recv.at[2:4])


def feed_forward(normed, cot, w_in, w_out, out, dnorm, grads):
    x = normed[...]
    top = cot[...]
    pre = nn(x, w_in[...])
    root = (2.0 / jnp.pi) ** 0.5
    square = pre * pre
    bend = jnp.tanh(root * (pre + 0.044715 * (square * pre)))
    act = (0.5 * pre * (1.0 + bend)).astype(BF16)
    slope = 0.5 * (1.0 + bend) + 0.5 * pre * (1.0 - bend * bend) * (root * (1.0 + 3 * 0.044715 * square))
    out[...] = nt(act, w_out[...]).astype(BF16)
    dpre = (nn(top, w_out[...]) * slope).astype(BF16)
    dnorm[...] = nt(dpre, w_in[...]).astype(BF16)
    batch, double, _ = grads.shape
    rows = double // 2
    width = x.shape[1]
    x_turned = x.T
    top_turned = top.T
    step = 256 if width % 256 == 0 else width
    g_in = nn(x_turned, dpre).astype(BF16)
    g_out = nn(top_turned, act).astype(BF16)
    for b in range(batch):
        grads[b, :rows] = g_in[b * rows : (b + 1) * rows]
        grads[b, rows:] = g_out[b * rows : (b + 1) * rows]


def hidden_combine(psg, out, dnorm, cot, after_rows, mixed_rows, wo, g3, wide, dots, grad_after, gain,
                   r_out, r_dnorm, buf, send, recv):
    me, question = place()
    psg_barrier(psg)
    parts = [(dnorm, r_dnorm, True), (out, r_out, True)]
    psg_start(psg, parts, send, recv)
    r_out[me] = out[me]
    r_dnorm[me] = dnorm[me]
    y = after_rows[...]
    factor = rms_factor(y)
    psg_wait(psg, parts, send, recv)
    width = y.shape[1]
    upstream = functools.reduce(jnp.add, [r_dnorm[p].astype(F32) for p in range(psg)])
    hidden = functools.reduce(jnp.add, [r_out[p].astype(F32) for p in range(psg)])
    scales = g3[...]
    gain[...] = jnp.sum(upstream * y * factor, 0, keepdims=True)
    grad = cot[me].astype(F32) + rms_back(y, factor, scales, upstream)
    grad_after[...] = grad
    dcross = grad.astype(BF16)
    dmixed = nt(dcross, wo[...]).astype(BF16)
    product = dmixed.astype(F32) * mixed_rows[...]
    lane = lax.broadcasted_iota(jnp.int32, (product.shape[0], LANES), 1)
    sums = jnp.zeros(lane.shape, F32)
    low = lane_is_low()
    for pair in range(HEADS // 2):
        here = product[:, pair * LANES : (pair + 1) * LANES]
        sums = jnp.where(lane == 2 * pair, jnp.sum(jnp.where(low, here, 0.0), -1, keepdims=True), sums)
        sums = jnp.where(lane == 2 * pair + 1, jnp.sum(jnp.where(low, 0.0, here), -1, keepdims=True), sums)
    dots[me] = sums
    buf[:, :width] = dmixed
    buf[:, width : 2 * width] = dcross
    buf[:, 2 * width :] = (y + hidden).astype(BF16)
    wide[me] = buf[...]
    parts = [(buf, wide, False), (dots.at[me], dots, False)]
    psg_start(psg, parts, send.at[2:4], recv.at[2:4])
    psg_wait(psg, parts, send.at[2:4], recv.at[2:4])


def cross_backward(enc, key, val, wk, wv, qc, dmixed, probs, stat, log_total, dots,
                   grad_enc, g_key, g_val, dquery, dkey_t, dval_t):
    tokens, width = qc.shape
    scale = (width // HEADS) ** (-0.5)
    ratio = jnp.exp(stat[:, :LANES] - log_total[...])
    dot_all = dots[...]
    for pair in range(HEADS // 2):
        cols = slice(pair * LANES, (pair + 1) * LANES)
        q2 = stack_heads(qc[:, cols])
        d2 = stack_heads(dmixed[:, cols])
        chances = probs[pair].astype(F32) * stack_stat(ratio, pair)
        dchance = nt(d2, val[:, cols])
        dscore = (chances * (dchance - stack_stat(dot_all, pair))).astype(BF16)
        dquery[:, cols] = (merge_heads(nn(dscore, key[:, cols])) * scale).astype(BF16)
        dkey_t[cols, :] = (nn(q2.T, dscore) * scale).astype(BF16)
        dval_t[cols, :] = nn(d2.T, chances.astype(BF16)).astype(BF16)
    dkey = dkey_t[...].T
    dval = dval_t[...].T
    step = 256
    enc_t = enc[...].T
    for first in range(0, width, step):
        cols = slice(first, first + step)
        grad_enc[:, cols] = nt(dkey, wk[cols, :]) + nt(dval, wv[cols, :])
    g_key[...] = nn(enc_t, dkey).astype(BF16)
    g_val[...] = nn(enc_t, dval).astype(BF16)


def query_combine(psg, dquery, after, grad_cross, wcq, g2, dq_all, grad_all, gain, r_dq, buf, buf32, send, recv):
    me, question = place()
    psg_barrier(psg)
    parts = [(dquery, r_dq, True)]
    psg_start(psg, parts, send, recv)
    r_dq[me] = dquery[me]
    y = after[me]
    factor = rms_factor(y)
    psg_wait(psg, parts, send, recv)
    total = functools.reduce(jnp.add, [r_dq[p].astype(F32) for p in range(psg)]).astype(BF16)
    upstream = nt(total, wcq[...])
    gain[...] = jnp.sum(upstream * y * factor, 0, keepdims=True)
    grad = grad_cross[...] + rms_back(y, factor, g2[...], upstream)
    buf[...] = total
    buf32[...] = grad
    dq_all[me] = total
    grad_all[me] = grad
    parts = [(buf, dq_all, False), (buf32, grad_all, False)]
    psg_start(psg, parts, send.at[1:3], recv.at[1:3])
    psg_wait(psg, parts, send.at[1:3], recv.at[1:3])


def self_backward(res, n1, q, k, v, probs, mix, n2, g1, wq, wk, wv, wo, grad_after, dq_cross, dcross, mixc,
                  grad_dec, gain, terms, turned, dq, dk, dv):
    me = lax.axis_index("psg")
    grad = grad_after[...]
    tokens, width = grad.shape
    scale = (width // HEADS) ** (-0.5)
    dself = grad.astype(BF16)
    dmixed = nt(dself, wo[...]).astype(BF16)
    for pair in range(HEADS // 2):
        cols = slice(pair * LANES, (pair + 1) * LANES)
        q2 = stack_heads(q[:, cols])
        d2 = stack_heads(dmixed[:, cols])
        chances = probs[pair]
        dchance = nt(d2, v[:, cols])
        dscore = chances * (dchance - jnp.sum(chances * dchance, -1, keepdims=True))
        low = dscore.astype(BF16)
        dq[:, cols] = (merge_heads(nn(low, k[:, cols])) * scale).astype(BF16)
        dk[:, cols] = (nn(low.T, q2) * scale).astype(BF16)
        dv[:, cols] = nn(chances.astype(BF16).T, d2).astype(BF16)
    upstream = nt(dq[...], wq[...]) + nt(dk[...], wk[...]) + nt(dv[...], wv[...])
    x = res[...]
    factor = rms_factor(x)
    grad = grad + rms_back(x, factor, g1[...], upstream)
    grad_dec[...] = grad
    share = tokens // lax.axis_size("psg")
    mine = lax.broadcasted_iota(jnp.int32, (tokens, 1), 0) // share == me
    gain[0:1] = jnp.sum(jnp.where(mine, upstream * x * factor, 0.0), 0, keepdims=True)
    gain[1:2] = jnp.sum(jnp.where(mine, grad, 0.0), 0, keepdims=True)
    rows = terms.shape[1]
    own = pl.ds(pl.multiple_of(me * rows, 16), rows)
    for slot, (left, rights) in enumerate(
        ((n1, (dq, dk, dv)), (mix, (None,)), (n2, (dq_cross,)), (mixc, (dcross,)))
    ):
        turned[slot] = left[...].T
        part = turned[slot, own, :]
        base = (0, 3, 4, 5)[slot]
        for offset, right in enumerate(rights):
            terms[base + offset] = nn(part, dself if right is None else right[...]).astype(BF16)


def call(body, outs, args, scratch=(), limit=40, collective=None):
    params = {"vmem_limit_bytes": limit * MIB}
    if collective is not None:
        params.update(collective_id=collective, has_side_effects=True)
    name = (body.func if isinstance(body, functools.partial) else body).__name__
    return pl.pallas_call(
        body,
        out_shape=tuple(jax.ShapeDtypeStruct(shape, dtype) for shape, dtype in outs),
        in_specs=[VMEM] * len(args),
        out_specs=[VMEM] * len(outs),
        scratch_shapes=list(scratch),
        compiler_params=pltpu.CompilerParams(**params),
        name=name,
    )(*args)


def local(
    psg,
    batch,
    decoder_in,
    encoded,
    cotangent,
    task_ids,
    task_embed,
    gain_self,
    self_query,
    self_key,
    self_value,
    self_output,
    gain_cross,
    cross_query,
    cross_key,
    cross_value,
    cross_output,
    gain_hidden,
    hidden_in,
    hidden_out,
):
    _, tokens, width = decoder_in.shape
    length = encoded.shape[1]
    groups = task_embed.shape[0]
    owned = gain_self.shape[0]
    pairs = HEADS // 2
    decoder, encoder, top = decoder_in[0], encoded[0], cotangent[0]

    attn = jnp.concatenate(
        [self_query, self_key, self_value, self_output, cross_query, cross_output, cross_key, cross_value], 0
    )
    hidden = jnp.concatenate([hidden_in, hidden_out.T], 0)
    gains = jnp.stack([gain_self, gain_cross, gain_hidden])
    small = jnp.zeros((SMALL_ROWS, LANES), BF16)
    small = small.at[:groups, :owned].set(task_embed).at[groups : groups + 3, :owned].set(gains)
    attn, hidden, small = gather_all(attn, hidden, small, psg, batch)
    attn = jnp.moveaxis(attn.reshape(psg, batch, 8, owned, width), 2, 0).reshape(8, width, width)
    wq, wk, wv, wo, wcq, wco, wck, wcv = [attn[i] for i in range(8)]
    hidden = jnp.moveaxis(hidden.reshape(batch, 2, -1, hidden.shape[-1]), 1, 0).reshape(2, width, -1)
    w_in, w_out = hidden[0], hidden[1]
    table = jnp.moveaxis(small[:, :, :, :owned], 2, 0).reshape(SMALL_ROWS, width).astype(F32)
    row = lax.dynamic_slice_in_dim(table, task_ids[0], 1, 0)
    g1, g2, g3 = [table[groups + i : groups + i + 1] for i in range(3)]

    whole = (tokens, width)
    res, n1, q, k, v, probs, mix, after, n2, qc = call(
        self_forward,
        [(whole, F32)] + [(whole, BF16)] * 4 + [((pairs, 2 * tokens, tokens), F32), (whole, BF16), (whole, F32)]
        + [(whole, BF16)] * 2,
        [decoder, row, g1, wq, wk, wv, wo, g2, wcq],
    )
    key, val, cprobs, out, stat = call(
        cross_forward,
        [((length, width), BF16)] * 2 + [((pairs, 2 * tokens, length), BF16), (whole, BF16), ((tokens, 2 * LANES), F32)],
        [encoder, wck, wcv, qc],
    )
    share = tokens // psg
    rows = (psg, share, width)
    dma = pltpu.SemaphoreType.DMA
    both, log_total, mixed_rows, after_rows = call(
        functools.partial(cross_combine, psg),
        [((psg, share, 2 * width), BF16), ((psg, share, LANES), F32), ((share, width), F32), ((share, width), F32)],
        [out.reshape(rows), stat.reshape(psg, share, 2 * LANES), after.reshape(rows), wco, g3],
        [
            pltpu.VMEM(rows, BF16),
            pltpu.VMEM((psg, share, 2 * LANES), F32),
            pltpu.VMEM((share, 2 * width), BF16),
            dma((4, psg)),
            dma((4, psg)),
        ],
        collective=2,
    )
    both = both.reshape(tokens, 2 * width)
    n3, mixc = both[:, :width], both[:, width:]
    hid = w_in.shape[1]
    part, dnorm, hidden_grads = call(
        feed_forward,
        [(whole, BF16), (whole, BF16), ((batch, 2 * width // batch, hid), BF16)],
        [n3, top, w_in, w_out],
    )
    wide, dots, grad_rows, gain_three = call(
        functools.partial(hidden_combine, psg),
        [((psg, share, 3 * width), BF16), ((psg, share, LANES), F32), ((share, width), F32), ((1, width), F32)],
        [part.reshape(rows), dnorm.reshape(rows), top.reshape(rows), after_rows, mixed_rows, wco, g3],
        [
            pltpu.VMEM(rows, BF16),
            pltpu.VMEM(rows, BF16),
            pltpu.VMEM((share, 3 * width), BF16),
            dma((4, psg)),
            dma((4, psg)),
        ],
        collective=3,
    )
    wide = wide.reshape(tokens, 3 * width)
    dmixed, dcross, block_out = [wide[:, i * width : (i + 1) * width] for i in range(3)]
    grad_encoded, g_key, g_val, dquery = call(
        cross_backward,
        [((length, width), F32)] + [((width, width), BF16)] * 2 + [(whole, BF16)],
        [encoder, key, val, wck, wcv, qc, dmixed, cprobs, stat, log_total.reshape(tokens, LANES), dots.reshape(tokens, LANES)],
        [pltpu.VMEM((width, length), BF16)] * 2,
    )
    dq_cross, grad_after, gain_two = call(
        functools.partial(query_combine, psg),
        [(rows, BF16), (rows, F32), ((1, width), F32)],
        [dquery.reshape(rows), after.reshape(rows), grad_rows, wcq, g2],
        [
            pltpu.VMEM(rows, BF16),
            pltpu.VMEM((share, width), BF16),
            pltpu.VMEM((share, width), F32),
            dma((3, psg)),
            dma((3, psg)),
        ],
        collective=4,
    )
    grad_decoder, sums, terms = call(
        self_backward,
        [(whole, F32), ((2, width), F32), ((6, width // psg, width), BF16)],
        [res, n1, q, k, v, probs, mix, n2, g1, wq, wk, wv, wo, grad_after.reshape(whole),
         dq_cross.reshape(whole), dcross, mixc],
        [pltpu.VMEM((4, width, tokens), BF16)] + [pltpu.VMEM(whole, BF16)] * 3,
    )

    kv = jnp.concatenate([g.reshape(psg, batch, owned, width) for g in (g_key, g_val)], 2)
    terms = jnp.moveaxis(terms.reshape(6, batch, owned, width), 0, 1).reshape(batch, 6 * owned, width)
    onehot = (task_ids[0] == jnp.arange(groups, dtype=jnp.int32)).astype(F32)
    sums = jnp.concatenate(
        [onehot[:, None] * sums[1:2], sums[0:1], gain_two, gain_three, jnp.zeros((8 - groups - 3, width), F32)], 0
    )
    kv, terms, hidden_grads, sums = reduce_all(kv, terms, hidden_grads, sums, psg, batch)
    first = (lax.axis_index("psg") * batch + lax.axis_index("batch")) * owned
    sums = lax.dynamic_slice_in_dim(sums, first, owned, 1)
    g_self = [terms[i * owned : (i + 1) * owned] for i in range(6)]
    cut = hidden_grads.shape[0] // 2
    return (
        block_out[None],
        grad_decoder[None],
        grad_encoded[None],
        sums[:groups],
        sums[groups],
        g_self[0],
        g_self[1],
        g_self[2],
        g_self[3],
        sums[groups + 1],
        g_self[4],
        kv[:owned],
        kv[owned:],
        g_self[5],
        sums[groups + 2],
        hidden_grads[:cut],
        hidden_grads[cut:].T,
    )


def solution(mesh):
    line, spread = P("batch", None, None), P("batch", "psg", None)
    flat, rows = P(("psg", "batch")), P(("psg", "batch"), None)
    table, wide, tall = P(None, ("psg", "batch")), P("batch", "psg"), P("psg", "batch")
    return jax.shard_map(
        functools.partial(local, mesh.shape["psg"], mesh.shape["batch"]),
        mesh=mesh,
        in_specs=(line, spread, line, P("batch"), table) + ((flat,) + (rows,) * 4) * 2 + (flat, wide, tall),
        out_specs=(line, line, spread, table) + ((flat,) + (rows,) * 4) * 2 + (flat, wide, tall),
        check_vma=False,
    )
```

```python
import functools
import types

import jax
import jax.numpy as jnp
from jax import lax
from jax.experimental import pallas as pl
from jax.experimental.pallas import tpu as pltpu
from jax.sharding import PartitionSpec as P

HEADS = 12
PASS_LEN = 192
EPSILON = 1e-06
MASKED = -1000000000.0
LANES = 128
MAX_BLOCKS = 32
MIB = 2**20

F32 = jnp.float32
BF16 = jnp.bfloat16
ID = pl.DeviceIdType.MESH

CK, CV, CO, CQ, SO, SQ, SK, SV = range(8)
GATHER = ((CK, 2, False), (SO, 4, False), (CO, 2, True))
REDUCE = ((CO, 1), (CQ, 2), (SQ, 3), (CK, 2))


def nn(former, latter):
    return jnp.dot(former, latter, preferred_element_type=F32)


def nt(former, latter):
    return lax.dot_general(former, latter, (((1,), (1,)), ((), ())), preferred_element_type=F32)


def rms_factor(values):
    return lax.rsqrt(jnp.mean(values * values, -1, keepdims=True) + EPSILON)


def norm_back(values, factor, scales, grad_out):
    scaled = grad_out * scales
    cubed = factor * factor * factor
    return factor * scaled - values * cubed * jnp.mean(scaled * values, -1, keepdims=True)


def lane_is_low():
    return lax.broadcasted_iota(jnp.int32, (1, LANES), 1) < LANES // 2


def stack_heads(pair):
    low = lane_is_low()
    zero = jnp.zeros_like(pair)
    return jnp.concatenate([jnp.where(low, pair, zero), jnp.where(low, zero, pair)], 0)


def merge_heads(stacked):
    half = stacked.shape[0] // 2
    return jnp.where(lane_is_low(), stacked[:half], stacked[half:])


def stack_stat(stats, pair):
    return jnp.concatenate([stats[:, 2 * pair : 2 * pair + 1], stats[:, 2 * pair + 1 : 2 * pair + 2]], 0)


def spread_stat(stats, pair):
    return jnp.where(
        lane_is_low(), stats[:, 2 * pair : 2 * pair + 1], stats[:, 2 * pair + 1 : 2 * pair + 2]
    )


def column_tiles(width, size=256):
    return [slice(first, min(first + size, width)) for first in range(0, width, size)]


def pair_lanes(pair):
    return slice(pair * LANES, (pair + 1) * LANES)


def self_forward(dec, row, g1, wq, wk, wv, wo, g2, res, n1, q, k, v, probs, mix, after, n2):
    x = dec + row
    res[...] = x
    normed = (x * rms_factor(x) * g1).astype(BF16)
    n1[...] = normed
    q[...] = nn(normed, wq).astype(BF16)
    k[...] = nn(normed, wk).astype(BF16)
    v[...] = nn(normed, wv).astype(BF16)
    tokens, width = x.shape
    scale = (width // HEADS) ** (-0.5)
    rows = lax.broadcasted_iota(jnp.int32, (2 * tokens, tokens), 0) % tokens
    causal = rows >= lax.broadcasted_iota(jnp.int32, (2 * tokens, tokens), 1)
    for pair in range(HEADS // 2):
        cols = pair_lanes(pair)
        scores = jnp.where(causal, nt(stack_heads(q[:, cols]), k[:, cols]) * scale, MASKED)
        expo = jnp.exp(scores - jnp.max(scores, -1, keepdims=True))
        chances = expo * (1.0 / jnp.sum(expo, -1, keepdims=True))
        probs[pair] = chances
        mix[:, cols] = merge_heads(nn(chances.astype(BF16), v[:, cols])).astype(BF16)
    y = x + nn(mix[...], wo)
    after[...] = y
    n2[...] = (y * rms_factor(y) * g2).astype(BF16)


def cross_attend(qc, key, val, probs, stat, part):
    tokens, width = qc.shape
    share = tokens // 4
    scale = (width // HEADS) ** (-0.5)
    lane = lax.broadcasted_iota(jnp.int32, (tokens, LANES), 1)
    tops = jnp.zeros((tokens, LANES), F32)
    sums = jnp.ones((tokens, LANES), F32)
    for pair in range(HEADS // 2):
        cols = pair_lanes(pair)
        scores = nt(stack_heads(qc[:, cols]), key[:, cols]) * scale
        top = jnp.max(scores, -1, keepdims=True)
        expo = jnp.exp(scores - top)
        total = jnp.sum(expo, -1, keepdims=True)
        low = expo.astype(BF16)
        probs[pair] = low
        mixed = merge_heads(nn(low, val[:, cols]) * (1.0 / total)).astype(BF16)
        for p in range(4):
            part[p // 2, p % 2, :, cols] = mixed[p * share : (p + 1) * share]
        for half in range(2):
            rows = slice(half * tokens, (half + 1) * tokens)
            here = lane == 2 * pair + half
            tops = jnp.where(here, top[rows], tops)
            sums = jnp.where(here, total[rows], sums)
    for p in range(4):
        rows = slice(p * share, (p + 1) * share)
        stat[p // 2, p % 2, :, :LANES] = tops[rows]
        stat[p // 2, p % 2, :, LANES:] = sums[rows]


def join_parts(o_a, s_a, o_b, s_b, out, stat):
    top_a, top_b = s_a[:, :LANES], s_b[:, :LANES]
    top = jnp.maximum(top_a, top_b)
    w_a = jnp.exp(top_a - top) * s_a[:, LANES:]
    w_b = jnp.exp(top_b - top) * s_b[:, LANES:]
    total = w_a + w_b
    inverse = 1.0 / total
    w_a, w_b = w_a * inverse, w_b * inverse
    for pair in range(HEADS // 2):
        cols = pair_lanes(pair)
        mixed = spread_stat(w_a, pair) * o_a[:, cols].astype(F32) + spread_stat(w_b, pair) * o_b[:, cols].astype(F32)
        out[:, cols] = mixed.astype(out.dtype)
    stat[:, :LANES] = top
    stat[:, LANES:] = total


def feed_forward(x, top, w_in, w_out):
    pre = nn(x, w_in)
    root = (2.0 / jnp.pi) ** 0.5
    square = pre * pre
    bend = jnp.tanh(root * (pre + 0.044715 * (square * pre)))
    act = (0.5 * pre * (1.0 + bend)).astype(BF16)
    slope = 0.5 * (1.0 + bend) + 0.5 * pre * (1.0 - bend * bend) * (root * (1.0 + 3 * 0.044715 * square))
    dpre = (nn(top, w_out) * slope).astype(BF16)
    return act, dpre


def head_sums(product):
    lane = lax.broadcasted_iota(jnp.int32, (product.shape[0], LANES), 1)
    sums = jnp.zeros(lane.shape, F32)
    low = lane_is_low()
    for pair in range(HEADS // 2):
        here = product[:, pair_lanes(pair)]
        sums = jnp.where(lane == 2 * pair, jnp.sum(jnp.where(low, here, 0.0), -1, keepdims=True), sums)
        sums = jnp.where(lane == 2 * pair + 1, jnp.sum(jnp.where(low, 0.0, here), -1, keepdims=True), sums)
    return sums


def cross_backward(pair, qc, dmixed, key, val, probs, ratio, dots, part):
    tokens, width = qc.shape
    share = tokens // 4
    scale = (width // HEADS) ** (-0.5)
    cols = pair_lanes(pair)
    q2 = stack_heads(qc[:, cols])
    d2 = stack_heads(dmixed[:, cols])
    chances = probs[pair].astype(F32) * stack_stat(ratio, pair)
    dchance = nt(d2, val[:, cols])
    dscore = (chances * (dchance - stack_stat(dots, pair))).astype(BF16)
    dquery = (merge_heads(nn(dscore, key[:, cols])) * scale).astype(BF16)
    for p in range(4):
        part[p // 2, p % 2, :, cols] = dquery[p * share : (p + 1) * share]
    probs[pair, :LANES] = (nn(q2.T, dscore) * scale).astype(BF16)
    probs[pair, LANES:] = nn(d2.T, chances.astype(BF16)).astype(BF16)


def self_backward(dmixed, q, k, v, probs, dq, dk, dv):
    width = q.shape[1]
    scale = (width // HEADS) ** (-0.5)
    for pair in range(HEADS // 2):
        cols = pair_lanes(pair)
        q2 = stack_heads(q[:, cols])
        d2 = stack_heads(dmixed[:, cols])
        chances = probs[pair]
        dchance = nt(d2, v[:, cols])
        dscore = chances * (dchance - jnp.sum(chances * dchance, -1, keepdims=True))
        low = dscore.astype(BF16)
        dq[:, cols] = (merge_heads(nn(low, k[:, cols])) * scale).astype(BF16)
        dk[:, cols] = (nn(low.T, q2) * scale).astype(BF16)
        dv[:, cols] = nn(chances.astype(BF16).T, d2).astype(BF16)


INPUTS = ["tid", "dec", "cot", "enc", "table", "g_one", "g_two", "g_three", "sq", "sk", "sv", "so", "cq", "co", "ck", "cv", "h_in", "h_out"]
OUTPUTS = ["block_out", "grad_dec", "grad_enc", "g_attn", "g_in", "g_out", "g_vec"]


def buffers(psg, batch, tokens, length, width, owned, hidden):
    spans, pairs, share, half = batch // 2, HEADS // 2, tokens // psg, width // 2
    dma = pltpu.SemaphoreType.DMA
    whole = (tokens, width)
    quad = (2, 2, share)
    band = 2 * owned
    runs = len(GATHER)

    def low(*shape):
        return pltpu.VMEM(shape, BF16)

    def full(*shape):
        return pltpu.VMEM(shape, F32)

    out = dict(
        w=low(8, 2, 2 * batch * owned, width),
        f=low(2, width, hidden // 2),
        m_send=low(4, band, half),
        m_recv=low(4, band, half),
        v_buf=full(4, 8, width),
        v_recv=full(3 + spans, 8, width),
        cots=low(2, tokens, width),
        key=low(length, width),
        val=low(length, width),
        c_probs=low(pairs, 2 * tokens, length),
        s_probs=full(pairs, 2 * tokens, tokens),
        res=full(*whole),
        after=full(*whole),
        n1=low(*whole),
        n2=low(*whole),
        q=low(*whole),
        k=low(*whole),
        v=low(*whole),
        mix=low(*whole),
        qc=low(*whole),
        o_part=low(*quad, width),
        o_stat=full(*quad, 2 * LANES),
        o_core=low(2, share, width),
        o_core_stat=full(2, share, 2 * LANES),
        o_to=low(share, width),
        o_to_stat=full(share, 2 * LANES),
        o_mid=full(share, width),
        o_mid_stat=full(share, 2 * LANES),
        o_x=low(share, width),
        o_x_stat=full(share, 2 * LANES),
        mixed_rows=full(share, width),
        stat_rows=full(share, 2 * LANES),
        after_rows=full(share, width),
        n3=low(2, *quad, width),
        mixc=low(*quad, width),
        log_total=full(*quad, LANES),
        dn=low(2, *quad, width),
        dn_core=low(2, 2, share, width),
        dn_to=low(3, share, width),
        dn_got=low(3, share, width),
        hp=low(2, *quad, width),
        hp_core=low(2, 2, share, width),
        hp_to=low(3, share, width),
        hp_got=low(3, share, width),
        grad_rows=full(share, width),
        dmixed=low(*quad, width),
        dcross=low(*quad, width),
        dots=full(*quad, LANES),
        dq_part=low(*quad, width),
        dq_core=low(2, share, width),
        dq_to=low(share, width),
        dq_x=low(share, width),
        dqc=low(*quad, width),
        dself=low(*quad, width),
        dself_rest=low(*quad, width),
        dq=low(*whole),
        dk=low(*whole),
        dv=low(*whole),
        turned=low(4, width, tokens),
        gf=low(2, width, hidden // 2),
        gkv=low(2, 2, 2 * batch * owned, width),
        kv_core=low(2, 2, batch * owned, width),
        kv_to=low(2, batch * owned, width),
        kv_x=low(2, batch * owned, width),
        g=low(8, batch * owned, width),
        gains=full(8, width),
        t_buf=full(4, 8, width),
        t_recv=full(3 + spans, 8, width),
        f_swap=low(2, width // batch, hidden // 2),
        f_swapped=low(2, width // batch, hidden // 2),
        f_came=low(spans, 2, width // spans, hidden // 2),
        f_sum=full(2, width // spans, hidden // 2),
        r_sum=full(max(count for _, count in REDUCE), band, half),
        one_send=dma((96,)),
        one_recv=dma((96,)),
        a_recv=dma((runs, psg * batch)),
        a_up=dma((runs, spans)),
        a_down=dma((runs, spans)),
        a_y=dma((runs, spans)),
        a_x=dma((runs, batch)),
        a_c=dma((runs, 2 * batch)),
        w_recv=dma((spans,)),
        w_up=dma((spans,)),
        w_down=dma((spans,)),
        v_sems=dma((2, spans)),
        t_sems=dma((2, spans)),
        f_line=dma((2, spans)),
    )
    for number, (_, count) in enumerate(REDUCE):
        out[f"r{number}_y"] = low(spans, count, band, half)
        out[f"r{number}_came"] = low(spans, count, band, half)
        out[f"r{number}_swap"] = low(count, owned, half)
        out[f"r{number}_swapped"] = low(count, owned, half)
        out[f"r{number}_sems"] = dma((4, spans))
    return out


def block_kernel(names, psg, batch, *refs):
    r = types.SimpleNamespace(**dict(zip(names, refs, strict=True)))
    spans = batch // 2
    index, question = lax.axis_index("psg"), lax.axis_index("batch")
    far, near = question // 2, question % 2
    side, core = index // 2, index % 2
    x_peer = ((1 - side) * 2 + core, question)
    c_peer = (side * 2 + 1 - core, question)
    y_peer = (index, far * 2 + 1 - near)
    d_peer = ((1 - side) * 2 + core, far * 2 + 1 - near)
    column = [(index, lax.rem(far + hop, spans) * 2 + near) for hop in range(1, spans)]
    tokens, width = r.dec.shape
    owned = r.sq.shape[0]
    band, quarter, half = 2 * owned, batch * owned, width // 2
    share = tokens // psg
    fan = width // batch
    shards = (r.ck, r.cv, r.co, r.cq, r.so, r.sq, r.sk, r.sv)
    pairs = HEADS // 2

    def aligned(value, to):
        return value if isinstance(value, int) else pl.multiple_of(value, to)

    def span(start, size, to):
        return pl.ds(aligned(start, to), size)

    def lanes(h):
        return span(h * half, half, LANES)

    sent = []

    def go(copy, when=None):
        if when is None:
            copy.start()
        else:
            pl.when(when)(copy.start)
        sent.append((copy, when))

    def remote(src, dst, send, recv, device):
        return pltpu.make_async_remote_copy(
            src_ref=src, dst_ref=dst, send_sem=send, recv_sem=recv, device_id=device, device_id_type=ID
        )

    numbers = iter(range(96))

    def pair(src, dst, device):
        number = next(numbers)
        copy = remote(src, dst, r.one_send.at[number], r.one_recv.at[number], device)
        go(copy)
        return copy

    barrier = pltpu.get_barrier_semaphore()
    greeted = column + [y_peer, x_peer, c_peer, d_peer]
    for other in greeted:
        pl.semaphore_signal(barrier, inc=1, device_id=other, device_id_type=ID)
    pl.semaphore_wait(barrier, len(greeted))

    def pack(number):
        first, second = shards[2 * number], shards[2 * number + 1]
        both = jnp.concatenate([first[:, lanes(1 - near)].astype(F32), second[:, lanes(1 - near)].astype(F32)], 0)
        r.m_send[number] = both.astype(BF16)

    def exchange(first, count):
        for number in range(first, first + count):
            pack(number)
        return pair(r.m_send.at[first : first + count], r.m_recv.at[first : first + count], y_peer)

    row = core * quarter + far * band

    def join(number):
        other = r.m_recv[number].astype(F32)
        for part in range(2):
            mine = shards[2 * number + part][:, lanes(near)].astype(F32)
            theirs = other[part * owned : (part + 1) * owned]
            block = jnp.where(near == 0, jnp.concatenate([mine, theirs], 0), jnp.concatenate([theirs, mine], 0))
            r.w[2 * number + part, side, span(row, band, 16), lanes(near)] = block.astype(BF16)

    def unit(run, x, c, z, h):
        first, count, joined = GATHER[run]
        rows = span(c * quarter + z * band, band, 16)
        return r.w.at[first : first + count, slice(None) if joined else x, rows, lanes(h)]

    def landing(run, x, c, z, h):
        place = 0 if GATHER[run][2] else x
        return r.a_recv.at[run, (place * 2 + c) * batch + z * 2 + h]

    def hand(run, x, c, z, h, sem, device, when=None):
        spot = unit(run, x, c, z, h)
        go(remote(spot, spot, sem, landing(run, x, c, z, h), device), when)

    def landed(run, x, c, z, h, when=None):
        spot = unit(run, x, c, z, h)
        copy = remote(spot, spot, r.a_up.at[0, 0], landing(run, x, c, z, h), c_peer)
        if when is None:
            copy.wait_recv()
        else:
            pl.when(when)(copy.wait_recv)

    def wide(run, z, h, when=None):
        if not GATHER[run][2]:
            hand(run, side, core, z, h, r.a_x.at[run, z * 2 + h], x_peer, when)
        hand(run, side, core, z, h, r.a_c.at[run, z * 2 + h], c_peer, when)

    def offer(run):
        hand(run, side, core, far, near, r.a_up.at[run, far], (index, question + 2), far < spans - 1)
        hand(run, side, core, far, near, r.a_down.at[run, far], (index, question - 2), far > 0)
        hand(run, side, core, far, near, r.a_y.at[run, far], y_peer)
        wide(run, far, near)

    def inside(z):
        return (z >= 0) & (z < spans)

    def from_y(run, step):
        for sign in (-1, 1) if 0 < step < spans else (1,) if step == 0 else ():
            z = far + sign * step
            valid = inside(z) if step else None
            landed(run, side, core, z, 1 - near, valid)
            wide(run, z, 1 - near, valid)

    def from_line(run, step):
        for sign in (-1, 1) if step < spans else ():
            z = far + sign * step
            valid = inside(z)
            landed(run, side, core, z, near, valid)
            if sign < 0:
                hand(run, side, core, z, near, r.a_up.at[run, z], (index, question + 2), valid & (far < spans - 1))
            else:
                hand(run, side, core, z, near, r.a_down.at[run, z], (index, question - 2), valid & (far > 0))
            hand(run, side, core, z, near, r.a_y.at[run, z], y_peer, valid)
            wide(run, z, near, valid)

    def from_x(run, step):
        for sign in (-1, 1) if 0 < step < spans else (1,) if step == 0 else ():
            z = far + sign * step
            valid = inside(z) if step else None
            for h in (near, 1 - near):
                landed(run, 1 - side, core, z, h, valid)
                hand(run, 1 - side, core, z, h, r.a_c.at[run, batch + z * 2 + h], c_peer, valid)

    def complete(run):
        for z in range(spans):
            for h in range(2):
                landed(run, side, 1 - core, z, h)
                if not GATHER[run][2]:
                    landed(run, 1 - side, 1 - core, z, h)

    def matrix(number):
        return r.w[number].reshape(width, width)

    m_kv = exchange(0, 1)
    m_self = exchange(2, 2)
    m_tail = exchange(1, 1)

    def ladder(buf, recv, sems):
        def first():
            return pair(buf.at[0], recv.at[0], c_peer)

        def second(copy):
            copy.wait_recv()
            buf[1] = (buf[0].astype(F32) + recv[0].astype(F32)).astype(buf.dtype)
            return pair(buf.at[1], recv.at[1], x_peer)

        def third(copy):
            copy.wait_recv()
            buf[2] = (buf[1].astype(F32) + recv[1].astype(F32)).astype(buf.dtype)
            return pair(buf.at[2], recv.at[2], y_peer)

        def fourth(copy):
            copy.wait_recv()
            buf[3] = (buf[2].astype(F32) + recv[2].astype(F32)).astype(buf.dtype)
            for hop in range(1, spans):
                z = lax.rem(far + hop, spans)
                go(remote(buf.at[3], recv.at[3 + far], sems.at[0, z], sems.at[1, far], (index, z * 2 + near)))

        def last():
            total = buf[3].astype(F32)
            for hop in range(1, spans):
                z = lax.rem(far + hop, spans)
                remote(buf.at[3], recv.at[3 + z], sems.at[0, z], sems.at[1, z], c_peer).wait_recv()
                total = total + recv[3 + z].astype(F32)
            return total

        return first, second, third, fourth, last

    device = index * batch + question
    place = jnp.where(
        lax.broadcasted_iota(jnp.int32, (owned, width), 1)
        == lax.broadcasted_iota(jnp.int32, (owned, width), 0) + device * owned,
        1.0,
        0.0,
    ).astype(BF16)
    r.v_buf[0, 0:3] = nn(r.table[...], place)
    for number, gain in enumerate((r.g_one, r.g_two, r.g_three)):
        r.v_buf[0, 3 + number : 4 + number] = nn(gain[...], place)
    r.v_buf[0, 6:8] = jnp.zeros((2, width), F32)
    v_first, v_second, v_third, v_fourth, v_last = ladder(r.v_buf, r.v_recv, r.v_sems)
    v_copy = v_first()

    m_kv.wait_recv()
    join(0)
    offer(0)
    m_self.wait_recv()
    join(2)
    join(3)
    offer(1)
    m_tail.wait_recv()
    join(1)
    own_tail = r.w.at[CO : CO + 2, side, span(row, band, 16), lanes(near)]
    x_tail = pair(own_tail, own_tail, x_peer)
    v_copy = v_second(v_copy)

    cut = r.f.shape[2]
    other_cols = span((1 - near) * cut, cut, LANES)
    own_cols = span(near * cut, cut, LANES)
    own_fan = span(question * fan, fan, 16)
    h_copies = [
        pair(r.h_in.at[:, other_cols], r.f.at[0, own_fan], y_peer),
        pair(r.h_out.at[:, other_cols], r.f.at[1, own_fan], y_peer),
    ]
    r.f[0, own_fan] = r.h_in[:, own_cols]
    r.f[1, own_fan] = r.h_out[:, own_cols]
    r.cots[near] = r.cot[...]

    def f_unit(z):
        return r.f.at[:, span(z * 2 * fan, 2 * fan, 16), :]

    def f_hand(z, sem, device, when):
        go(remote(f_unit(z), f_unit(z), sem, r.w_recv.at[z], device), when)

    def f_landed(step):
        for sign in (-1, 1) if step < spans else ():
            z = far + sign * step
            pl.when(inside(z))(remote(f_unit(z), f_unit(z), r.w_up.at[0], r.w_recv.at[z], c_peer).wait_recv)
            if sign < 0:
                f_hand(z, r.w_up.at[z], (index, question + 2), inside(z) & (far < spans - 1))
            else:
                f_hand(z, r.w_down.at[z], (index, question - 2), inside(z) & (far > 0))

    from_y(0, 0)
    from_y(1, 0)
    from_line(0, 1)
    from_line(1, 1)
    x_tail.wait_recv()
    offer(2)
    from_y(0, 1)
    from_y(1, 1)
    v_copy = v_third(v_copy)
    from_x(0, 0)
    from_x(1, 0)
    from_line(0, 2)
    from_line(1, 2)
    from_y(2, 0)
    from_line(2, 1)
    for copy in h_copies:
        copy.wait_recv()
    f_hand(far, r.w_up.at[far], (index, question + 2), far < spans - 1)
    f_hand(far, r.w_down.at[far], (index, question - 2), far > 0)
    from_y(0, 2)
    from_y(1, 2)
    from_x(0, 1)
    v_fourth(v_copy)
    from_line(0, 3)
    from_line(1, 3)
    from_line(2, 2)
    from_y(2, 1)
    from_x(1, 1)
    from_y(0, 3)
    from_y(1, 3)
    from_x(0, 2)
    from_line(2, 3)
    from_y(2, 2)
    f_landed(1)
    cot_copy = pair(r.cot, r.cots.at[near], y_peer)
    from_x(1, 2)
    from_x(0, 3)
    from_y(2, 3)
    complete(0)
    vectors = v_last()
    for cols in column_tiles(width):
        r.key[:, cols] = nn(r.enc[...], r.w[CK, :, :, cols].reshape(width, -1)).astype(BF16)
        r.val[:, cols] = nn(r.enc[...], r.w[CV, :, :, cols].reshape(width, -1)).astype(BF16)
    f_landed(2)
    from_x(1, 3)
    complete(1)

    gains = [vectors[3 + i : 4 + i] for i in range(3)]
    chosen = r.tid[0]
    row_embed = functools.reduce(
        jnp.add, [vectors[i : i + 1] * jnp.where(chosen == i, 1.0, 0.0).astype(F32) for i in range(3)]
    )
    r.gains[0:3] = vectors[3:6]
    self_forward(
        r.dec[...].astype(F32), row_embed, gains[0], matrix(SQ), matrix(SK), matrix(SV), matrix(SO), gains[1],
        r.res, r.n1, r.q, r.k, r.v, r.s_probs, r.mix, r.after, r.n2,
    )
    complete(2)
    r.qc[...] = nn(r.n2[...], matrix(CQ)).astype(BF16)

    cross_attend(r.qc, r.key, r.val, r.c_probs, r.o_stat, r.o_part)
    first = [pair(r.o_part.at[:, 1 - core], r.o_core, c_peer), pair(r.o_stat.at[:, 1 - core], r.o_core_stat, c_peer)]
    for copy in first:
        copy.wait_recv()
    join_parts(
        r.o_part[1 - side, core], r.o_stat[1 - side, core], r.o_core[1 - side], r.o_core_stat[1 - side],
        r.o_to, r.o_to_stat,
    )
    second = [pair(r.o_to, r.o_x, x_peer), pair(r.o_to_stat, r.o_x_stat, x_peer)]
    join_parts(
        r.o_part[side, core], r.o_stat[side, core], r.o_core[side], r.o_core_stat[side], r.o_mid, r.o_mid_stat
    )
    for copy in second:
        copy.wait_recv()
    join_parts(r.o_mid[...], r.o_mid_stat[...], r.o_x[...], r.o_x_stat[...], r.mixed_rows, r.stat_rows)
    my_rows = span(index * share, share, 16)
    r.log_total[side, core] = r.stat_rows[:, :LANES] + jnp.log(r.stat_rows[:, LANES:])
    mixed_low = r.mixed_rows[...].astype(BF16)
    r.mixc[side, core] = mixed_low
    y = r.after[my_rows, :] + nn(mixed_low, matrix(CO))
    r.after_rows[...] = y
    r.n3[near, side, core] = (y * rms_factor(y) * r.gains[2:3]).astype(BF16)

    def block8(h, x, c):
        return r.n3.at[h, x, c]

    def spread4(buf):
        spot = buf.at[side, core]
        over_x, over_c = pair(spot, spot, x_peer), pair(spot, spot, c_peer)

        def then():
            over_x.wait_recv()
            onward = buf.at[1 - side, core]
            last = pair(onward, onward, c_peer)

            def end():
                over_c.wait_recv()
                last.wait_recv()

            return end

        return then

    mine = block8(near, side, core)
    to_y, to_x, to_d, to_c = [pair(mine, mine, peer) for peer in (y_peer, x_peer, d_peer, c_peer)]
    log_then = spread4(r.log_total)
    mixc_then = spread4(r.mixc)
    onward = [to_c]
    for copy, h, x in ((to_y, 1 - near, side), (to_x, near, 1 - side), (to_d, 1 - near, 1 - side)):
        copy.wait_recv()
        onward.append(pair(block8(h, x, core), block8(h, x, core), c_peer))
    log_end = log_then()
    f_landed(3)
    cot_copy.wait_recv()
    for copy in onward:
        copy.wait_recv()

    x = r.n3[...].reshape(2 * tokens, width)
    top = r.cots[...].reshape(2 * tokens, width)
    act, dpre = feed_forward(x, top, r.f[0], r.f[1])
    r.dn[...] = nt(dpre, r.f[0]).astype(BF16).reshape(r.dn.shape)

    def shrink8(part, got_c, to, got):
        over_c = pair(part.at[:, :, 1 - core], got_c, c_peer)

        def second():
            over_c.wait_recv()

            def total(h, x):
                return part[h, x, core].astype(F32) + got_c[h, x].astype(F32)

            copies = []
            for slot, (h, x, peer) in enumerate(
                ((1 - near, 1 - side, d_peer), (near, 1 - side, x_peer), (1 - near, side, y_peer))
            ):
                to[slot] = total(h, x).astype(BF16)
                copies.append(pair(to.at[slot], got.at[slot], peer))

            def last():
                out = total(near, side)
                for slot, copy in enumerate(copies):
                    copy.wait_recv()
                    out = out + got[slot].astype(F32)
                return out

            return last

        return second

    dn_second = shrink8(r.dn, r.dn_core, r.dn_to, r.dn_got)
    r.hp[...] = nt(act, r.f[1]).astype(BF16).reshape(r.hp.shape)
    dn_last = dn_second()
    hp_second = shrink8(r.hp, r.hp_core, r.hp_to, r.hp_got)
    r.gf[0] = nn(x.T, dpre).astype(BF16)
    r.gf[1] = nn(top.T, act).astype(BF16)

    others = [lax.rem(far + hop, spans) for hop in range(1, spans)]

    def line_kit(came, src, sems):
        def copy(z, slot):
            return remote(src(z), came.at[slot], sems.at[0, z], sems.at[1, slot], (index, z * 2 + near))

        def send(z):
            go(copy(z, far))

        def total(value, out):
            out[...] = value
            for z in others:
                copy(far, z).wait_recv()
                out[...] = out[...] + came[z].astype(F32)

        return send, total

    def f_piece(z):
        return r.gf.at[:, span(z * 2 * fan, 2 * fan, 16), :]

    f_send, f_total = line_kit(r.f_came, f_piece, r.f_line)
    for z in others:
        f_send(z)

    upstream = dn_last()
    y = r.after_rows[...]
    factor = rms_factor(y)
    scales = r.gains[2:3]
    gain_three = jnp.sum(upstream * y * factor, 0, keepdims=True)
    grad = r.cot[my_rows, :].astype(F32) + norm_back(y, factor, scales, upstream)
    r.grad_rows[...] = grad
    low = grad.astype(BF16)
    r.dcross[side, core] = low
    dmixed = nt(low, matrix(CO)).astype(BF16)
    r.dmixed[side, core] = dmixed
    dmixed_then = spread4(r.dmixed)
    r.dots[side, core] = head_sums(dmixed.astype(F32) * r.mixed_rows[...])
    dots_then = spread4(r.dots)
    dcross_then = spread4(r.dcross)
    mixc_end = mixc_then()
    hp_last = hp_second()
    dmixed_end = dmixed_then()
    dots_end = dots_then()
    dcross_end = dcross_then()
    for end in (log_end, mixc_end, dmixed_end, dots_end, dcross_end):
        end()

    def rows_of(ref):
        return ref[...].reshape(tokens, ref.shape[-1])

    def reduce_kit(number):
        first, count = REDUCE[number]
        got_y, sems = getattr(r, f"r{number}_y"), getattr(r, f"r{number}_sems")

        def piece(z, h):
            return r.g.at[first : first + count, span(z * band, band, 16), lanes(h)]

        def y_copy(z):
            return remote(piece(z, 1 - near), got_y.at[z], sems.at[0, z], sems.at[1, z], y_peer)

        send, total = line_kit(getattr(r, f"r{number}_came"), lambda z: got_y.at[z], sems.at[2:4])

        def begin():
            for z in others + [far]:
                go(y_copy(z))

        def value(z):
            y_copy(z).wait_recv()
            mine = r.g[first : first + count, span(z * band, band, 16), lanes(near)]
            return mine.astype(F32) + got_y[z].astype(F32)

        def forward():
            for z in others:
                got_y[z] = value(z).astype(BF16)
                send(z)

        swap, swapped = getattr(r, f"r{number}_swap"), getattr(r, f"r{number}_swapped")
        out = r.g_attn.at[first : first + count]

        def finish():
            sums = r.r_sum.at[:count]

            total(value(far), sums)
            both = sums[...]
            upper, lower = both[:, :owned], both[:, owned:]
            swap[...] = jnp.where(near == 0, lower, upper).astype(BF16)
            copy = pair(swap, swapped, y_peer)
            out[:, :, lanes(near)] = jnp.where(near == 0, upper, lower)

            def end():
                copy.wait_recv()
                out[:, :, lanes(1 - near)] = swapped[...].astype(F32)

            return end

        return begin, forward, finish

    own_rows = span(index * quarter, quarter, 16)

    def turn(slot, value):
        r.turned[slot] = value.T
        return r.turned[slot, own_rows, :]

    co_begin, co_forward, co_finish = reduce_kit(0)
    so_begin, so_forward, so_finish = reduce_kit(1)
    late_begin, late_forward, late_finish = reduce_kit(2)
    kv_begin, kv_forward, kv_finish = reduce_kit(3)
    r.g[CO] = nn(turn(0, rows_of(r.mixc)), rows_of(r.dcross)).astype(BF16)
    co_begin()

    ratio = jnp.exp(rows_of(r.o_stat)[:, :LANES] - rows_of(r.log_total))
    dots = rows_of(r.dots)
    dmixed = rows_of(r.dmixed)
    for number in range(pairs):
        cross_backward(
            number, r.qc, dmixed, r.key, r.val, r.c_probs, ratio, dots, r.dq_part
        )
    q_first = pair(r.dq_part.at[:, 1 - core], r.dq_core, c_peer)
    r.key[...] = r.c_probs[:, :LANES].reshape(width, -1).T
    q_first.wait_recv()
    r.dq_to[...] = (r.dq_part[1 - side, core].astype(F32) + r.dq_core[1 - side].astype(F32)).astype(BF16)
    q_second = pair(r.dq_to, r.dq_x, x_peer)
    r.c_probs[:, :LANES] = r.enc[...].T.reshape(pairs, LANES, -1)
    for cols in column_tiles(width):
        r.gkv[0, :, :, cols] = nn(r.c_probs[:, :LANES].reshape(width, -1), r.key[:, cols]).astype(BF16).reshape(2, 2 * quarter, -1)
    q_second.wait_recv()
    dq_rows = (
        r.dq_part[side, core].astype(F32) + r.dq_core[side].astype(F32) + r.dq_x[...].astype(F32)
    ).astype(BF16)
    r.dqc[side, core] = dq_rows
    upstream = nt(dq_rows, matrix(CQ))
    y = r.after[my_rows, :]
    factor = rms_factor(y)
    gain_two = jnp.sum(upstream * y * factor, 0, keepdims=True)
    grad = r.grad_rows[...] + norm_back(y, factor, r.gains[1:2], upstream)
    low = grad.astype(BF16)
    r.dself[side, core] = low
    dself_then = spread4(r.dself)
    r.dself_rest[side, core] = (grad - low.astype(F32)).astype(BF16)
    rest_then = spread4(r.dself_rest)
    dqc_then = spread4(r.dqc)
    r.val[...] = r.c_probs[:, LANES:].reshape(width, -1).T
    for cols in column_tiles(width):
        r.gkv[1, :, :, cols] = nn(r.c_probs[:, :LANES].reshape(width, -1), r.val[:, cols]).astype(BF16).reshape(2, 2 * quarter, -1)
    kv_first = pair(r.gkv.at[:, :, span((1 - core) * quarter, quarter, 16), :], r.kv_core, c_peer)
    dself_end = dself_then()
    dqc_end = dqc_then()
    rest_end = rest_then()
    co_forward()
    kv_first.wait_recv()
    kv_own = span(core * quarter, quarter, 16)
    r.kv_to[...] = (
        r.gkv[:, 1 - side, kv_own, :].astype(F32) + r.kv_core[:, 1 - side].astype(F32)
    ).astype(BF16)
    kv_second = pair(r.kv_to, r.kv_x, x_peer)
    dself_end()
    dqc_end()

    dself = rows_of(r.dself)
    r.g[SO] = nn(turn(1, r.mix[...]), dself).astype(BF16)
    r.g[CQ] = nn(turn(2, r.n2[...]), rows_of(r.dqc)).astype(BF16)
    so_begin()
    dmixed = nt(dself, matrix(SO)).astype(BF16)
    self_backward(dmixed, r.q, r.k, r.v, r.s_probs, r.dq, r.dk, r.dv)
    normed = turn(3, r.n1[...])
    for number, ref in ((SQ, r.dq), (SK, r.dk), (SV, r.dv)):
        r.g[number] = nn(normed, ref[...]).astype(BF16)
    late_begin()
    rest_end()
    upstream = nt(r.dq[...], matrix(SQ)) + nt(r.dk[...], matrix(SK)) + nt(r.dv[...], matrix(SV))
    x = r.res[...]
    factor = rms_factor(x)
    grad = dself.astype(F32) + rows_of(r.dself_rest).astype(F32) + norm_back(x, factor, r.gains[0:1], upstream)
    r.grad_dec[...] = grad
    mine = lax.broadcasted_iota(jnp.int32, (tokens, 1), 0) // share == index
    task = jnp.sum(jnp.where(mine, grad, 0.0), 0, keepdims=True)
    r.t_buf[0, 0:3] = jnp.concatenate([task * jnp.where(chosen == i, 1.0, 0.0).astype(F32) for i in range(3)], 0)
    r.t_buf[0, 3:4] = jnp.sum(jnp.where(mine, upstream * x * factor, 0.0), 0, keepdims=True)
    r.t_buf[0, 4:5] = gain_two
    r.t_buf[0, 5:6] = gain_three
    r.t_buf[0, 6:8] = jnp.zeros((2, width), F32)
    t_first, t_second, t_third, t_fourth, t_last = ladder(r.t_buf, r.t_recv, r.t_sems)
    t_copy = t_first()
    hidden = hp_last()
    r.block_out[side, core] = (r.after_rows[...] + hidden).astype(BF16)
    out_then = spread4(r.block_out)
    so_forward()
    t_copy = t_second(t_copy)
    for cols in column_tiles(width):
        r.grad_enc[:, cols] = nt(r.key[...], matrix(CK)[cols]) + nt(r.val[...], matrix(CV)[cols])
    late_forward()
    kv_second.wait_recv()
    r.g[CK : CK + 2] = (
        r.gkv[:, side, kv_own, :].astype(F32) + r.kv_core[:, side].astype(F32) + r.kv_x[...].astype(F32)
    ).astype(BF16)
    kv_begin()
    t_copy = t_third(t_copy)
    out_end = out_then()

    f_total(f_piece(far)[...].astype(F32), r.f_sum)
    both = r.f_sum[...]
    upper, lower = both[:, :fan], both[:, fan:]
    r.f_swap[...] = jnp.where(near == 0, lower, upper).astype(BF16)
    f_copy = pair(r.f_swap, r.f_swapped, y_peer)
    kept = jnp.where(near == 0, upper, lower)
    r.g_in[:, own_cols] = kept[0]
    r.g_out[:, own_cols] = kept[1]
    co_end = co_finish()
    so_end = so_finish()
    t_fourth(t_copy)
    kv_forward()
    late_end = late_finish()
    f_copy.wait_recv()
    r.g_in[:, other_cols] = r.f_swapped[0].astype(F32)
    r.g_out[:, other_cols] = r.f_swapped[1].astype(F32)
    kv_end = kv_finish()
    r.g_vec[...] = t_last()
    out_end()
    co_end()
    so_end()
    late_end()
    kv_end()
    for copy, when in sent:
        if when is None:
            copy.wait_send()
        else:
            pl.when(when)(copy.wait_send)


def regular(owned, psg, batch, tokens, width):
    return psg == 4 and batch in (4, 6, 8) and owned % 8 == 0 and tokens % 128 == 0 and (width // 2) % LANES == 0


def fused(psg, batch, decoder_in, encoded, cotangent, task_ids, task_embed, gain_self, self_query, self_key, self_value,
          self_output, gain_cross, cross_query, cross_key, cross_value, cross_output, gain_hidden, hidden_in, hidden_out):
    _, tokens, width = decoder_in.shape
    length = encoded.shape[1]
    groups, owned = task_embed.shape
    hidden = hidden_in.shape[1]
    scratch = buffers(psg, batch, tokens, length, width, owned, hidden)
    names = INPUTS + OUTPUTS + list(scratch)
    vmem = pl.BlockSpec(memory_space=pltpu.VMEM)
    quad = (2, 2, tokens // psg, width)
    block_out, grad_decoder, grad_encoded, g_attn, g_in, g_out, g_vec = pl.pallas_call(
        functools.partial(block_kernel, names, psg, batch),
        out_shape=(
            jax.ShapeDtypeStruct(quad, BF16),
            jax.ShapeDtypeStruct((tokens, width), F32),
            jax.ShapeDtypeStruct((length, width), F32),
            jax.ShapeDtypeStruct((8, owned, width), F32),
            jax.ShapeDtypeStruct((width // batch, hidden), F32),
            jax.ShapeDtypeStruct((width // batch, hidden), F32),
            jax.ShapeDtypeStruct((8, width), F32),
        ),
        in_specs=[pl.BlockSpec(memory_space=pltpu.SMEM)] + [vmem] * (len(INPUTS) - 1),
        out_specs=[vmem] * len(OUTPUTS),
        scratch_shapes=list(scratch.values()),
        compiler_params=pltpu.CompilerParams(collective_id=0, has_side_effects=True, vmem_limit_bytes=56 * MIB),
        name="decoder_block",
    )(task_ids, decoder_in[0], cotangent[0], encoded[0], task_embed, gain_self[None],
      gain_cross[None], gain_hidden[None], self_query, self_key, self_value, self_output,
      cross_query, cross_output, cross_key, cross_value, hidden_in, hidden_out.T)
    first = (lax.axis_index("psg") * batch + lax.axis_index("batch")) * owned
    mine = lax.dynamic_slice_in_dim(g_vec, first, owned, 1)
    return (
        block_out.reshape(decoder_in.shape),
        grad_decoder[None],
        grad_encoded[None],
        mine[:groups],
        mine[groups],
        g_attn[SQ],
        g_attn[SK],
        g_attn[SV],
        g_attn[SO],
        mine[groups + 1],
        g_attn[CQ],
        g_attn[CK],
        g_attn[CV],
        g_attn[CO],
        mine[groups + 2],
        g_in,
        g_out.T,
    )


def rms_norm(values, scales):
    factor = lax.rsqrt(jnp.mean(values * values, -1, keepdims=True) + EPSILON)
    return (values * factor * scales, factor)


def rms_back(values, factor, scales, grad_out):
    scaled = grad_out * scales
    cubed = factor * factor * factor
    lower = factor * scaled - values * cubed * jnp.mean(scaled * values, -1, keepdims=True)
    return (lower, grad_out * values * factor)


def gelu_tanh(values):
    return jax.nn.gelu(values, approximate=True)


def matmul(former, latter):
    return jnp.dot(former, latter, preferred_element_type=jnp.float32)


def inner_rows(former, latter):
    return lax.dot_general(
        former, latter, (((0,), (0,)), ((), ())), preferred_element_type=jnp.float32
    )


def outer_cols(former, latter):
    return lax.dot_general(
        former, latter, (((1,), (1,)), ((), ())), preferred_element_type=jnp.float32
    )


def split_heads(values, questions):
    return values.reshape(questions, values.shape[0] // questions, HEADS, values.shape[1] // HEADS)


def key_blocks(values):
    questions, length, width = values.shape
    shaped = values.reshape(questions, length // PASS_LEN, PASS_LEN, HEADS, width // HEADS)
    return jnp.moveaxis(shaped, 1, 0)


def block_scores(queries, key_block):
    scale = queries.shape[-1] ** (-0.5)
    return (
        jnp.einsum("bqhe,bkhe->bhqk", queries, key_block, preferred_element_type=jnp.float32)
        * scale
    )


def score_stats(queries, keys):
    questions, tokens, heads, width = queries.shape
    initial = (
        jnp.full((questions, heads, tokens), -1e30, jnp.float32),
        jnp.zeros((questions, heads, tokens), jnp.float32),
    )

    def score_advance(running, key_block):
        scores = block_scores(queries, key_block)
        highest = jnp.maximum(running[0], jnp.max(scores, -1))
        totals = running[1] * jnp.exp(running[0] - highest) + jnp.sum(
            jnp.exp(scores - highest[..., None]), -1
        )
        return ((highest, totals), None)

    return lax.scan(score_advance, initial, key_blocks(keys))[0]


def weighted_values(queries, keys, values, log_total):

    def weighted_advance(running, blocks):
        chances = jnp.exp(block_scores(queries, blocks[0]) - log_total[..., None]).astype(
            jnp.bfloat16
        )
        return (
            running
            + jnp.einsum("bhqk,bkhe->bqhe", chances, blocks[1], preferred_element_type=jnp.float32),
            None,
        )

    return lax.scan(
        weighted_advance,
        jnp.zeros(queries.shape, jnp.float32),
        (key_blocks(keys), key_blocks(values)),
    )[0]


def grad_dots(queries, keys, values, log_total, grad_out):
    questions, tokens, heads, width = queries.shape

    def grad_advance(running, blocks):
        chances = jnp.exp(block_scores(queries, blocks[0]) - log_total[..., None])
        dchance = jnp.einsum(
            "bqhe,bkhe->bhqk", grad_out, blocks[1], preferred_element_type=jnp.float32
        )
        return (running + jnp.sum(chances * dchance, -1), None)

    initial = jnp.zeros((questions, heads, tokens), jnp.float32)
    return lax.scan(grad_advance, initial, (key_blocks(keys), key_blocks(values)))[0]


def cross_back(queries, keys, values, log_total, dots, grad_out, with_keys):
    scale = queries.shape[-1] ** (-0.5)

    def cross_advance(running, blocks):
        chances = jnp.exp(block_scores(queries, blocks[0]) - log_total[..., None])
        dchance = jnp.einsum(
            "bqhe,bkhe->bhqk", grad_out, blocks[1], preferred_element_type=jnp.float32
        )
        dscore = (chances * (dchance - dots[..., None])).astype(jnp.bfloat16)
        running = (
            running
            + jnp.einsum("bhqk,bkhe->bqhe", dscore, blocks[0], preferred_element_type=jnp.float32)
            * scale
        )
        if with_keys:
            dkey = (
                jnp.einsum("bhqk,bqhe->bkhe", dscore, queries, preferred_element_type=jnp.float32)
                * scale
            ).astype(jnp.bfloat16)
            dvalue = jnp.einsum(
                "bhqk,bqhe->bkhe",
                chances.astype(jnp.bfloat16),
                grad_out,
                preferred_element_type=jnp.float32,
            ).astype(jnp.bfloat16)
            return (running, (dkey, dvalue))
        return (running, None)

    query_grad, pieces = lax.scan(
        cross_advance, jnp.zeros(queries.shape, jnp.float32), (key_blocks(keys), key_blocks(values))
    )
    if not with_keys:
        return (query_grad, None)
    questions, length, width = keys.shape
    key_grad = jnp.moveaxis(pieces[0], 0, 1).reshape(questions, length, width)
    value_grad = jnp.moveaxis(pieces[1], 0, 1).reshape(questions, length, width)
    return (query_grad, (key_grad, value_grad))


def general(
    decoder_in,
    encoded,
    cotangent,
    task_ids,
    task_embed,
    gain_self,
    self_query,
    self_key,
    self_value,
    self_output,
    gain_cross,
    cross_query,
    cross_key,
    cross_value,
    cross_output,
    gain_hidden,
    hidden_in,
    hidden_out,
):
    gathered = (
        lax.all_gather(task_embed, ("psg", "batch"), axis=1, tiled=True),
        lax.all_gather(gain_self, ("psg", "batch"), axis=0, tiled=True),
        lax.all_gather(self_query, ("psg", "batch"), axis=0, tiled=True),
        lax.all_gather(self_key, ("psg", "batch"), axis=0, tiled=True),
        lax.all_gather(self_value, ("psg", "batch"), axis=0, tiled=True),
        lax.all_gather(self_output, ("psg", "batch"), axis=0, tiled=True),
        lax.all_gather(gain_cross, ("psg", "batch"), axis=0, tiled=True),
        lax.all_gather(cross_query, ("psg", "batch"), axis=0, tiled=True),
        lax.all_gather(cross_key, ("psg", "batch"), axis=0, tiled=True),
        lax.all_gather(cross_value, ("psg", "batch"), axis=0, tiled=True),
        lax.all_gather(cross_output, ("psg", "batch"), axis=0, tiled=True),
        lax.all_gather(gain_hidden, ("psg", "batch"), axis=0, tiled=True),
    )
    (
        wide_table,
        wide_gain_self,
        wide_self_query,
        wide_self_key,
        wide_self_value,
        wide_self_output,
        wide_gain_cross,
        wide_cross_query,
        wide_cross_key,
        wide_cross_value,
        wide_cross_output,
        wide_gain_hidden,
    ) = gathered
    pieces = (
        lax.all_gather(hidden_in, "batch", axis=0, tiled=True),
        lax.all_gather(hidden_out, "batch", axis=1, tiled=True),
    )
    wide_in, wide_out = (
        lax.all_gather(pieces[0], "psg", axis=1, tiled=True),
        lax.all_gather(pieces[1], "psg", axis=0, tiled=True),
    )
    questions, tokens, width = decoder_in.shape
    rows = questions * tokens
    groups = task_embed.shape[0]
    onehot = (task_ids[:, None] == jnp.arange(groups, dtype=jnp.int32)[None, :]).astype(jnp.float32)
    embed_rows = jnp.dot(onehot, wide_table.astype(jnp.float32), precision=lax.Precision.HIGHEST)
    residual_in = (decoder_in.astype(jnp.float32) + embed_rows[:, None, :]).reshape(rows, width)
    gain_one = wide_gain_self.astype(jnp.float32)
    gain_two = wide_gain_cross.astype(jnp.float32)
    gain_three = wide_gain_hidden.astype(jnp.float32)
    normed_value, factor_one = rms_norm(residual_in, gain_one)
    normed_self = normed_value.astype(jnp.bfloat16)
    query_self = split_heads(matmul(normed_self, wide_self_query).astype(jnp.bfloat16), questions)
    key_self = split_heads(matmul(normed_self, wide_self_key).astype(jnp.bfloat16), questions)
    value_self = split_heads(matmul(normed_self, wide_self_value).astype(jnp.bfloat16), questions)
    causal = jnp.arange(tokens)[:, None] >= jnp.arange(tokens)[None, :]
    scores_self = jnp.where(causal, block_scores(query_self, key_self), MASKED)
    expo = jnp.exp(scores_self - jnp.max(scores_self, -1, keepdims=True))
    chances_self = expo / jnp.sum(expo, -1, keepdims=True)
    chances_low = chances_self.astype(jnp.bfloat16)
    mixed_self = (
        jnp.einsum("bhqk,bkhe->bqhe", chances_low, value_self, preferred_element_type=jnp.float32)
        .astype(jnp.bfloat16)
        .reshape(rows, width)
    )
    after_self = residual_in + matmul(mixed_self, wide_self_output)
    normed_value, factor_two = rms_norm(after_self, gain_two)
    normed_cross = normed_value.astype(jnp.bfloat16)
    query_cross = split_heads(
        matmul(normed_cross, wide_cross_query).astype(jnp.bfloat16), questions
    )
    encoder_rows = encoded.reshape(-1, width)
    key_cross = matmul(encoder_rows, wide_cross_key).astype(jnp.bfloat16).reshape(encoded.shape)
    value_cross = matmul(encoder_rows, wide_cross_value).astype(jnp.bfloat16).reshape(encoded.shape)
    length = encoded.shape[1]
    all_keys, all_values = (
        lax.all_gather(key_cross, "psg", axis=1, tiled=True),
        lax.all_gather(value_cross, "psg", axis=1, tiled=True),
    )
    highest, totals = score_stats(query_cross, all_keys)
    log_total = highest + jnp.log(totals)
    mixed = weighted_values(query_cross, all_keys, all_values, log_total)
    mixed_cross = mixed.astype(jnp.bfloat16).reshape(rows, width)
    after_cross = after_self + matmul(mixed_cross, wide_cross_output)
    normed_value, factor_three = rms_norm(after_cross, gain_three)
    normed_hidden = normed_value.astype(jnp.bfloat16)
    pre_act = matmul(normed_hidden, wide_in)
    activation, gelu_pull = jax.vjp(gelu_tanh, pre_act)
    act_low = activation.astype(jnp.bfloat16)
    hidden_part = matmul(act_low, wide_out)
    result = after_cross + hidden_part
    block_out = result.astype(jnp.bfloat16).reshape(decoder_in.shape)
    psg_count = lax.axis_size("psg")
    row_share = rows // psg_count
    first_row = lax.axis_index("psg") * row_share

    def own(values):
        return lax.dynamic_slice_in_dim(values, first_row, row_share, 0)

    grad_top = cotangent.reshape(rows, width)
    dhidden = outer_cols(grad_top, wide_out)
    dpre = gelu_pull(dhidden)[0].astype(jnp.bfloat16)
    term_out = inner_rows(own(act_low), own(grad_top))
    term_in = inner_rows(own(normed_hidden), own(dpre))
    dnorm_hidden = outer_cols(dpre, wide_in)
    lower, gterm_three = rms_back(after_cross, factor_three, gain_three, dnorm_hidden)
    grad_after_cross = grad_top.astype(jnp.float32) + lower
    dcross = grad_after_cross.astype(jnp.bfloat16)
    term_cross_output = inner_rows(own(mixed_cross), own(dcross))
    dmixed_cross = split_heads(
        outer_cols(dcross, wide_cross_output).astype(jnp.bfloat16), questions
    )
    dots_cross = grad_dots(query_cross, all_keys, all_values, log_total, dmixed_cross)
    query_own, key_pair = cross_back(
        query_cross, key_cross, value_cross, log_total, dots_cross, dmixed_cross, True
    )
    begin = (lax.axis_index("psg") + 1) * length
    span = (psg_count - 1) * length
    other_keys = lax.dynamic_slice_in_dim(jnp.concatenate([all_keys, all_keys], 1), begin, span, 1)
    other_values = lax.dynamic_slice_in_dim(
        jnp.concatenate([all_values, all_values], 1), begin, span, 1
    )
    query_rest = cross_back(
        query_cross, other_keys, other_values, log_total, dots_cross, dmixed_cross, False
    )[0]
    query_grad = query_own + query_rest
    dquery_cross = query_grad.astype(jnp.bfloat16).reshape(rows, width)
    dkey_rows = key_pair[0].reshape(-1, width)
    dvalue_rows = key_pair[1].reshape(-1, width)
    grad_encoded = (
        outer_cols(dkey_rows, wide_cross_key) + outer_cols(dvalue_rows, wide_cross_value)
    ).reshape(encoded.shape)
    term_cross_key = inner_rows(encoder_rows, dkey_rows)
    term_cross_value = inner_rows(encoder_rows, dvalue_rows)
    term_cross_query = inner_rows(own(normed_cross), own(dquery_cross))
    dnorm_cross = outer_cols(dquery_cross, wide_cross_query)
    lower, gterm_two = rms_back(after_self, factor_two, gain_two, dnorm_cross)
    grad_after_self = grad_after_cross + lower
    dself = grad_after_self.astype(jnp.bfloat16)
    term_self_output = inner_rows(own(mixed_self), own(dself))
    dmixed_self = split_heads(outer_cols(dself, wide_self_output).astype(jnp.bfloat16), questions)
    dchance = jnp.einsum(
        "bqhe,bkhe->bhqk", dmixed_self, value_self, preferred_element_type=jnp.float32
    )
    dots_self = jnp.sum(chances_self * dchance, -1, keepdims=True)
    dscore = (chances_self * (dchance - dots_self)).astype(jnp.bfloat16)
    scale = query_self.shape[-1] ** (-0.5)
    dquery_self = (
        (
            jnp.einsum("bhqk,bkhe->bqhe", dscore, key_self, preferred_element_type=jnp.float32)
            * scale
        )
        .astype(jnp.bfloat16)
        .reshape(rows, width)
    )
    dkey_self = (
        (
            jnp.einsum("bhqk,bqhe->bkhe", dscore, query_self, preferred_element_type=jnp.float32)
            * scale
        )
        .astype(jnp.bfloat16)
        .reshape(rows, width)
    )
    dvalue_self = (
        jnp.einsum("bhqk,bqhe->bkhe", chances_low, dmixed_self, preferred_element_type=jnp.float32)
        .astype(jnp.bfloat16)
        .reshape(rows, width)
    )
    dnorm_self = (
        outer_cols(dquery_self, wide_self_query)
        + outer_cols(dkey_self, wide_self_key)
        + outer_cols(dvalue_self, wide_self_value)
    )
    normed_own = own(normed_self)
    term_self_query = inner_rows(normed_own, own(dquery_self))
    term_self_key = inner_rows(normed_own, own(dkey_self))
    term_self_value = inner_rows(normed_own, own(dvalue_self))
    lower, gterm_one = rms_back(residual_in, factor_one, gain_one, dnorm_self)
    grad_decoder = grad_after_self + lower
    row_hot = jnp.repeat(onehot, tokens, 0)
    term_table = lax.dot_general(
        own(row_hot), own(grad_decoder), (((0,), (0,)), ((), ())), precision=lax.Precision.HIGHEST
    )
    sums = (
        lax.psum_scatter(term_table, ("psg", "batch"), scatter_dimension=1, tiled=True),
        lax.psum_scatter(
            jnp.sum(own(gterm_one), 0), ("psg", "batch"), scatter_dimension=0, tiled=True
        ),
        lax.psum_scatter(term_self_query, ("psg", "batch"), scatter_dimension=0, tiled=True),
        lax.psum_scatter(term_self_key, ("psg", "batch"), scatter_dimension=0, tiled=True),
        lax.psum_scatter(term_self_value, ("psg", "batch"), scatter_dimension=0, tiled=True),
        lax.psum_scatter(term_self_output, ("psg", "batch"), scatter_dimension=0, tiled=True),
        lax.psum_scatter(
            jnp.sum(own(gterm_two), 0), ("psg", "batch"), scatter_dimension=0, tiled=True
        ),
        lax.psum_scatter(term_cross_query, ("psg", "batch"), scatter_dimension=0, tiled=True),
        lax.psum_scatter(term_cross_key, ("psg", "batch"), scatter_dimension=0, tiled=True),
        lax.psum_scatter(term_cross_value, ("psg", "batch"), scatter_dimension=0, tiled=True),
        lax.psum_scatter(term_cross_output, ("psg", "batch"), scatter_dimension=0, tiled=True),
        lax.psum_scatter(
            jnp.sum(own(gterm_three), 0), ("psg", "batch"), scatter_dimension=0, tiled=True
        ),
    )
    hidden_pair = (
        lax.psum_scatter(
            term_in.astype(jnp.bfloat16), "psg", scatter_dimension=1, tiled=True
        ).astype(jnp.float32),
        lax.psum_scatter(
            term_out.astype(jnp.bfloat16), "psg", scatter_dimension=0, tiled=True
        ).astype(jnp.float32),
    )
    hidden_grads = (
        lax.psum_scatter(hidden_pair[0], "batch", scatter_dimension=0, tiled=True),
        lax.psum_scatter(hidden_pair[1], "batch", scatter_dimension=1, tiled=True),
    )
    return (
        block_out,
        grad_decoder.reshape(decoder_in.shape),
        grad_encoded,
        sums[0],
        sums[1],
        sums[2],
        sums[3],
        sums[4],
        sums[5],
        sums[6],
        sums[7],
        sums[8],
        sums[9],
        sums[10],
        sums[11],
        hidden_grads[0],
        hidden_grads[1],
    )


def local(psg, batch, *arrays):
    decoder_in, gain = arrays[0], arrays[5]
    if regular(gain.shape[0], psg, batch, decoder_in.shape[1], decoder_in.shape[2]) and decoder_in.shape[0] == 1:
        return fused(psg, batch, *arrays)
    return general(*arrays)


def solution(mesh):
    line, spread = P("batch", None, None), P("batch", "psg", None)
    flat, rows = P(("psg", "batch")), P(("psg", "batch"), None)
    table, wide, tall = P(None, ("psg", "batch")), P("batch", "psg"), P("psg", "batch")
    return jax.shard_map(
        functools.partial(local, mesh.shape["psg"], mesh.shape["batch"]),
        mesh=mesh,
        in_specs=(line, spread, line, P("batch"), table) + ((flat,) + (rows,) * 4) * 2 + (flat, wide, tall),
        out_specs=(line, line, spread, table) + ((flat,) + (rows,) * 4) * 2 + (flat, wide, tall),
        check_vma=False,
    )
```

```python
import functools
import types

import jax
import jax.numpy as jnp
from jax import lax
from jax.experimental import pallas as pl
from jax.experimental.pallas import tpu as pltpu
from jax.sharding import PartitionSpec as P

SPANS = 4
HEADS = 12
PASS_LEN = 192
EPSILON = 1e-06
MASKED = -1000000000.0
LANES = 128
MIB = 2**20
PAIRS = 100

F32 = jnp.float32
BF16 = jnp.bfloat16
ID = pl.DeviceIdType.MESH

CK, CV, CO, CQ, SO, SK, SQ, SV = range(8)
GATHER = ((CK, 2, False), (SK, 3, False), (SO, 1, True), (CQ, 1, True), (CO, 1, False))
REDUCE = ((CO, 1, True), (CQ, 2, True), (SK, 3, True), (CK, 1, False), (CV, 1, False))


def nn(former, latter):
    return jnp.dot(former, latter, preferred_element_type=F32)


def nt(former, latter):
    return lax.dot_general(former, latter, (((1,), (1,)), ((), ())), preferred_element_type=F32)


def rms_factor(values):
    return lax.rsqrt(jnp.mean(values * values, -1, keepdims=True) + EPSILON)


def norm_back(values, factor, scales, grad_out):
    scaled = grad_out * scales
    cubed = factor * factor * factor
    return factor * scaled - values * cubed * jnp.mean(scaled * values, -1, keepdims=True)


def lane_is_low():
    return lax.broadcasted_iota(jnp.int32, (1, LANES), 1) < LANES // 2


def stack_heads(pair):
    low = lane_is_low()
    zero = jnp.zeros_like(pair)
    return jnp.concatenate([jnp.where(low, pair, zero), jnp.where(low, zero, pair)], 0)


def merge_heads(stacked):
    half = stacked.shape[0] // 2
    return jnp.where(lane_is_low(), stacked[:half], stacked[half:])


def stack_stat(stats, pair):
    return jnp.concatenate([stats[:, 2 * pair : 2 * pair + 1], stats[:, 2 * pair + 1 : 2 * pair + 2]], 0)


def spread_stat(stats, pair):
    return jnp.where(
        lane_is_low(), stats[:, 2 * pair : 2 * pair + 1], stats[:, 2 * pair + 1 : 2 * pair + 2]
    )


def column_tiles(width, size=256):
    return [slice(first, min(first + size, width)) for first in range(0, width, size)]


def pair_lanes(pair):
    return slice(pair * LANES, (pair + 1) * LANES)


def self_forward(dec, row, g1, wq, wk, wv, wo, g2, res, n1, q, k, v, probs, mix, after, n2):
    x = dec + row
    res[...] = x
    normed = (x * rms_factor(x) * g1).astype(BF16)
    n1[...] = normed
    q[...] = nn(normed, wq).astype(BF16)
    k[...] = nn(normed, wk).astype(BF16)
    v[...] = nn(normed, wv).astype(BF16)
    tokens, width = x.shape
    scale = (width // HEADS) ** (-0.5)
    rows = lax.broadcasted_iota(jnp.int32, (2 * tokens, tokens), 0) % tokens
    causal = rows >= lax.broadcasted_iota(jnp.int32, (2 * tokens, tokens), 1)
    for pair in range(HEADS // 2):
        cols = pair_lanes(pair)
        scores = jnp.where(causal, nt(stack_heads(q[:, cols]), k[:, cols]) * scale, MASKED)
        expo = jnp.exp(scores - jnp.max(scores, -1, keepdims=True))
        chances = expo * (1.0 / jnp.sum(expo, -1, keepdims=True))
        probs[pair] = chances
        mix[:, cols] = merge_heads(nn(chances.astype(BF16), v[:, cols])).astype(BF16)
    y = x + nn(mix[...], wo)
    after[...] = y
    n2[...] = (y * rms_factor(y) * g2).astype(BF16)


def cross_attend(qc, key, val, probs, stat, part):
    tokens, width = qc.shape
    share = tokens // 4
    scale = (width // HEADS) ** (-0.5)
    lane = lax.broadcasted_iota(jnp.int32, (tokens, LANES), 1)
    tops = jnp.zeros((tokens, LANES), F32)
    sums = jnp.ones((tokens, LANES), F32)
    for pair in range(HEADS // 2):
        cols = pair_lanes(pair)
        scores = nt(stack_heads(qc[:, cols]), key[:, cols]) * scale
        top = jnp.max(scores, -1, keepdims=True)
        expo = jnp.exp(scores - top)
        total = jnp.sum(expo, -1, keepdims=True)
        low = expo.astype(BF16)
        probs[pair] = low
        mixed = merge_heads(nn(low, val[:, cols]) * (1.0 / total)).astype(BF16)
        for p in range(4):
            part[p // 2, p % 2, :, cols] = mixed[p * share : (p + 1) * share]
        for half in range(2):
            rows = slice(half * tokens, (half + 1) * tokens)
            here = lane == 2 * pair + half
            tops = jnp.where(here, top[rows], tops)
            sums = jnp.where(here, total[rows], sums)
    for p in range(4):
        rows = slice(p * share, (p + 1) * share)
        stat[p // 2, p % 2, :, :LANES] = tops[rows]
        stat[p // 2, p % 2, :, LANES:] = sums[rows]


def join_parts(o_a, s_a, o_b, s_b, out, stat):
    top_a, top_b = s_a[:, :LANES], s_b[:, :LANES]
    top = jnp.maximum(top_a, top_b)
    w_a = jnp.exp(top_a - top) * s_a[:, LANES:]
    w_b = jnp.exp(top_b - top) * s_b[:, LANES:]
    total = w_a + w_b
    inverse = 1.0 / total
    w_a, w_b = w_a * inverse, w_b * inverse
    for pair in range(HEADS // 2):
        cols = pair_lanes(pair)
        mixed = spread_stat(w_a, pair) * o_a[:, cols].astype(F32) + spread_stat(w_b, pair) * o_b[:, cols].astype(F32)
        out[:, cols] = mixed.astype(out.dtype)
    stat[:, :LANES] = top
    stat[:, LANES:] = total


def feed_forward(x, top, w_in, w_out):
    pre = nn(x, w_in)
    root = (2.0 / jnp.pi) ** 0.5
    square = pre * pre
    bend = jnp.tanh(root * (pre + 0.044715 * (square * pre)))
    act = (0.5 * pre * (1.0 + bend)).astype(BF16)
    slope = 0.5 * (1.0 + bend) + 0.5 * pre * (1.0 - bend * bend) * (root * (1.0 + 3 * 0.044715 * square))
    dpre = (nn(top, w_out) * slope).astype(BF16)
    return act, dpre


def head_sums(product):
    lane = lax.broadcasted_iota(jnp.int32, (product.shape[0], LANES), 1)
    sums = jnp.zeros(lane.shape, F32)
    low = lane_is_low()
    for pair in range(HEADS // 2):
        here = product[:, pair_lanes(pair)]
        sums = jnp.where(lane == 2 * pair, jnp.sum(jnp.where(low, here, 0.0), -1, keepdims=True), sums)
        sums = jnp.where(lane == 2 * pair + 1, jnp.sum(jnp.where(low, 0.0, here), -1, keepdims=True), sums)
    return sums


def cross_backward(pair, qc, dmixed, key, val, probs, ratio, dots, part):
    tokens, width = qc.shape
    share = tokens // 4
    scale = (width // HEADS) ** (-0.5)
    cols = pair_lanes(pair)
    q2 = stack_heads(qc[:, cols])
    d2 = stack_heads(dmixed[:, cols])
    chances = probs[pair].astype(F32) * stack_stat(ratio, pair)
    dchance = nt(d2, val[:, cols])
    dscore = (chances * (dchance - stack_stat(dots, pair))).astype(BF16)
    dquery = (merge_heads(nn(dscore, key[:, cols])) * scale).astype(BF16)
    for p in range(4):
        part[p // 2, p % 2, :, cols] = dquery[p * share : (p + 1) * share]
    probs[pair, :LANES] = (nn(q2.T, dscore) * scale).astype(BF16)
    probs[pair, LANES:] = nn(d2.T, chances.astype(BF16)).astype(BF16)


def self_backward(dmixed, q, k, v, probs, dq, dk, dv):
    width = q.shape[1]
    scale = (width // HEADS) ** (-0.5)
    for pair in range(HEADS // 2):
        cols = pair_lanes(pair)
        q2 = stack_heads(q[:, cols])
        d2 = stack_heads(dmixed[:, cols])
        chances = probs[pair]
        dchance = nt(d2, v[:, cols])
        dscore = chances * (dchance - jnp.sum(chances * dchance, -1, keepdims=True))
        low = dscore.astype(BF16)
        dq[:, cols] = (merge_heads(nn(low, k[:, cols])) * scale).astype(BF16)
        dk[:, cols] = (nn(low.T, q2) * scale).astype(BF16)
        dv[:, cols] = nn(chances.astype(BF16).T, d2).astype(BF16)


INPUTS = ["tid", "dec", "cot", "enc", "table", "g_one", "g_two", "g_three", "sq", "sk", "sv", "so", "cq", "co", "ck", "cv", "h_in", "h_out"]
OUTPUTS = ["block_out", "grad_dec", "grad_enc", "g_attn", "g_in", "g_out", "g_vec"]


def buffers(psg, batch, tokens, length, width, owned, hidden):
    spans, pairs, share, half = batch // 2, HEADS // 2, tokens // psg, width // 2
    dma = pltpu.SemaphoreType.DMA
    whole = (tokens, width)
    quad = (2, 2, share)
    band = 2 * owned
    runs = len(GATHER)

    def low(*shape):
        return pltpu.VMEM(shape, BF16)

    def full(*shape):
        return pltpu.VMEM(shape, F32)

    out = dict(
        w=low(8, 2, 2 * batch * owned, width),
        f=low(2, width, hidden // 2),
        m_send=low(4, band, half),
        m_recv=low(4, band, half),
        v_buf=full(4, 8, width),
        v_recv=full(3 + spans, 8, width),
        cots=low(2, tokens, width),
        dec_here=low(tokens, width),
        enc_here=low(length, width),
        block_here=low(*quad, width),
        grad_dec_here=full(*whole),
        grad_enc_here=full(length, width),
        g_attn_here=full(8, owned, width),
        g_in_here=full(width // batch, hidden),
        g_out_here=full(width // batch, hidden),
        g_vec_here=full(8, owned),
        load=dma((3,)),
        store=dma((16,)),
        key=low(length, width),
        val=low(length, width),
        c_probs=low(pairs, 2 * tokens, length),
        s_probs=full(pairs, 2 * tokens, tokens),
        res=full(*whole),
        after=full(*whole),
        n1=low(*whole),
        n2=low(*whole),
        q=low(*whole),
        k=low(*whole),
        v=low(*whole),
        mix=low(*whole),
        qc=low(*whole),
        o_part=low(*quad, width),
        o_stat=full(*quad, 2 * LANES),
        o_core=low(2, share, width),
        o_core_stat=full(2, share, 2 * LANES),
        o_to=low(share, width),
        o_to_stat=full(share, 2 * LANES),
        o_mid=full(share, width),
        o_mid_stat=full(share, 2 * LANES),
        o_x=low(share, width),
        o_x_stat=full(share, 2 * LANES),
        mixed_rows=full(share, width),
        stat_rows=full(share, 2 * LANES),
        after_rows=full(share, width),
        n3=low(2, *quad, width),
        mixc=low(*quad, width),
        log_total=full(*quad, LANES),
        dn=low(2, *quad, width),
        dn_core=low(2, 2, share, width),
        dn_to=low(3, share, width),
        dn_got=low(3, share, width),
        hp=low(2, *quad, width),
        hp_core=low(2, 2, share, width),
        hp_to=low(3, share, width),
        hp_got=low(3, share, width),
        grad_rows=full(share, width),
        dcross=low(*quad, width),
        dq_part=low(*quad, width),
        dq_core=low(2, share, width),
        dq_to=low(share, width),
        dq_x=low(share, width),
        dqc=low(*quad, width),
        dself=low(*quad, width),
        dself_rest=low(*quad, width),
        dq=low(*whole),
        dk=low(*whole),
        dv=low(*whole),
        turned=low(4, width, tokens),
        gf=low(2, width, hidden // 2),
        gkv=low(2, 2, 2 * batch * owned, width),
        kv_core=low(2, 2, batch * owned, width),
        kv_to=low(2, batch * owned, width),
        kv_x=low(2, batch * owned, width),
        g=low(8, batch * owned, width),
        gains=full(8, width),
        t_buf=full(4, 8, width),
        t_recv=full(3 + spans, 8, width),
        f_swap=low(2, width // batch, hidden // 2),
        f_swapped=low(2, width // batch, hidden // 2),
        f_came=low(3, 2, width // spans, hidden // 2),
        f_sum=full(2, width // spans, hidden // 2),
        one_send=dma((PAIRS,)),
        one_recv=dma((PAIRS,)),
        a_recv=dma((runs, 2 * batch)),
        a_send=dma((runs, 4)),
        a_core=dma((runs,)),
        w_recv=dma((spans,)),
        w_send=dma((3,)),
        v_sems=dma((2, spans)),
        t_sems=dma((2, spans)),
        f_line=dma((6,)),
    )
    for number, (_, count, y_first) in enumerate(REDUCE):
        rows = -(-count * owned // 16) * 16
        if y_first:
            out[f"r{number}_y"] = low(2, count, band, width)
            out[f"r{number}_one"] = low(count, band, width)
            out[f"r{number}_own"] = full(count * owned, width)
        else:
            out[f"r{number}_one"] = low(2 * band, width)
            out[f"r{number}_two_to"] = low(band, width)
            out[f"r{number}_two"] = low(band, width)
            out[f"r{number}_own"] = full(band, width)
        out[f"r{number}_last_to"] = low(rows, width)
        out[f"r{number}_last"] = low(rows, width)
    return out


def block_kernel(names, psg, batch, *refs):
    r = types.SimpleNamespace(**dict(zip(names, refs, strict=True)))
    index, question = lax.axis_index("psg"), lax.axis_index("batch")
    far, near = question // 2, question % 2
    side, core = index // 2, index % 2
    x_peer = ((1 - side) * 2 + core, question)
    c_peer = (side * 2 + 1 - core, question)
    y_peer = (index, far * 2 + 1 - near)
    d_peer = ((1 - side) * 2 + core, far * 2 + 1 - near)
    places = [far, far + 1 - 2 * (far % 2), lax.rem(far + 2, SPANS), SPANS - 1 - far]
    column = [(index, z * 2 + near) for z in places[1:]]
    one_peer, two_peer = column[0], column[1]
    tokens, width = r.dec_here.shape
    owned = r.sq.shape[0]
    band, quarter, half = 2 * owned, batch * owned, width // 2
    share = tokens // psg
    fan = width // batch
    shards = (r.ck, r.cv, r.co, r.cq, r.so, r.sk, r.sq, r.sv)
    pairs = HEADS // 2

    def aligned(value, to):
        return value if isinstance(value, int) else pl.multiple_of(value, to)

    def span(start, size, to):
        return pl.ds(aligned(start, to), size)

    def lanes(h):
        return span(h * half, half, LANES)

    sent = []

    def go(copy):
        copy.start()
        sent.append(copy)

    def remote(src, dst, send, recv, device):
        return pltpu.make_async_remote_copy(
            src_ref=src, dst_ref=dst, send_sem=send, recv_sem=recv, device_id=device, device_id_type=ID
        )

    numbers = iter(range(PAIRS))

    def pair(src, dst, device):
        number = next(numbers)
        copy = remote(src, dst, r.one_send.at[number], r.one_recv.at[number], device)
        go(copy)
        return copy

    loads = [
        pltpu.make_async_copy(r.cot, r.cots.at[near], r.load.at[0]),
        pltpu.make_async_copy(r.dec, r.dec_here, r.load.at[1]),
        pltpu.make_async_copy(r.enc, r.enc_here, r.load.at[2]),
    ]
    for copy in loads:
        copy.start()
    stores = []

    def store(src, dst):
        copy = pltpu.make_async_copy(src, dst, r.store.at[len(stores)])
        copy.start()
        stores.append(copy)

    barrier = pltpu.get_barrier_semaphore()
    greeted = column + [y_peer, x_peer, c_peer, d_peer]
    for other in greeted:
        pl.semaphore_signal(barrier, inc=1, device_id=other, device_id_type=ID)
    pl.semaphore_wait(barrier, len(greeted))

    def pack(number):
        first, second = shards[2 * number], shards[2 * number + 1]
        both = jnp.concatenate([first[:, lanes(1 - near)].astype(F32), second[:, lanes(1 - near)].astype(F32)], 0)
        r.m_send[number] = both.astype(BF16)

    def exchange(first, count):
        for number in range(first, first + count):
            pack(number)
        return pair(r.m_send.at[first : first + count], r.m_recv.at[first : first + count], y_peer)

    row = core * quarter + far * band

    def join(number):
        other = r.m_recv[number].astype(F32)
        for part in range(2):
            mine = shards[2 * number + part][:, lanes(near)].astype(F32)
            theirs = other[part * owned : (part + 1) * owned]
            block = jnp.where(near == 0, jnp.concatenate([mine, theirs], 0), jnp.concatenate([theirs, mine], 0))
            r.w[2 * number + part, side, span(row, band, 16), lanes(near)] = block.astype(BF16)

    def unit(run, x, c, z, h):
        first, count, joined = GATHER[run]
        rows = span(c * quarter + z * band, band, 16)
        return r.w.at[first : first + count, slice(None) if joined else x, rows, lanes(h)]

    def landing(run, x, c, z, h):
        return r.a_recv.at[run, (0 if GATHER[run][2] else x) * batch + z * 2 + h]

    def hand(run, x, c, z, h, kind, device, recv=None):
        spot = unit(run, x, c, z, h)
        remote(spot, spot, r.a_send.at[run, kind], landing(run, x, c, z, h) if recv is None else recv, device).start()

    def landed(run, x, c, z, h):
        spot = unit(run, x, c, z, h)
        remote(spot, spot, r.a_send.at[run, 0], landing(run, x, c, z, h), c_peer).wait_recv()

    def wide(run, z, h):
        if not GATHER[run][2]:
            hand(run, side, core, z, h, 2, x_peer)
        hand(run, side, core, z, h, 3, c_peer, r.a_core.at[run])

    def offer(run):
        hand(run, side, core, far, near, 0, two_peer)
        hand(run, side, core, far, near, 0, one_peer)
        hand(run, side, core, far, near, 1, y_peer)
        wide(run, far, near)

    def from_y(run, step):
        landed(run, side, core, places[step], 1 - near)
        wide(run, places[step], 1 - near)

    def from_line(run, step):
        z = places[step]
        landed(run, side, core, z, near)
        if step == 2:
            hand(run, side, core, z, near, 0, one_peer)
        hand(run, side, core, z, near, 1, y_peer)
        wide(run, z, near)

    def from_x(run, step):
        z = places[step]
        for h in (near, 1 - near):
            landed(run, 1 - side, core, z, h)
            hand(run, 1 - side, core, z, h, 3, c_peer, r.a_core.at[run])

    def sent_of(run):
        first, count, joined = GATHER[run]
        lower = r.w.at[first : first + count, slice(None) if joined else 0]
        quarters = (slice(None),) * (2 if joined else 1)
        sizes = [
            lower.at[(*quarters, pl.ds(0, 3 * band), pl.ds(0, half))],
            lower.at[(*quarters, pl.ds(0, quarter), pl.ds(0, half))],
            None if joined else lower.at[(*quarters, pl.ds(0, quarter), slice(None))],
            r.w.at[first : first + count, :, pl.ds(0, quarter), :],
        ]
        for kind, size in enumerate(sizes):
            if size is not None:
                remote(size, size, r.a_send.at[run, kind], r.a_core.at[run], c_peer).wait_send()

    def complete(run):
        first, count, _ = GATHER[run]
        all_of = r.w.at[first : first + count, :, span((1 - core) * quarter, quarter, 16), :]
        remote(all_of, all_of, r.a_send.at[run, 0], r.a_core.at[run], c_peer).wait_recv()

    def matrix(number):
        return r.w[number].reshape(width, width)

    m_kv = exchange(0, 1)
    m_self = exchange(2, 2)
    m_tail = exchange(1, 1)

    def ladder(buf, recv, sems):
        def first():
            return pair(buf.at[0], recv.at[0], c_peer)

        def second(copy):
            copy.wait_recv()
            buf[1] = (buf[0].astype(F32) + recv[0].astype(F32)).astype(buf.dtype)
            return pair(buf.at[1], recv.at[1], x_peer)

        def third(copy):
            copy.wait_recv()
            buf[2] = (buf[1].astype(F32) + recv[1].astype(F32)).astype(buf.dtype)
            return pair(buf.at[2], recv.at[2], y_peer)

        def fourth(copy):
            copy.wait_recv()
            buf[3] = (buf[2].astype(F32) + recv[2].astype(F32)).astype(buf.dtype)
            for z in places[1:]:
                go(remote(buf.at[3], recv.at[3 + far], sems.at[0, z], sems.at[1, far], (index, z * 2 + near)))

        def last():
            total = buf[3].astype(F32)
            for z in places[1:]:
                remote(buf.at[3], recv.at[3 + z], sems.at[0, z], sems.at[1, z], c_peer).wait_recv()
                total = total + recv[3 + z].astype(F32)
            return total

        return first, second, third, fourth, last

    device = index * batch + question
    place = jnp.where(
        lax.broadcasted_iota(jnp.int32, (owned, width), 1)
        == lax.broadcasted_iota(jnp.int32, (owned, width), 0) + device * owned,
        1.0,
        0.0,
    ).astype(BF16)
    r.v_buf[0, 0:3] = nn(r.table[...], place)
    for number, gain in enumerate((r.g_one, r.g_two, r.g_three)):
        r.v_buf[0, 3 + number : 4 + number] = nn(gain[...], place)
    r.v_buf[0, 6:8] = jnp.zeros((2, width), F32)
    v_first, v_second, v_third, v_fourth, v_last = ladder(r.v_buf, r.v_recv, r.v_sems)
    v_copy = v_first()

    m_kv.wait_recv()
    join(0)
    offer(0)
    m_self.wait_recv()
    join(2)
    join(3)
    offer(1)
    m_tail.wait_recv()
    join(1)
    own_tail = r.w.at[CQ : CQ + 2, side, span(row, band, 16), lanes(near)]
    x_tail = pair(own_tail, own_tail, x_peer)
    v_copy = v_second(v_copy)

    cut = r.f.shape[2]
    other_cols = span((1 - near) * cut, cut, LANES)
    own_cols = span(near * cut, cut, LANES)
    own_fan = span(question * fan, fan, 16)
    r.f[0, own_fan] = r.h_in[:, own_cols]
    r.f[1, own_fan] = r.h_out[:, own_cols]

    def f_unit(z):
        return r.f.at[:, span(z * 2 * fan, 2 * fan, 16), :]

    def f_hand(z, sem, device):
        go(remote(f_unit(z), f_unit(z), sem, r.w_recv.at[z], device))

    def f_landed(step):
        z = places[step]
        remote(f_unit(z), f_unit(z), r.w_send.at[0], r.w_recv.at[z], c_peer).wait_recv()
        if step == 2:
            f_hand(z, r.w_send.at[2], one_peer)

    def near_units(run):
        from_y(run, 0)
        from_line(run, 2)
        from_line(run, 1)

    def far_units(run):
        from_line(run, 3)
        from_y(run, 1)
        from_y(run, 2)

    near_units(0)
    near_units(1)
    x_tail.wait_recv()
    offer(2)
    far_units(0)
    far_units(1)
    offer(3)
    near_units(2)
    from_y(0, 3)
    from_y(1, 3)
    offer(4)
    from_x(0, 0)
    from_x(1, 0)
    v_copy = v_third(v_copy)
    far_units(2)
    from_x(0, 1)
    from_x(1, 1)
    near_units(3)
    v_fourth(v_copy)
    from_x(0, 2)
    from_x(1, 2)
    from_y(2, 3)
    h_copies = [
        pair(r.h_in.at[:, other_cols], r.f.at[0, own_fan], y_peer),
        pair(r.h_out.at[:, other_cols], r.f.at[1, own_fan], y_peer),
    ]
    far_units(3)
    loads[0].wait()
    loads[1].wait()
    from_x(0, 3)
    from_x(1, 3)
    from_y(3, 3)
    near_units(4)
    for copy in h_copies:
        copy.wait_recv()
    f_hand(far, r.w_send.at[0], two_peer)
    f_hand(far, r.w_send.at[1], one_peer)
    for run in range(3):
        complete(run)
    vectors = v_last()

    gains = [vectors[3 + i : 4 + i] for i in range(3)]
    chosen = r.tid[0]
    row_embed = functools.reduce(
        jnp.add, [vectors[i : i + 1] * jnp.where(chosen == i, 1.0, 0.0).astype(F32) for i in range(3)]
    )
    r.gains[0:3] = vectors[3:6]
    self_forward(
        r.dec_here[...].astype(F32), row_embed, gains[0], matrix(SQ), matrix(SK), matrix(SV), matrix(SO), gains[1],
        r.res, r.n1, r.q, r.k, r.v, r.s_probs, r.mix, r.after, r.n2,
    )
    far_units(4)
    loads[2].wait()
    for cols in column_tiles(width):
        r.key[:, cols] = nn(r.enc_here[...], r.w[CK, :, :, cols].reshape(width, -1)).astype(BF16)
        r.val[:, cols] = nn(r.enc_here[...], r.w[CV, :, :, cols].reshape(width, -1)).astype(BF16)
    complete(3)
    r.qc[...] = nn(r.n2[...], matrix(CQ)).astype(BF16)

    cross_attend(r.qc, r.key, r.val, r.c_probs, r.o_stat, r.o_part)
    first = [pair(r.o_part.at[:, 1 - core], r.o_core, c_peer), pair(r.o_stat.at[:, 1 - core], r.o_core_stat, c_peer)]
    from_y(4, 3)
    for step in range(SPANS):
        from_x(4, step)
    f_landed(2)
    f_landed(1)
    for copy in first:
        copy.wait_recv()
    join_parts(
        r.o_part[1 - side, core], r.o_stat[1 - side, core], r.o_core[1 - side], r.o_core_stat[1 - side],
        r.o_to, r.o_to_stat,
    )
    second = [pair(r.o_to, r.o_x, x_peer), pair(r.o_to_stat, r.o_x_stat, x_peer)]
    cot_copy = pair(r.cots.at[near], r.cots.at[near], y_peer)
    join_parts(
        r.o_part[side, core], r.o_stat[side, core], r.o_core[side], r.o_core_stat[side], r.o_mid, r.o_mid_stat
    )
    complete(4)
    for copy in second:
        copy.wait_recv()
    join_parts(r.o_mid[...], r.o_mid_stat[...], r.o_x[...], r.o_x_stat[...], r.mixed_rows, r.stat_rows)
    my_rows = span(index * share, share, 16)
    r.log_total[side, core] = r.stat_rows[:, :LANES] + jnp.log(r.stat_rows[:, LANES:])
    mixed_low = r.mixed_rows[...].astype(BF16)
    r.mixc[side, core] = mixed_low
    y = r.after[my_rows, :] + nn(mixed_low, matrix(CO))
    r.after_rows[...] = y
    r.n3[near, side, core] = (y * rms_factor(y) * r.gains[2:3]).astype(BF16)

    def block8(h, x, c):
        return r.n3.at[h, x, c]

    def spread4(buf):
        spot = buf.at[side, core]
        over_x, over_c = pair(spot, spot, x_peer), pair(spot, spot, c_peer)

        def then():
            over_x.wait_recv()
            onward = buf.at[1 - side, core]
            last = pair(onward, onward, c_peer)

            def end():
                over_c.wait_recv()
                last.wait_recv()

            return end

        return then

    mine = block8(near, side, core)
    to_y, to_x, to_d, to_c = [pair(mine, mine, peer) for peer in (y_peer, x_peer, d_peer, c_peer)]
    onward = [to_c]
    for copy, h, x in ((to_y, 1 - near, side), (to_x, near, 1 - side), (to_d, 1 - near, 1 - side)):
        copy.wait_recv()
        onward.append(pair(block8(h, x, core), block8(h, x, core), c_peer))
    f_landed(3)
    cot_copy.wait_recv()
    for copy in onward:
        copy.wait_recv()

    log_then = spread4(r.log_total)
    mixc_then = spread4(r.mixc)
    x = r.n3[...].reshape(2 * tokens, width)
    top = r.cots[...].reshape(2 * tokens, width)
    act, dpre = feed_forward(x, top, r.f[0], r.f[1])
    r.dn[...] = nt(dpre, r.f[0]).astype(BF16).reshape(r.dn.shape)

    def shrink8(part, got_c, to, got):
        over_c = pair(part.at[:, :, 1 - core], got_c, c_peer)

        def second():
            over_c.wait_recv()

            def total(h, x):
                return part[h, x, core].astype(F32) + got_c[h, x].astype(F32)

            copies = []
            for slot, (h, x, peer) in enumerate(
                ((1 - near, 1 - side, d_peer), (near, 1 - side, x_peer), (1 - near, side, y_peer))
            ):
                to[slot] = total(h, x).astype(BF16)
                copies.append(pair(to.at[slot], got.at[slot], peer))

            def last():
                out = total(near, side)
                for slot, copy in enumerate(copies):
                    copy.wait_recv()
                    out = out + got[slot].astype(F32)
                return out

            return last

        return second

    dn_second = shrink8(r.dn, r.dn_core, r.dn_to, r.dn_got)
    r.hp[...] = nt(act, r.f[1]).astype(BF16).reshape(r.hp.shape)
    dn_last = dn_second()
    hp_second = shrink8(r.hp, r.hp_core, r.hp_to, r.hp_got)
    r.gf[0] = nn(x.T, dpre).astype(BF16)
    r.gf[1] = nn(top.T, act).astype(BF16)

    def line_kit(came, src, sems):
        def over_pair(step):
            slot = step // 2
            return remote(src(places[step]), came.at[slot], sems.at[slot], sems.at[3 + slot], one_peer)

        def over_pairs():
            return remote(src(places[2]), came.at[2], sems.at[2], sems.at[5], two_peer)

        def first():
            go(over_pair(3))
            go(over_pair(1))

        def second(value):
            over_pair(3).wait_recv()
            src(places[2])[...] = (value + came[1].astype(F32)).astype(BF16)
            go(over_pairs())

        def total(value, out):
            over_pair(1).wait_recv()
            both = value + came[0].astype(F32)
            over_pairs().wait_recv()
            out[...] = both + came[2].astype(F32)

        return first, second, total

    def f_piece(z):
        return r.gf.at[:, span(z * 2 * fan, 2 * fan, 16), :]

    f_first, f_second, f_total = line_kit(r.f_came, f_piece, r.f_line)
    f_first()
    log_end = log_then()
    mixc_end = mixc_then()

    upstream = dn_last()
    y = r.after_rows[...]
    factor = rms_factor(y)
    scales = r.gains[2:3]
    gain_three = jnp.sum(upstream * y * factor, 0, keepdims=True)
    grad = r.cots[near, my_rows, :].astype(F32) + norm_back(y, factor, scales, upstream)
    r.grad_rows[...] = grad
    low = grad.astype(BF16)
    r.dcross[side, core] = low
    dcross_then = spread4(r.dcross)
    hp_last = hp_second()
    log_end()
    mixc_end()
    dcross_end = dcross_then()
    dcross_end()

    def rows_of(ref):
        return ref[...].reshape(tokens, ref.shape[-1])

    parity, high = far % 2, far // 2

    def ordered(value, y_first):
        blocks = [(z, h) for z in range(SPANS) for h in range(2)]
        if y_first:
            blocks.sort(key=lambda block: (block[1], block[0] % 2, block[0] // 2))
        else:
            blocks.sort(key=lambda block: (block[0] % 2, block[0] // 2, block[1]))
        parts = [value[(z * 2 + h) * owned : (z * 2 + h + 1) * owned] for z, h in blocks]
        return jnp.concatenate(parts, 0).astype(BF16)

    def last_step(number, mine, theirs, peer):
        first, count, _ = REDUCE[number]
        to, got = getattr(r, f"r{number}_last_to"), getattr(r, f"r{number}_last")
        if to.shape[0] > theirs.shape[0]:
            theirs = jnp.concatenate([theirs, jnp.zeros((to.shape[0] - theirs.shape[0], width), F32)], 0)
        to[...] = theirs.astype(BF16)
        copy = pair(to, got, peer)
        r.g_attn_here[first : first + count] = mine.reshape(count, owned, width)

        def end():
            copy.wait_recv()
            more = got[...].astype(F32)[: count * owned]
            r.g_attn_here[first : first + count] = r.g_attn_here[first : first + count] + more.reshape(count, owned, width)
            store(r.g_attn_here.at[first : first + count], r.g_attn.at[first : first + count])

        return end

    def line_first(number):
        m = REDUCE[number][0]
        one, two_to, two, own = [getattr(r, f"r{number}_{name}") for name in ("one", "two_to", "two", "own")]
        copies = []

        def forward():
            copies.append(pair(r.g.at[m, span((1 - parity) * 2 * band, 2 * band, 16), :], one, one_peer))

        def again():
            copies[0].wait_recv()
            total = r.g[m, span(parity * 2 * band, 2 * band, 16), :].astype(F32) + one[...].astype(F32)
            upper, lower = total[:band], total[band:]
            two_to[...] = jnp.where(high == 0, lower, upper).astype(BF16)
            copies.append(pair(two_to, two, two_peer))
            own[...] = jnp.where(high == 0, upper, lower)

        def finish():
            copies[1].wait_recv()
            total = own[...] + two[...].astype(F32)
            upper, lower = total[:owned], total[owned:]
            return last_step(
                number, jnp.where(near == 0, upper, lower), jnp.where(near == 0, lower, upper), y_peer
            )

        return forward, again, finish

    def y_first(number):
        first, count, _ = REDUCE[number]
        got_y, one = getattr(r, f"r{number}_y"), getattr(r, f"r{number}_one")
        copies = {}

        def piece(h, p):
            return r.g.at[first : first + count, span(h * 2 * band + p * band, band, 16), :]

        def begin(mine):
            p = parity if mine else 1 - parity
            copies[mine] = pair(piece(1 - near, p), got_y.at[1 if mine else 0], y_peer)

        def value(mine):
            copies[mine].wait_recv()
            return piece(near, parity if mine else 1 - parity)[...].astype(F32) + got_y[1 if mine else 0].astype(F32)

        def forward():
            got_y[0] = value(False).astype(BF16)
            copies["one"] = pair(got_y.at[0], one, one_peer)

        def again():
            total = value(True)
            copies["one"].wait_recv()
            total = total + one[...].astype(F32)
            upper = total[:, :owned].reshape(count * owned, width)
            lower = total[:, owned:].reshape(count * owned, width)
            return last_step(
                number, jnp.where(high == 0, upper, lower), jnp.where(high == 0, lower, upper), two_peer
            )

        return begin, forward, again

    own_rows = span(index * quarter, quarter, 16)

    def turn(slot, value):
        r.turned[slot] = value.T
        return r.turned[slot, own_rows, :]

    co_begin, co_forward, co_again = y_first(0)
    so_begin, so_forward, so_again = y_first(1)
    late_begin, late_forward, late_again = y_first(2)
    k_forward, k_again, k_finish = line_first(3)
    v_forward, v_again, v_finish = line_first(4)

    ratio = jnp.exp(rows_of(r.o_stat)[:, :LANES] - rows_of(r.log_total))
    dmixed = nt(rows_of(r.dcross), matrix(CO)).astype(BF16)
    dots = head_sums(dmixed.astype(F32) * rows_of(r.mixc).astype(F32))
    for number in range(pairs):
        cross_backward(
            number, r.qc, dmixed, r.key, r.val, r.c_probs, ratio, dots, r.dq_part
        )
    q_first = pair(r.dq_part.at[:, 1 - core], r.dq_core, c_peer)
    r.key[...] = r.c_probs[:, :LANES].reshape(width, -1).T
    q_first.wait_recv()
    r.dq_to[...] = (r.dq_part[1 - side, core].astype(F32) + r.dq_core[1 - side].astype(F32)).astype(BF16)
    q_second = pair(r.dq_to, r.dq_x, x_peer)
    r.c_probs[:, :LANES] = r.enc_here[...].T.reshape(pairs, LANES, -1)
    kv_other, kv_own = span((1 - core) * quarter, quarter, 16), span(core * quarter, quarter, 16)

    def kv_first(part, ref):
        for cols in column_tiles(width):
            product = nn(r.c_probs[:, :LANES].reshape(width, -1), ref[:, cols])
            r.gkv[part, :, :, cols] = product.astype(BF16).reshape(2, 2 * quarter, -1)
        return pair(r.gkv.at[part, :, kv_other, :], r.kv_core.at[part], c_peer)

    def kv_second(part, copy):
        copy.wait_recv()
        total = r.gkv[part, 1 - side, kv_own, :].astype(F32) + r.kv_core[part, 1 - side].astype(F32)
        r.kv_to[part] = total.astype(BF16)
        return pair(r.kv_to.at[part], r.kv_x.at[part], x_peer)

    def kv_third(part, copy):
        copy.wait_recv()
        total = r.gkv[part, side, kv_own, :].astype(F32) + r.kv_core[part, side].astype(F32)
        r.g[CK + part] = ordered(total + r.kv_x[part].astype(F32), False)

    f_second(f_piece(places[2])[...].astype(F32))
    k_copy = kv_first(0, r.key)
    q_second.wait_recv()
    dq_rows = (
        r.dq_part[side, core].astype(F32) + r.dq_core[side].astype(F32) + r.dq_x[...].astype(F32)
    ).astype(BF16)
    r.dqc[side, core] = dq_rows
    upstream = nt(dq_rows, matrix(CQ))
    y = r.after[my_rows, :]
    factor = rms_factor(y)
    gain_two = jnp.sum(upstream * y * factor, 0, keepdims=True)
    grad = r.grad_rows[...] + norm_back(y, factor, r.gains[1:2], upstream)
    low = grad.astype(BF16)
    r.dself[side, core] = low
    dself_then = spread4(r.dself)
    r.dself_rest[side, core] = (grad - low.astype(F32)).astype(BF16)
    dqc_then = spread4(r.dqc)
    r.g[CO] = ordered(nn(turn(0, rows_of(r.mixc)), rows_of(r.dcross)), True)
    co_begin(False)
    co_begin(True)
    r.val[...] = r.c_probs[:, LANES:].reshape(width, -1).T
    dself_end = dself_then()
    k_copy = kv_second(0, k_copy)
    v_copy = kv_first(1, r.val)
    dself_end()
    dqc_end = dqc_then()

    dself = rows_of(r.dself)
    r.g[SO] = ordered(nn(turn(1, r.mix[...]), dself), True)
    dmixed = nt(dself, matrix(SO)).astype(BF16)
    dqc_end()
    r.g[CQ] = ordered(nn(turn(2, r.n2[...]), rows_of(r.dqc)), True)
    so_begin(False)
    v_copy = kv_second(1, v_copy)
    rest_then = spread4(r.dself_rest)
    self_backward(dmixed, r.q, r.k, r.v, r.s_probs, r.dq, r.dk, r.dv)
    co_forward()
    kv_third(0, k_copy)
    k_forward()
    normed = turn(3, r.n1[...])
    for number, ref in ((SQ, r.dq), (SK, r.dk), (SV, r.dv)):
        r.g[number] = ordered(nn(normed, ref[...]), True)
    late_begin(False)
    so_begin(True)
    co_end = co_again()
    so_forward()
    late_begin(True)

    f_total(f_piece(far)[...].astype(F32), r.f_sum)
    both = r.f_sum[...]
    upper, lower = both[:, :fan], both[:, fan:]
    r.f_swap[...] = jnp.where(near == 0, lower, upper).astype(BF16)
    f_copy = pair(r.f_swap, r.f_swapped, y_peer)
    kept = jnp.where(near == 0, upper, lower)
    r.g_in_here[:, own_cols] = kept[0]
    r.g_out_here[:, own_cols] = kept[1]

    upstream = nt(r.dq[...], matrix(SQ)) + nt(r.dk[...], matrix(SK)) + nt(r.dv[...], matrix(SV))
    kv_third(1, v_copy)
    k_again()
    v_forward()
    late_forward()
    rest_then()()
    x = r.res[...]
    factor = rms_factor(x)
    grad = dself.astype(F32) + rows_of(r.dself_rest).astype(F32) + norm_back(x, factor, r.gains[0:1], upstream)
    r.grad_dec_here[...] = grad
    store(r.grad_dec_here, r.grad_dec)
    mine = lax.broadcasted_iota(jnp.int32, (tokens, 1), 0) // share == index
    task = jnp.sum(jnp.where(mine, grad, 0.0), 0, keepdims=True)
    r.t_buf[0, 0:3] = jnp.concatenate([task * jnp.where(chosen == i, 1.0, 0.0).astype(F32) for i in range(3)], 0)
    r.t_buf[0, 3:4] = jnp.sum(jnp.where(mine, upstream * x * factor, 0.0), 0, keepdims=True)
    r.t_buf[0, 4:5] = gain_two
    r.t_buf[0, 5:6] = gain_three
    r.t_buf[0, 6:8] = jnp.zeros((2, width), F32)
    t_first, t_second, t_third, t_fourth, t_last = ladder(r.t_buf, r.t_recv, r.t_sems)
    t_copy = t_first()
    so_end = so_again()
    hidden = hp_last()
    r.block_here[side, core] = (r.after_rows[...] + hidden).astype(BF16)
    out_then = spread4(r.block_here)
    t_copy = t_second(t_copy)
    def encoded_columns(cols):
        r.grad_enc_here[:, cols] = nt(r.key[...], matrix(CK)[cols]) + nt(r.val[...], matrix(CV)[cols])

    tiles = column_tiles(width)
    encoded_columns(tiles[0])
    t_copy = t_third(t_copy)
    out_end = out_then()
    v_again()
    k_end = k_finish()
    t_fourth(t_copy)
    for cols in tiles[1:-1]:
        encoded_columns(cols)
    late_end = late_again()
    encoded_columns(tiles[-1])
    store(r.grad_enc_here, r.grad_enc)
    co_end()
    so_end()
    v_end = v_finish()
    out_end()
    for p in range(psg):
        store(r.block_here.at[p // 2, p % 2], r.block_out.at[p])
    f_copy.wait_recv()
    r.g_in_here[:, other_cols] = r.f_swapped[0].astype(F32)
    r.g_out_here[:, other_cols] = r.f_swapped[1].astype(F32)
    store(r.g_in_here, r.g_in)
    store(r.g_out_here, r.g_out)
    r.g_vec_here[...] = lax.dot_general(
        t_last(), place.astype(F32), (((1,), (1,)), ((), ())), precision=lax.Precision.HIGHEST
    )
    store(r.g_vec_here, r.g_vec)
    k_end()
    v_end()
    late_end()
    for copy in stores:
        copy.wait()
    for run in range(len(GATHER)):
        sent_of(run)
    for copy in sent:
        copy.wait_send()


def settle_kernel(block_out, grad_dec, grad_enc, g_attn, g_in, g_out, g_vec, *rest):
    outs, vectors, here, sems = rest[:13], rest[13:17], rest[17:23], rest[23]
    sources = [grad_enc, block_out, grad_dec, g_attn, g_in, g_out]
    arrivals = [
        pltpu.make_async_copy(source, spot, sems.at[0, number])
        for number, (source, spot) in enumerate(zip(sources, here, strict=True))
    ]
    for copy in arrivals:
        copy.start()
    first = 0
    for out in vectors:
        out[...] = g_vec[first : first + out.shape[0]]
        first += out.shape[0]
    spots = [[outs[2]], [outs[0]], [outs[1]], outs[3:11], [outs[11]], [outs[12]]]
    departures = []
    for copy, spot, places in zip(arrivals, here, spots, strict=True):
        copy.wait()
        for number, out in enumerate(places):
            source = spot if len(places) == 1 else spot.at[number]
            departures.append(pltpu.make_async_copy(source, out, sems.at[1, len(departures)]))
            departures[-1].start()
    for copy in departures:
        copy.wait()


def regular(owned, psg, batch, tokens, width):
    return psg == 4 and batch == 2 * SPANS and owned % 8 == 0 and tokens % 128 == 0 and (width // 2) % LANES == 0


def fused(psg, batch, decoder_in, encoded, cotangent, task_ids, task_embed, gain_self, self_query, self_key, self_value,
          self_output, gain_cross, cross_query, cross_key, cross_value, cross_output, gain_hidden, hidden_in, hidden_out):
    _, tokens, width = decoder_in.shape
    length = encoded.shape[1]
    groups, owned = task_embed.shape
    hidden = hidden_in.shape[1]
    scratch = buffers(psg, batch, tokens, length, width, owned, hidden)
    names = INPUTS + OUTPUTS + list(scratch)
    vmem = pl.BlockSpec(memory_space=pltpu.VMEM)
    hbm = pl.BlockSpec(memory_space=pl.ANY)
    block_out, grad_decoder, grad_encoded, g_attn, g_in, g_out, g_vec = pl.pallas_call(
        functools.partial(block_kernel, names, psg, batch),
        out_shape=(
            jax.ShapeDtypeStruct((psg,) + (tokens // psg, width), BF16),
            jax.ShapeDtypeStruct((tokens, width), F32),
            jax.ShapeDtypeStruct((length, width), F32),
            jax.ShapeDtypeStruct((8, owned, width), F32),
            jax.ShapeDtypeStruct((width // batch, hidden), F32),
            jax.ShapeDtypeStruct((width // batch, hidden), F32),
            jax.ShapeDtypeStruct((8, owned), F32),
        ),
        in_specs=[pl.BlockSpec(memory_space=pltpu.SMEM)] + [hbm] * 3 + [vmem] * (len(INPUTS) - 4),
        out_specs=[hbm] * len(OUTPUTS),
        scratch_shapes=list(scratch.values()),
        compiler_params=pltpu.CompilerParams(collective_id=0, has_side_effects=True, vmem_limit_bytes=56 * MIB),
        name="decoder_block",
    )(task_ids, decoder_in[0], cotangent[0], encoded[0], task_embed, gain_self[None],
      gain_cross[None], gain_hidden[None], self_query, self_key, self_value, self_output,
      cross_query, cross_output, cross_key, cross_value, hidden_in, hidden_out.T)
    shapes = [(tokens, width), (tokens, width), (length, width)] + [(owned, width)] * 8 + [(width // batch, hidden)] * 2
    small = [(groups, owned)] + [(1, owned)] * 3
    outs = pl.pallas_call(
        settle_kernel,
        out_shape=tuple(
            jax.ShapeDtypeStruct(shape, F32 if number else BF16) for number, shape in enumerate(shapes + small)
        ),
        in_specs=[hbm] * 6 + [vmem],
        out_specs=[hbm] * len(shapes) + [vmem] * len(small),
        scratch_shapes=[
            pltpu.VMEM((length, width), F32),
            pltpu.VMEM((tokens, width), BF16),
            pltpu.VMEM((tokens, width), F32),
            pltpu.VMEM((8, owned, width), F32),
            pltpu.VMEM((width // batch, hidden), F32),
            pltpu.VMEM((width // batch, hidden), F32),
            pltpu.SemaphoreType.DMA((2, len(shapes))),
        ],
        compiler_params=pltpu.CompilerParams(vmem_limit_bytes=60 * MIB),
        name="settle",
    )(block_out.reshape(tokens, width), grad_decoder, grad_encoded, g_attn, g_in, g_out, g_vec)
    block_out, grad_decoder, grad_encoded = outs[:3]
    g_attn, (g_in, g_out) = outs[3:11], outs[11:13]
    table, gain_one, gain_two, gain_three = outs[13:]
    return (
        block_out[None],
        grad_decoder[None],
        grad_encoded[None],
        table,
        gain_one[0],
        g_attn[SQ],
        g_attn[SK],
        g_attn[SV],
        g_attn[SO],
        gain_two[0],
        g_attn[CQ],
        g_attn[CK],
        g_attn[CV],
        g_attn[CO],
        gain_three[0],
        g_in,
        g_out.T,
    )


def rms_norm(values, scales):
    factor = lax.rsqrt(jnp.mean(values * values, -1, keepdims=True) + EPSILON)
    return (values * factor * scales, factor)


def rms_back(values, factor, scales, grad_out):
    scaled = grad_out * scales
    cubed = factor * factor * factor
    lower = factor * scaled - values * cubed * jnp.mean(scaled * values, -1, keepdims=True)
    return (lower, grad_out * values * factor)


def gelu_tanh(values):
    return jax.nn.gelu(values, approximate=True)


def matmul(former, latter):
    return jnp.dot(former, latter, preferred_element_type=jnp.float32)


def inner_rows(former, latter):
    return lax.dot_general(
        former, latter, (((0,), (0,)), ((), ())), preferred_element_type=jnp.float32
    )


def outer_cols(former, latter):
    return lax.dot_general(
        former, latter, (((1,), (1,)), ((), ())), preferred_element_type=jnp.float32
    )


def split_heads(values, questions):
    return values.reshape(questions, values.shape[0] // questions, HEADS, values.shape[1] // HEADS)


def key_blocks(values):
    questions, length, width = values.shape
    shaped = values.reshape(questions, length // PASS_LEN, PASS_LEN, HEADS, width // HEADS)
    return jnp.moveaxis(shaped, 1, 0)


def block_scores(queries, key_block):
    scale = queries.shape[-1] ** (-0.5)
    return (
        jnp.einsum("bqhe,bkhe->bhqk", queries, key_block, preferred_element_type=jnp.float32)
        * scale
    )


def score_stats(queries, keys):
    questions, tokens, heads, width = queries.shape
    initial = (
        jnp.full((questions, heads, tokens), -1e30, jnp.float32),
        jnp.zeros((questions, heads, tokens), jnp.float32),
    )

    def score_advance(running, key_block):
        scores = block_scores(queries, key_block)
        highest = jnp.maximum(running[0], jnp.max(scores, -1))
        totals = running[1] * jnp.exp(running[0] - highest) + jnp.sum(
            jnp.exp(scores - highest[..., None]), -1
        )
        return ((highest, totals), None)

    return lax.scan(score_advance, initial, key_blocks(keys))[0]


def weighted_values(queries, keys, values, log_total):

    def weighted_advance(running, blocks):
        chances = jnp.exp(block_scores(queries, blocks[0]) - log_total[..., None]).astype(
            jnp.bfloat16
        )
        return (
            running
            + jnp.einsum("bhqk,bkhe->bqhe", chances, blocks[1], preferred_element_type=jnp.float32),
            None,
        )

    return lax.scan(
        weighted_advance,
        jnp.zeros(queries.shape, jnp.float32),
        (key_blocks(keys), key_blocks(values)),
    )[0]


def grad_dots(queries, keys, values, log_total, grad_out):
    questions, tokens, heads, width = queries.shape

    def grad_advance(running, blocks):
        chances = jnp.exp(block_scores(queries, blocks[0]) - log_total[..., None])
        dchance = jnp.einsum(
            "bqhe,bkhe->bhqk", grad_out, blocks[1], preferred_element_type=jnp.float32
        )
        return (running + jnp.sum(chances * dchance, -1), None)

    initial = jnp.zeros((questions, heads, tokens), jnp.float32)
    return lax.scan(grad_advance, initial, (key_blocks(keys), key_blocks(values)))[0]


def cross_back(queries, keys, values, log_total, dots, grad_out, with_keys):
    scale = queries.shape[-1] ** (-0.5)

    def cross_advance(running, blocks):
        chances = jnp.exp(block_scores(queries, blocks[0]) - log_total[..., None])
        dchance = jnp.einsum(
            "bqhe,bkhe->bhqk", grad_out, blocks[1], preferred_element_type=jnp.float32
        )
        dscore = (chances * (dchance - dots[..., None])).astype(jnp.bfloat16)
        running = (
            running
            + jnp.einsum("bhqk,bkhe->bqhe", dscore, blocks[0], preferred_element_type=jnp.float32)
            * scale
        )
        if with_keys:
            dkey = (
                jnp.einsum("bhqk,bqhe->bkhe", dscore, queries, preferred_element_type=jnp.float32)
                * scale
            ).astype(jnp.bfloat16)
            dvalue = jnp.einsum(
                "bhqk,bqhe->bkhe",
                chances.astype(jnp.bfloat16),
                grad_out,
                preferred_element_type=jnp.float32,
            ).astype(jnp.bfloat16)
            return (running, (dkey, dvalue))
        return (running, None)

    query_grad, pieces = lax.scan(
        cross_advance, jnp.zeros(queries.shape, jnp.float32), (key_blocks(keys), key_blocks(values))
    )
    if not with_keys:
        return (query_grad, None)
    questions, length, width = keys.shape
    key_grad = jnp.moveaxis(pieces[0], 0, 1).reshape(questions, length, width)
    value_grad = jnp.moveaxis(pieces[1], 0, 1).reshape(questions, length, width)
    return (query_grad, (key_grad, value_grad))


def general(
    decoder_in,
    encoded,
    cotangent,
    task_ids,
    task_embed,
    gain_self,
    self_query,
    self_key,
    self_value,
    self_output,
    gain_cross,
    cross_query,
    cross_key,
    cross_value,
    cross_output,
    gain_hidden,
    hidden_in,
    hidden_out,
):
    gathered = (
        lax.all_gather(task_embed, ("psg", "batch"), axis=1, tiled=True),
        lax.all_gather(gain_self, ("psg", "batch"), axis=0, tiled=True),
        lax.all_gather(self_query, ("psg", "batch"), axis=0, tiled=True),
        lax.all_gather(self_key, ("psg", "batch"), axis=0, tiled=True),
        lax.all_gather(self_value, ("psg", "batch"), axis=0, tiled=True),
        lax.all_gather(self_output, ("psg", "batch"), axis=0, tiled=True),
        lax.all_gather(gain_cross, ("psg", "batch"), axis=0, tiled=True),
        lax.all_gather(cross_query, ("psg", "batch"), axis=0, tiled=True),
        lax.all_gather(cross_key, ("psg", "batch"), axis=0, tiled=True),
        lax.all_gather(cross_value, ("psg", "batch"), axis=0, tiled=True),
        lax.all_gather(cross_output, ("psg", "batch"), axis=0, tiled=True),
        lax.all_gather(gain_hidden, ("psg", "batch"), axis=0, tiled=True),
    )
    (
        wide_table,
        wide_gain_self,
        wide_self_query,
        wide_self_key,
        wide_self_value,
        wide_self_output,
        wide_gain_cross,
        wide_cross_query,
        wide_cross_key,
        wide_cross_value,
        wide_cross_output,
        wide_gain_hidden,
    ) = gathered
    pieces = (
        lax.all_gather(hidden_in, "batch", axis=0, tiled=True),
        lax.all_gather(hidden_out, "batch", axis=1, tiled=True),
    )
    wide_in, wide_out = (
        lax.all_gather(pieces[0], "psg", axis=1, tiled=True),
        lax.all_gather(pieces[1], "psg", axis=0, tiled=True),
    )
    questions, tokens, width = decoder_in.shape
    rows = questions * tokens
    groups = task_embed.shape[0]
    onehot = (task_ids[:, None] == jnp.arange(groups, dtype=jnp.int32)[None, :]).astype(jnp.float32)
    embed_rows = jnp.dot(onehot, wide_table.astype(jnp.float32), precision=lax.Precision.HIGHEST)
    residual_in = (decoder_in.astype(jnp.float32) + embed_rows[:, None, :]).reshape(rows, width)
    gain_one = wide_gain_self.astype(jnp.float32)
    gain_two = wide_gain_cross.astype(jnp.float32)
    gain_three = wide_gain_hidden.astype(jnp.float32)
    normed_value, factor_one = rms_norm(residual_in, gain_one)
    normed_self = normed_value.astype(jnp.bfloat16)
    query_self = split_heads(matmul(normed_self, wide_self_query).astype(jnp.bfloat16), questions)
    key_self = split_heads(matmul(normed_self, wide_self_key).astype(jnp.bfloat16), questions)
    value_self = split_heads(matmul(normed_self, wide_self_value).astype(jnp.bfloat16), questions)
    causal = jnp.arange(tokens)[:, None] >= jnp.arange(tokens)[None, :]
    scores_self = jnp.where(causal, block_scores(query_self, key_self), MASKED)
    expo = jnp.exp(scores_self - jnp.max(scores_self, -1, keepdims=True))
    chances_self = expo / jnp.sum(expo, -1, keepdims=True)
    chances_low = chances_self.astype(jnp.bfloat16)
    mixed_self = (
        jnp.einsum("bhqk,bkhe->bqhe", chances_low, value_self, preferred_element_type=jnp.float32)
        .astype(jnp.bfloat16)
        .reshape(rows, width)
    )
    after_self = residual_in + matmul(mixed_self, wide_self_output)
    normed_value, factor_two = rms_norm(after_self, gain_two)
    normed_cross = normed_value.astype(jnp.bfloat16)
    query_cross = split_heads(
        matmul(normed_cross, wide_cross_query).astype(jnp.bfloat16), questions
    )
    encoder_rows = encoded.reshape(-1, width)
    key_cross = matmul(encoder_rows, wide_cross_key).astype(jnp.bfloat16).reshape(encoded.shape)
    value_cross = matmul(encoder_rows, wide_cross_value).astype(jnp.bfloat16).reshape(encoded.shape)
    length = encoded.shape[1]
    all_keys, all_values = (
        lax.all_gather(key_cross, "psg", axis=1, tiled=True),
        lax.all_gather(value_cross, "psg", axis=1, tiled=True),
    )
    highest, totals = score_stats(query_cross, all_keys)
    log_total = highest + jnp.log(totals)
    mixed = weighted_values(query_cross, all_keys, all_values, log_total)
    mixed_cross = mixed.astype(jnp.bfloat16).reshape(rows, width)
    after_cross = after_self + matmul(mixed_cross, wide_cross_output)
    normed_value, factor_three = rms_norm(after_cross, gain_three)
    normed_hidden = normed_value.astype(jnp.bfloat16)
    pre_act = matmul(normed_hidden, wide_in)
    activation, gelu_pull = jax.vjp(gelu_tanh, pre_act)
    act_low = activation.astype(jnp.bfloat16)
    hidden_part = matmul(act_low, wide_out)
    result = after_cross + hidden_part
    block_out = result.astype(jnp.bfloat16).reshape(decoder_in.shape)
    psg_count = lax.axis_size("psg")
    row_share = rows // psg_count
    first_row = lax.axis_index("psg") * row_share

    def own(values):
        return lax.dynamic_slice_in_dim(values, first_row, row_share, 0)

    grad_top = cotangent.reshape(rows, width)
    dhidden = outer_cols(grad_top, wide_out)
    dpre = gelu_pull(dhidden)[0].astype(jnp.bfloat16)
    term_out = inner_rows(own(act_low), own(grad_top))
    term_in = inner_rows(own(normed_hidden), own(dpre))
    dnorm_hidden = outer_cols(dpre, wide_in)
    lower, gterm_three = rms_back(after_cross, factor_three, gain_three, dnorm_hidden)
    grad_after_cross = grad_top.astype(jnp.float32) + lower
    dcross = grad_after_cross.astype(jnp.bfloat16)
    term_cross_output = inner_rows(own(mixed_cross), own(dcross))
    dmixed_cross = split_heads(
        outer_cols(dcross, wide_cross_output).astype(jnp.bfloat16), questions
    )
    dots_cross = grad_dots(query_cross, all_keys, all_values, log_total, dmixed_cross)
    query_own, key_pair = cross_back(
        query_cross, key_cross, value_cross, log_total, dots_cross, dmixed_cross, True
    )
    begin = (lax.axis_index("psg") + 1) * length
    span = (psg_count - 1) * length
    other_keys = lax.dynamic_slice_in_dim(jnp.concatenate([all_keys, all_keys], 1), begin, span, 1)
    other_values = lax.dynamic_slice_in_dim(
        jnp.concatenate([all_values, all_values], 1), begin, span, 1
    )
    query_rest = cross_back(
        query_cross, other_keys, other_values, log_total, dots_cross, dmixed_cross, False
    )[0]
    query_grad = query_own + query_rest
    dquery_cross = query_grad.astype(jnp.bfloat16).reshape(rows, width)
    dkey_rows = key_pair[0].reshape(-1, width)
    dvalue_rows = key_pair[1].reshape(-1, width)
    grad_encoded = (
        outer_cols(dkey_rows, wide_cross_key) + outer_cols(dvalue_rows, wide_cross_value)
    ).reshape(encoded.shape)
    term_cross_key = inner_rows(encoder_rows, dkey_rows)
    term_cross_value = inner_rows(encoder_rows, dvalue_rows)
    term_cross_query = inner_rows(own(normed_cross), own(dquery_cross))
    dnorm_cross = outer_cols(dquery_cross, wide_cross_query)
    lower, gterm_two = rms_back(after_self, factor_two, gain_two, dnorm_cross)
    grad_after_self = grad_after_cross + lower
    dself = grad_after_self.astype(jnp.bfloat16)
    term_self_output = inner_rows(own(mixed_self), own(dself))
    dmixed_self = split_heads(outer_cols(dself, wide_self_output).astype(jnp.bfloat16), questions)
    dchance = jnp.einsum(
        "bqhe,bkhe->bhqk", dmixed_self, value_self, preferred_element_type=jnp.float32
    )
    dots_self = jnp.sum(chances_self * dchance, -1, keepdims=True)
    dscore = (chances_self * (dchance - dots_self)).astype(jnp.bfloat16)
    scale = query_self.shape[-1] ** (-0.5)
    dquery_self = (
        (
            jnp.einsum("bhqk,bkhe->bqhe", dscore, key_self, preferred_element_type=jnp.float32)
            * scale
        )
        .astype(jnp.bfloat16)
        .reshape(rows, width)
    )
    dkey_self = (
        (
            jnp.einsum("bhqk,bqhe->bkhe", dscore, query_self, preferred_element_type=jnp.float32)
            * scale
        )
        .astype(jnp.bfloat16)
        .reshape(rows, width)
    )
    dvalue_self = (
        jnp.einsum("bhqk,bqhe->bkhe", chances_low, dmixed_self, preferred_element_type=jnp.float32)
        .astype(jnp.bfloat16)
        .reshape(rows, width)
    )
    dnorm_self = (
        outer_cols(dquery_self, wide_self_query)
        + outer_cols(dkey_self, wide_self_key)
        + outer_cols(dvalue_self, wide_self_value)
    )
    normed_own = own(normed_self)
    term_self_query = inner_rows(normed_own, own(dquery_self))
    term_self_key = inner_rows(normed_own, own(dkey_self))
    term_self_value = inner_rows(normed_own, own(dvalue_self))
    lower, gterm_one = rms_back(residual_in, factor_one, gain_one, dnorm_self)
    grad_decoder = grad_after_self + lower
    row_hot = jnp.repeat(onehot, tokens, 0)
    term_table = lax.dot_general(
        own(row_hot), own(grad_decoder), (((0,), (0,)), ((), ())), precision=lax.Precision.HIGHEST
    )
    sums = (
        lax.psum_scatter(term_table, ("psg", "batch"), scatter_dimension=1, tiled=True),
        lax.psum_scatter(
            jnp.sum(own(gterm_one), 0), ("psg", "batch"), scatter_dimension=0, tiled=True
        ),
        lax.psum_scatter(term_self_query, ("psg", "batch"), scatter_dimension=0, tiled=True),
        lax.psum_scatter(term_self_key, ("psg", "batch"), scatter_dimension=0, tiled=True),
        lax.psum_scatter(term_self_value, ("psg", "batch"), scatter_dimension=0, tiled=True),
        lax.psum_scatter(term_self_output, ("psg", "batch"), scatter_dimension=0, tiled=True),
        lax.psum_scatter(
            jnp.sum(own(gterm_two), 0), ("psg", "batch"), scatter_dimension=0, tiled=True
        ),
        lax.psum_scatter(term_cross_query, ("psg", "batch"), scatter_dimension=0, tiled=True),
        lax.psum_scatter(term_cross_key, ("psg", "batch"), scatter_dimension=0, tiled=True),
        lax.psum_scatter(term_cross_value, ("psg", "batch"), scatter_dimension=0, tiled=True),
        lax.psum_scatter(term_cross_output, ("psg", "batch"), scatter_dimension=0, tiled=True),
        lax.psum_scatter(
            jnp.sum(own(gterm_three), 0), ("psg", "batch"), scatter_dimension=0, tiled=True
        ),
    )
    hidden_pair = (
        lax.psum_scatter(
            term_in.astype(jnp.bfloat16), "psg", scatter_dimension=1, tiled=True
        ).astype(jnp.float32),
        lax.psum_scatter(
            term_out.astype(jnp.bfloat16), "psg", scatter_dimension=0, tiled=True
        ).astype(jnp.float32),
    )
    hidden_grads = (
        lax.psum_scatter(hidden_pair[0], "batch", scatter_dimension=0, tiled=True),
        lax.psum_scatter(hidden_pair[1], "batch", scatter_dimension=1, tiled=True),
    )
    return (
        block_out,
        grad_decoder.reshape(decoder_in.shape),
        grad_encoded,
        sums[0],
        sums[1],
        sums[2],
        sums[3],
        sums[4],
        sums[5],
        sums[6],
        sums[7],
        sums[8],
        sums[9],
        sums[10],
        sums[11],
        hidden_grads[0],
        hidden_grads[1],
    )


def local(psg, batch, *arrays):
    decoder_in, gain = arrays[0], arrays[5]
    if regular(gain.shape[0], psg, batch, decoder_in.shape[1], decoder_in.shape[2]) and decoder_in.shape[0] == 1:
        return fused(psg, batch, *arrays)
    return general(*arrays)


def solution(mesh):
    line, spread = P("batch", None, None), P("batch", "psg", None)
    flat, rows = P(("psg", "batch")), P(("psg", "batch"), None)
    table, wide, tall = P(None, ("psg", "batch")), P("batch", "psg"), P("psg", "batch")
    return jax.shard_map(
        functools.partial(local, mesh.shape["psg"], mesh.shape["batch"]),
        mesh=mesh,
        in_specs=(line, spread, line, P("batch"), table) + ((flat,) + (rows,) * 4) * 2 + (flat, wide, tall),
        out_specs=(line, line, spread, table) + ((flat,) + (rows,) * 4) * 2 + (flat, wide, tall),
        check_vma=False,
    )
```

```python
import functools
import types

import jax
import jax.numpy as jnp
from jax import lax
from jax.experimental import pallas as pl
from jax.experimental.pallas import tpu as pltpu
from jax.sharding import PartitionSpec as P

SPANS = 4
HEADS = 12
PASS_LEN = 192
EPSILON = 1e-06
MASKED = -1000000000.0
LANES = 128
MIB = 2**20
ENCODED_PARTS = 3
PAIRS = 80
LEAVING = 24

F32 = jnp.float32
BF16 = jnp.bfloat16
ID = pl.DeviceIdType.MESH

CK, CV, CO, CQ, SO, SK, SQ, SV = range(8)
GATHER = ((CK, 2, False), (SK, 3, False), (SO, 1, True), (CQ, 1, True), (CO, 1, True))
REDUCE = ((CO, 1, True), (CQ, 2, True), (SK, 3, True), (CK, 1, False), (CV, 1, False))


def nn(former, latter):
    return jnp.dot(former, latter, preferred_element_type=F32)


def nt(former, latter):
    return lax.dot_general(former, latter, (((1,), (1,)), ((), ())), preferred_element_type=F32)


def rms_factor(values):
    return lax.rsqrt(jnp.mean(values * values, -1, keepdims=True) + EPSILON)


def norm_back(values, factor, scales, grad_out):
    scaled = grad_out * scales
    cubed = factor * factor * factor
    return factor * scaled - values * cubed * jnp.mean(scaled * values, -1, keepdims=True)


def lane_is_low():
    return lax.broadcasted_iota(jnp.int32, (1, LANES), 1) < LANES // 2


def stack_heads(pair):
    low = lane_is_low()
    zero = jnp.zeros_like(pair)
    return jnp.concatenate([jnp.where(low, pair, zero), jnp.where(low, zero, pair)], 0)


def merge_heads(stacked):
    half = stacked.shape[0] // 2
    return jnp.where(lane_is_low(), stacked[:half], stacked[half:])


def stack_stat(stats, pair):
    return jnp.concatenate([stats[:, 2 * pair : 2 * pair + 1], stats[:, 2 * pair + 1 : 2 * pair + 2]], 0)


def spread_stat(stats, pair):
    return jnp.where(
        lane_is_low(), stats[:, 2 * pair : 2 * pair + 1], stats[:, 2 * pair + 1 : 2 * pair + 2]
    )


def column_tiles(width, size=256):
    return [slice(first, min(first + size, width)) for first in range(0, width, size)]


def pair_lanes(pair):
    return slice(pair * LANES, (pair + 1) * LANES)


def self_forward(dec, row, g1, wq, wk, wv, wo, g2, res, n1, q, k, v, probs, mix, after, n2):
    x = dec + row
    res[...] = x
    normed = (x * rms_factor(x) * g1).astype(BF16)
    n1[...] = normed
    q[...] = nn(normed, wq).astype(BF16)
    k[...] = nn(normed, wk).astype(BF16)
    v[...] = nn(normed, wv).astype(BF16)
    tokens, width = x.shape
    scale = (width // HEADS) ** (-0.5)
    rows = lax.broadcasted_iota(jnp.int32, (2 * tokens, tokens), 0) % tokens
    causal = rows >= lax.broadcasted_iota(jnp.int32, (2 * tokens, tokens), 1)
    for pair in range(HEADS // 2):
        cols = pair_lanes(pair)
        scores = jnp.where(causal, nt(stack_heads(q[:, cols]), k[:, cols]) * scale, MASKED)
        expo = jnp.exp(scores - jnp.max(scores, -1, keepdims=True))
        chances = expo * (1.0 / jnp.sum(expo, -1, keepdims=True))
        probs[pair] = chances
        mix[:, cols] = merge_heads(nn(chances.astype(BF16), v[:, cols])).astype(BF16)
    y = x + nn(mix[...], wo)
    after[...] = y
    n2[...] = (y * rms_factor(y) * g2).astype(BF16)


def cross_attend(qc, key, val, probs, stat, part):
    tokens, width = qc.shape
    share = tokens // 4
    scale = (width // HEADS) ** (-0.5)
    lane = lax.broadcasted_iota(jnp.int32, (tokens, LANES), 1)
    tops = jnp.zeros((tokens, LANES), F32)
    sums = jnp.ones((tokens, LANES), F32)
    for pair in range(HEADS // 2):
        cols = pair_lanes(pair)
        scores = nt(stack_heads(qc[:, cols]), key[:, cols]) * scale
        top = jnp.max(scores, -1, keepdims=True)
        expo = jnp.exp(scores - top)
        total = jnp.sum(expo, -1, keepdims=True)
        low = expo.astype(BF16)
        probs[pair] = low
        mixed = merge_heads(nn(low, val[:, cols]) * (1.0 / total)).astype(BF16)
        for p in range(4):
            part[p // 2, p % 2, :, cols] = mixed[p * share : (p + 1) * share]
        for half in range(2):
            rows = slice(half * tokens, (half + 1) * tokens)
            here = lane == 2 * pair + half
            tops = jnp.where(here, top[rows], tops)
            sums = jnp.where(here, total[rows], sums)
    for p in range(4):
        rows = slice(p * share, (p + 1) * share)
        stat[p // 2, p % 2, :, :LANES] = tops[rows]
        stat[p // 2, p % 2, :, LANES:] = sums[rows]


def join_parts(o_a, s_a, o_b, s_b, out, stat):
    top_a, top_b = s_a[:, :LANES], s_b[:, :LANES]
    top = jnp.maximum(top_a, top_b)
    w_a = jnp.exp(top_a - top) * s_a[:, LANES:]
    w_b = jnp.exp(top_b - top) * s_b[:, LANES:]
    total = w_a + w_b
    inverse = 1.0 / total
    w_a, w_b = w_a * inverse, w_b * inverse
    for pair in range(HEADS // 2):
        cols = pair_lanes(pair)
        mixed = spread_stat(w_a, pair) * o_a[:, cols].astype(F32) + spread_stat(w_b, pair) * o_b[:, cols].astype(F32)
        out[:, cols] = mixed.astype(out.dtype)
    stat[:, :LANES] = top
    stat[:, LANES:] = total


def feed_forward(x, top, w_in, w_out):
    pre = nn(x, w_in)
    root = (2.0 / jnp.pi) ** 0.5
    square = pre * pre
    bend = jnp.tanh(root * (pre + 0.044715 * (square * pre)))
    act = (0.5 * pre * (1.0 + bend)).astype(BF16)
    slope = 0.5 * (1.0 + bend) + 0.5 * pre * (1.0 - bend * bend) * (root * (1.0 + 3 * 0.044715 * square))
    dpre = (nn(top, w_out) * slope).astype(BF16)
    return act, dpre


def head_sums(product):
    lane = lax.broadcasted_iota(jnp.int32, (product.shape[0], LANES), 1)
    sums = jnp.zeros(lane.shape, F32)
    low = lane_is_low()
    for pair in range(HEADS // 2):
        here = product[:, pair_lanes(pair)]
        sums = jnp.where(lane == 2 * pair, jnp.sum(jnp.where(low, here, 0.0), -1, keepdims=True), sums)
        sums = jnp.where(lane == 2 * pair + 1, jnp.sum(jnp.where(low, 0.0, here), -1, keepdims=True), sums)
    return sums


def cross_backward(pair, qc, dmixed, key, val, probs, ratio, dots, part):
    tokens, width = qc.shape
    share = tokens // 4
    scale = (width // HEADS) ** (-0.5)
    cols = pair_lanes(pair)
    q2 = stack_heads(qc[:, cols])
    d2 = stack_heads(dmixed[:, cols])
    chances = probs[pair].astype(F32) * stack_stat(ratio, pair)
    dchance = nt(d2, val[:, cols])
    dscore = (chances * (dchance - stack_stat(dots, pair))).astype(BF16)
    dquery = (merge_heads(nn(dscore, key[:, cols])) * scale).astype(BF16)
    for p in range(4):
        part[p // 2, p % 2, :, cols] = dquery[p * share : (p + 1) * share]
    probs[pair, :LANES] = (nn(q2.T, dscore) * scale).astype(BF16)
    probs[pair, LANES:] = nn(d2.T, chances.astype(BF16)).astype(BF16)


def self_backward(dmixed, q, k, v, probs, dq, dk, dv):
    width = q.shape[1]
    scale = (width // HEADS) ** (-0.5)
    for pair in range(HEADS // 2):
        cols = pair_lanes(pair)
        q2 = stack_heads(q[:, cols])
        d2 = stack_heads(dmixed[:, cols])
        chances = probs[pair]
        dchance = nt(d2, v[:, cols])
        dscore = chances * (dchance - jnp.sum(chances * dchance, -1, keepdims=True))
        low = dscore.astype(BF16)
        dq[:, cols] = (merge_heads(nn(low, k[:, cols])) * scale).astype(BF16)
        dk[:, cols] = (nn(low.T, q2) * scale).astype(BF16)
        dv[:, cols] = nn(chances.astype(BF16).T, d2).astype(BF16)


INPUTS = ["tid", "dec", "cot", "enc", "table", "g_one", "g_two", "g_three", "sq", "sk", "sv", "so", "cq", "co", "ck", "cv", "h_in", "h_out"]
OUTPUTS = ["block_out", "grad_dec", "grad_enc", "g_attn", "g_in", "g_out", "g_vec"]


def buffers(psg, batch, tokens, length, width, owned, hidden):
    spans, pairs, share, half = batch // 2, HEADS // 2, tokens // psg, width // 2
    dma = pltpu.SemaphoreType.DMA
    whole = (tokens, width)
    quad = (2, 2, share)
    band = 2 * owned
    runs = len(GATHER)

    def low(*shape):
        return pltpu.VMEM(shape, BF16)

    def full(*shape):
        return pltpu.VMEM(shape, F32)

    out = dict(
        w=low(8, 2, 2 * batch * owned, width),
        f=low(2, width, hidden // 2),
        m_send=low(4, band, half),
        m_recv=low(4, band, half),
        v_buf=full(4, 8, width),
        v_recv=full(3 + spans, 8, width),
        cots=low(2, tokens, width),
        dec_here=low(tokens, width),
        enc_here=low(length, width),
        block_here=low(*quad, width),
        grad_dec_here=full(*whole),
        grad_enc_here=full(length, width),
        g_attn_here=full(8, owned, width),
        g_in_here=full(width // batch, hidden),
        g_out_here=full(width // batch, hidden),
        g_vec_here=full(8, owned),
        load=dma((3,)),
        store=dma((16,)),
        key=low(length, width),
        val=low(length, width),
        c_probs=low(pairs, 2 * tokens, length),
        s_probs=full(pairs, 2 * tokens, tokens),
        res=full(*whole),
        after=full(*whole),
        n1=low(*whole),
        n2=low(*whole),
        q=low(*whole),
        k=low(*whole),
        v=low(*whole),
        mix=low(*whole),
        qc=low(*whole),
        o_part=low(*quad, width),
        o_stat=full(*quad, 2 * LANES),
        o_core=low(2, share, width),
        o_core_stat=full(2, share, 2 * LANES),
        o_to=low(share, width),
        o_to_stat=full(share, 2 * LANES),
        o_mid=full(share, width),
        o_mid_stat=full(share, 2 * LANES),
        o_x=low(share, width),
        o_x_stat=full(share, 2 * LANES),
        mixed_rows=full(share, width),
        stat_rows=full(share, 2 * LANES),
        after_rows=full(share, width),
        n3=low(2, *quad, width),
        mixc=low(*quad, width),
        log_total=full(*quad, LANES),
        dn=low(2, *quad, width),
        dn_core=low(2, 2, share, width),
        dn_to=low(3, share, width),
        dn_got=low(3, share, width),
        hp=low(2, *quad, width),
        hp_core=low(2, 2, share, width),
        hp_to=low(3, share, width),
        hp_got=low(3, share, width),
        grad_rows=full(share, width),
        dcross=low(*quad, width),
        dq_part=low(*quad, width),
        dq_core=low(2, share, width),
        dq_to=low(share, width),
        dq_x=low(share, width),
        dqc=low(*quad, width),
        dself=low(*quad, width),
        dself_rest=low(*quad, width),
        dq=low(*whole),
        dk=low(*whole),
        dv=low(*whole),
        turned=low(4, width, tokens),
        gf=low(2, width, hidden // 2),
        gkv=low(2, 2, 2 * batch * owned, width),
        kv_core=low(2, 2, batch * owned, width),
        kv_to=low(2, batch * owned, width),
        kv_x=low(2, batch * owned, width),
        g=low(8, batch * owned, width),
        gains=full(8, width),
        t_buf=full(4, 8, width),
        t_recv=full(3 + spans, 8, width),
        f_swap=low(2, width // batch, hidden // 2),
        f_swapped=low(2, width // batch, hidden // 2),
        f_came=low(3, 2, width // spans, hidden // 2),
        f_sum=full(2, width // spans, hidden // 2),
        one_send=dma((LEAVING,)),
        one_recv=dma((PAIRS,)),
        a_recv=dma((runs, 2 * batch)),
        a_send=dma((runs, 4)),
        a_core=dma((runs,)),
        w_recv=dma((spans,)),
        w_send=dma((3,)),
        v_sems=dma((2, spans)),
        t_sems=dma((2, spans)),
        f_line=dma((6,)),
    )
    for number, (_, count, y_first) in enumerate(REDUCE):
        rows = -(-count * owned // 16) * 16
        if y_first:
            out[f"r{number}_y"] = low(2, count, band, width)
            out[f"r{number}_one"] = low(count, band, width)
            out[f"r{number}_own"] = full(count * owned, width)
        else:
            out[f"r{number}_one"] = low(2 * band, width)
            out[f"r{number}_two_to"] = low(band, width)
            out[f"r{number}_two"] = low(band, width)
            out[f"r{number}_own"] = full(band, width)
        out[f"r{number}_last_to"] = low(rows, width)
        out[f"r{number}_last"] = low(rows, width)
    return out


def block_kernel(names, psg, batch, *refs):
    r = types.SimpleNamespace(**dict(zip(names, refs, strict=True)))
    index, question = lax.axis_index("psg"), lax.axis_index("batch")
    far, near = question // 2, question % 2
    side, core = index // 2, index % 2
    x_peer = ((1 - side) * 2 + core, question)
    c_peer = (side * 2 + 1 - core, question)
    y_peer = (index, far * 2 + 1 - near)
    d_peer = ((1 - side) * 2 + core, far * 2 + 1 - near)
    places = [far, far + 1 - 2 * (far % 2), lax.rem(far + 2, SPANS), SPANS - 1 - far]
    column = [(index, z * 2 + near) for z in places[1:]]
    one_peer, two_peer = column[0], column[1]
    tokens, width = r.dec_here.shape
    owned = r.sq.shape[0]
    band, quarter, half = 2 * owned, batch * owned, width // 2
    share = tokens // psg
    fan = width // batch
    shards = (r.ck, r.cv, r.co, r.cq, r.so, r.sk, r.sq, r.sv)
    pairs = HEADS // 2

    def aligned(value, to):
        return value if isinstance(value, int) else pl.multiple_of(value, to)

    def span(start, size, to):
        return pl.ds(aligned(start, to), size)

    def lanes(h):
        return span(h * half, half, LANES)

    sent = []

    def go(copy):
        copy.start()
        sent.append(copy)

    def remote(src, dst, send, recv, device):
        return pltpu.make_async_remote_copy(
            src_ref=src, dst_ref=dst, send_sem=send, recv_sem=recv, device_id=device, device_id_type=ID
        )

    numbers = iter(range(PAIRS))
    leaving = []

    def pair(src, dst, device):
        number = next(numbers)
        if number >= LEAVING:
            leaving[number - LEAVING].wait_send()
        copy = remote(src, dst, r.one_send.at[number % LEAVING], r.one_recv.at[number], device)
        copy.start()
        leaving.append(copy)
        return copy

    loads = [
        pltpu.make_async_copy(r.cot, r.cots.at[near], r.load.at[0]),
        pltpu.make_async_copy(r.dec, r.dec_here, r.load.at[1]),
        pltpu.make_async_copy(r.enc, r.enc_here, r.load.at[2]),
    ]
    for copy in loads:
        copy.start()
    stores = []

    def store(src, dst):
        copy = pltpu.make_async_copy(src, dst, r.store.at[len(stores)])
        copy.start()
        stores.append(copy)

    barrier = pltpu.get_barrier_semaphore()
    greeted = column + [y_peer, x_peer, c_peer, d_peer]
    for other in greeted:
        pl.semaphore_signal(barrier, inc=1, device_id=other, device_id_type=ID)
    pl.semaphore_wait(barrier, len(greeted))

    def pack(number):
        first, second = shards[2 * number], shards[2 * number + 1]
        both = jnp.concatenate([first[:, lanes(1 - near)].astype(F32), second[:, lanes(1 - near)].astype(F32)], 0)
        r.m_send[number] = both.astype(BF16)

    def exchange(first, count):
        for number in range(first, first + count):
            pack(number)
        return pair(r.m_send.at[first : first + count], r.m_recv.at[first : first + count], y_peer)

    row = core * quarter + far * band

    def join(number):
        other = r.m_recv[number].astype(F32)
        for part in range(2):
            mine = shards[2 * number + part][:, lanes(near)].astype(F32)
            theirs = other[part * owned : (part + 1) * owned]
            block = jnp.where(near == 0, jnp.concatenate([mine, theirs], 0), jnp.concatenate([theirs, mine], 0))
            r.w[2 * number + part, side, span(row, band, 16), lanes(near)] = block.astype(BF16)

    def unit(run, x, c, z, h):
        first, count, joined = GATHER[run]
        rows = span(c * quarter + z * band, band, 16)
        return r.w.at[first : first + count, slice(None) if joined else x, rows, lanes(h)]

    def landing(run, x, c, z, h):
        return r.a_recv.at[run, (0 if GATHER[run][2] else x) * batch + z * 2 + h]

    def hand(run, x, c, z, h, kind, device, recv=None):
        spot = unit(run, x, c, z, h)
        remote(spot, spot, r.a_send.at[run, kind], landing(run, x, c, z, h) if recv is None else recv, device).start()

    def landed(run, x, c, z, h):
        spot = unit(run, x, c, z, h)
        remote(spot, spot, r.a_send.at[run, 0], landing(run, x, c, z, h), c_peer).wait_recv()

    held = []

    def wide(run, z, h, hold=False):
        to_x = functools.partial(hand, run, side, core, z, h, 2, x_peer)
        if hold:
            held.append(to_x)
        elif not GATHER[run][2]:
            to_x()
        hand(run, side, core, z, h, 3, c_peer, r.a_core.at[run])

    def offer(run):
        hand(run, side, core, far, near, 0, two_peer)
        hand(run, side, core, far, near, 0, one_peer)
        hand(run, side, core, far, near, 1, y_peer)
        wide(run, far, near)

    def from_y(run, step, hold=False):
        landed(run, side, core, places[step], 1 - near)
        wide(run, places[step], 1 - near, hold)

    def from_line(run, step, hold=False):
        z = places[step]
        landed(run, side, core, z, near)
        if step == 2:
            hand(run, side, core, z, near, 0, one_peer)
        hand(run, side, core, z, near, 1, y_peer)
        wide(run, z, near, hold)

    def from_x(run, step):
        z = places[step]
        for h in (near, 1 - near):
            landed(run, 1 - side, core, z, h)
            hand(run, 1 - side, core, z, h, 3, c_peer, r.a_core.at[run])

    def sent_of(run):
        first, count, joined = GATHER[run]
        lower = r.w.at[first : first + count, slice(None) if joined else 0]
        quarters = (slice(None),) * (2 if joined else 1)
        sizes = [
            lower.at[(*quarters, pl.ds(0, 3 * band), pl.ds(0, half))],
            lower.at[(*quarters, pl.ds(0, quarter), pl.ds(0, half))],
            None if joined else lower.at[(*quarters, pl.ds(0, quarter), slice(None))],
            r.w.at[first : first + count, :, pl.ds(0, quarter), :],
        ]
        for kind, size in enumerate(sizes):
            if size is not None:
                remote(size, size, r.a_send.at[run, kind], r.a_core.at[run], c_peer).wait_send()

    def complete(run):
        first, count, _ = GATHER[run]
        all_of = r.w.at[first : first + count, :, span((1 - core) * quarter, quarter, 16), :]
        remote(all_of, all_of, r.a_send.at[run, 0], r.a_core.at[run], c_peer).wait_recv()

    def matrix(number):
        return r.w[number].reshape(width, width)

    m_kv = exchange(0, 1)
    m_self = exchange(2, 2)
    m_tail = exchange(1, 1)

    def ladder(buf, recv, sems):
        def first():
            return pair(buf.at[0], recv.at[0], c_peer)

        def second(copy):
            copy.wait_recv()
            buf[1] = (buf[0].astype(F32) + recv[0].astype(F32)).astype(buf.dtype)
            return pair(buf.at[1], recv.at[1], x_peer)

        def third(copy):
            copy.wait_recv()
            buf[2] = (buf[1].astype(F32) + recv[1].astype(F32)).astype(buf.dtype)
            return pair(buf.at[2], recv.at[2], y_peer)

        def fourth(copy):
            copy.wait_recv()
            buf[3] = (buf[2].astype(F32) + recv[2].astype(F32)).astype(buf.dtype)
            for z in places[1:]:
                go(remote(buf.at[3], recv.at[3 + far], sems.at[0, z], sems.at[1, far], (index, z * 2 + near)))

        def last():
            total = buf[3].astype(F32)
            for z in places[1:]:
                remote(buf.at[3], recv.at[3 + z], sems.at[0, z], sems.at[1, z], c_peer).wait_recv()
                total = total + recv[3 + z].astype(F32)
            return total

        return first, second, third, fourth, last

    device = index * batch + question
    place = jnp.where(
        lax.broadcasted_iota(jnp.int32, (owned, width), 1)
        == lax.broadcasted_iota(jnp.int32, (owned, width), 0) + device * owned,
        1.0,
        0.0,
    ).astype(BF16)
    r.v_buf[0, 0:3] = nn(r.table[...], place)
    for number, gain in enumerate((r.g_one, r.g_two, r.g_three)):
        r.v_buf[0, 3 + number : 4 + number] = nn(gain[...], place)
    r.v_buf[0, 6:8] = jnp.zeros((2, width), F32)
    v_first, v_second, v_third, v_fourth, v_last = ladder(r.v_buf, r.v_recv, r.v_sems)
    v_copy = v_first()

    m_kv.wait_recv()
    join(0)
    offer(0)
    m_self.wait_recv()
    join(2)
    join(3)
    offer(1)
    m_tail.wait_recv()
    join(1)
    own_tail = r.w.at[CO : CO + 3, side, span(row, band, 16), lanes(near)]
    x_tail = pair(own_tail, own_tail, x_peer)
    v_copy = v_second(v_copy)

    cut = r.f.shape[2]
    other_cols = span((1 - near) * cut, cut, LANES)
    own_cols = span(near * cut, cut, LANES)
    own_fan = span(question * fan, fan, 16)
    r.f[0, own_fan] = r.h_in[:, own_cols]
    r.f[1, own_fan] = r.h_out[:, own_cols]

    def f_unit(z):
        return r.f.at[:, span(z * 2 * fan, 2 * fan, 16), :]

    def f_hand(z, sem, device):
        go(remote(f_unit(z), f_unit(z), sem, r.w_recv.at[z], device))

    def f_landed(step):
        z = places[step]
        remote(f_unit(z), f_unit(z), r.w_send.at[0], r.w_recv.at[z], c_peer).wait_recv()
        if step == 2:
            f_hand(z, r.w_send.at[2], one_peer)

    def near_units(run, hold=False):
        from_y(run, 0, hold)
        from_line(run, 2, hold)
        from_line(run, 1, hold)

    def far_units(run):
        from_line(run, 3)
        from_y(run, 1)
        from_y(run, 2)

    near_units(0)
    far_units(0)
    near_units(1, True)
    x_tail.wait_recv()
    offer(2)
    from_y(0, 3)
    for to_x in held:
        to_x()
    far_units(1)
    near_units(2)
    offer(3)
    v_copy = v_third(v_copy)
    for step in range(3):
        from_x(0, step)
    from_y(1, 3)
    h_copies = [
        pair(r.h_in.at[:, other_cols], r.f.at[0, own_fan], y_peer),
        pair(r.h_out.at[:, other_cols], r.f.at[1, own_fan], y_peer),
    ]
    far_units(2)
    from_x(1, 0)
    offer(4)
    from_x(0, 3)
    near_units(3)
    complete(0)
    loads[2].wait()
    for cols in column_tiles(width):
        r.key[:, cols] = nn(r.enc_here[...], r.w[CK, :, :, cols].reshape(width, -1)).astype(BF16)
        r.val[:, cols] = nn(r.enc_here[...], r.w[CV, :, :, cols].reshape(width, -1)).astype(BF16)
    v_fourth(v_copy)
    from_y(2, 3)
    far_units(3)
    from_x(1, 1)
    from_x(1, 2)
    near_units(4)
    from_y(3, 3)
    from_x(1, 3)
    for copy in h_copies:
        copy.wait_recv()
    f_hand(far, r.w_send.at[0], two_peer)
    f_hand(far, r.w_send.at[1], one_peer)
    loads[0].wait()
    loads[1].wait()
    cot_copy = pair(r.cots.at[near], r.cots.at[near], y_peer)
    complete(1)
    complete(2)
    vectors = v_last()

    gains = [vectors[3 + i : 4 + i] for i in range(3)]
    chosen = r.tid[0]
    row_embed = functools.reduce(
        jnp.add, [vectors[i : i + 1] * jnp.where(chosen == i, 1.0, 0.0).astype(F32) for i in range(3)]
    )
    r.gains[0:3] = vectors[3:6]
    self_forward(
        r.dec_here[...].astype(F32), row_embed, gains[0], matrix(SQ), matrix(SK), matrix(SV), matrix(SO), gains[1],
        r.res, r.n1, r.q, r.k, r.v, r.s_probs, r.mix, r.after, r.n2,
    )
    far_units(4)
    complete(3)
    r.qc[...] = nn(r.n2[...], matrix(CQ)).astype(BF16)

    cross_attend(r.qc, r.key, r.val, r.c_probs, r.o_stat, r.o_part)
    first = [pair(r.o_part.at[:, 1 - core], r.o_core, c_peer), pair(r.o_stat.at[:, 1 - core], r.o_core_stat, c_peer)]
    from_y(4, 3)
    for copy in first:
        copy.wait_recv()
    join_parts(
        r.o_part[1 - side, core], r.o_stat[1 - side, core], r.o_core[1 - side], r.o_core_stat[1 - side],
        r.o_to, r.o_to_stat,
    )
    second = [pair(r.o_to, r.o_x, x_peer), pair(r.o_to_stat, r.o_x_stat, x_peer)]
    join_parts(
        r.o_part[side, core], r.o_stat[side, core], r.o_core[side], r.o_core_stat[side], r.o_mid, r.o_mid_stat
    )
    f_landed(2)
    f_landed(1)
    complete(4)
    for copy in second:
        copy.wait_recv()
    join_parts(r.o_mid[...], r.o_mid_stat[...], r.o_x[...], r.o_x_stat[...], r.mixed_rows, r.stat_rows)
    my_rows = span(index * share, share, 16)
    r.log_total[side, core] = r.stat_rows[:, :LANES] + jnp.log(r.stat_rows[:, LANES:])
    mixed_low = r.mixed_rows[...].astype(BF16)
    r.mixc[side, core] = mixed_low
    y = r.after[my_rows, :] + nn(mixed_low, matrix(CO))
    r.after_rows[...] = y
    r.n3[near, side, core] = (y * rms_factor(y) * r.gains[2:3]).astype(BF16)

    def block8(h, x, c):
        return r.n3.at[h, x, c]

    def spread4(buf):
        spot = buf.at[side, core]
        over_x, over_c = pair(spot, spot, x_peer), pair(spot, spot, c_peer)

        def then():
            over_x.wait_recv()
            onward = buf.at[1 - side, core]
            last = pair(onward, onward, c_peer)

            def end():
                over_c.wait_recv()
                last.wait_recv()

            return end

        return then

    mine = block8(near, side, core)
    to_y, to_x, to_d, to_c = [pair(mine, mine, peer) for peer in (y_peer, x_peer, d_peer, c_peer)]
    onward = [to_c]
    for copy, h, x in ((to_y, 1 - near, side), (to_x, near, 1 - side), (to_d, 1 - near, 1 - side)):
        copy.wait_recv()
        onward.append(pair(block8(h, x, core), block8(h, x, core), c_peer))
    f_landed(3)
    cot_copy.wait_recv()
    for copy in onward:
        copy.wait_recv()

    log_then = spread4(r.log_total)
    mixc_then = spread4(r.mixc)
    x = r.n3[...].reshape(2 * tokens, width)
    top = r.cots[...].reshape(2 * tokens, width)
    act, dpre = feed_forward(x, top, r.f[0], r.f[1])
    r.dn[...] = nt(dpre, r.f[0]).astype(BF16).reshape(r.dn.shape)

    def shrink8(part, got_c, to, got):
        over_c = pair(part.at[:, :, 1 - core], got_c, c_peer)

        def second():
            over_c.wait_recv()

            def total(h, x):
                return part[h, x, core].astype(F32) + got_c[h, x].astype(F32)

            copies = []
            for slot, (h, x, peer) in enumerate(
                ((1 - near, 1 - side, d_peer), (near, 1 - side, x_peer), (1 - near, side, y_peer))
            ):
                to[slot] = total(h, x).astype(BF16)
                copies.append(pair(to.at[slot], got.at[slot], peer))

            def last():
                out = total(near, side)
                for slot, copy in enumerate(copies):
                    copy.wait_recv()
                    out = out + got[slot].astype(F32)
                return out

            return last

        return second

    dn_second = shrink8(r.dn, r.dn_core, r.dn_to, r.dn_got)
    r.hp[...] = nt(act, r.f[1]).astype(BF16).reshape(r.hp.shape)
    dn_last = dn_second()
    hp_second = shrink8(r.hp, r.hp_core, r.hp_to, r.hp_got)
    r.gf[0] = nn(x.T, dpre).astype(BF16)
    r.gf[1] = nn(top.T, act).astype(BF16)

    def line_kit(came, src, sems):
        def over_pair(step):
            slot = step // 2
            return remote(src(places[step]), came.at[slot], sems.at[slot], sems.at[3 + slot], one_peer)

        def over_pairs():
            return remote(src(places[2]), came.at[2], sems.at[2], sems.at[5], two_peer)

        def first():
            go(over_pair(3))
            go(over_pair(1))

        def second(value):
            over_pair(3).wait_recv()
            src(places[2])[...] = (value + came[1].astype(F32)).astype(BF16)
            go(over_pairs())

        def total(value, out):
            over_pair(1).wait_recv()
            both = value + came[0].astype(F32)
            over_pairs().wait_recv()
            out[...] = both + came[2].astype(F32)

        return first, second, total

    def f_piece(z):
        return r.gf.at[:, span(z * 2 * fan, 2 * fan, 16), :]

    f_first, f_second, f_total = line_kit(r.f_came, f_piece, r.f_line)
    f_first()
    log_end = log_then()
    mixc_end = mixc_then()

    upstream = dn_last()
    y = r.after_rows[...]
    factor = rms_factor(y)
    scales = r.gains[2:3]
    gain_three = jnp.sum(upstream * y * factor, 0, keepdims=True)
    grad = r.cots[near, my_rows, :].astype(F32) + norm_back(y, factor, scales, upstream)
    r.grad_rows[...] = grad
    low = grad.astype(BF16)
    r.dcross[side, core] = low
    dcross_then = spread4(r.dcross)
    hp_last = hp_second()
    log_end()
    mixc_end()
    dcross_end = dcross_then()
    dcross_end()

    def rows_of(ref):
        return ref[...].reshape(tokens, ref.shape[-1])

    parity, high = far % 2, far // 2

    def ordered(value, y_first):
        blocks = [(z, h) for z in range(SPANS) for h in range(2)]
        if y_first:
            blocks.sort(key=lambda block: (block[1], block[0] % 2, block[0] // 2))
        else:
            blocks.sort(key=lambda block: (block[0] % 2, block[0] // 2, block[1]))
        parts = [value[(z * 2 + h) * owned : (z * 2 + h + 1) * owned] for z, h in blocks]
        return jnp.concatenate(parts, 0).astype(BF16)

    def last_step(number, mine, theirs, peer):
        first, count, _ = REDUCE[number]
        to, got = getattr(r, f"r{number}_last_to"), getattr(r, f"r{number}_last")
        if to.shape[0] > theirs.shape[0]:
            theirs = jnp.concatenate([theirs, jnp.zeros((to.shape[0] - theirs.shape[0], width), F32)], 0)
        to[...] = theirs.astype(BF16)
        copy = pair(to, got, peer)
        r.g_attn_here[first : first + count] = mine.reshape(count, owned, width)

        def end():
            copy.wait_recv()
            more = got[...].astype(F32)[: count * owned]
            r.g_attn_here[first : first + count] = r.g_attn_here[first : first + count] + more.reshape(count, owned, width)
            store(r.g_attn_here.at[first : first + count], r.g_attn.at[first : first + count])

        return end

    def line_first(number):
        m = REDUCE[number][0]
        one, two_to, two, own = [getattr(r, f"r{number}_{name}") for name in ("one", "two_to", "two", "own")]
        copies = []

        def forward():
            copies.append(pair(r.g.at[m, span((1 - parity) * 2 * band, 2 * band, 16), :], one, one_peer))

        def again():
            copies[0].wait_recv()
            total = r.g[m, span(parity * 2 * band, 2 * band, 16), :].astype(F32) + one[...].astype(F32)
            upper, lower = total[:band], total[band:]
            two_to[...] = jnp.where(high == 0, lower, upper).astype(BF16)
            copies.append(pair(two_to, two, two_peer))
            own[...] = jnp.where(high == 0, upper, lower)

        def finish():
            copies[1].wait_recv()
            total = own[...] + two[...].astype(F32)
            upper, lower = total[:owned], total[owned:]
            return last_step(
                number, jnp.where(near == 0, upper, lower), jnp.where(near == 0, lower, upper), y_peer
            )

        return forward, again, finish

    def y_first(number):
        first, count, _ = REDUCE[number]
        got_y, one = getattr(r, f"r{number}_y"), getattr(r, f"r{number}_one")
        copies = {}

        def piece(h, p):
            return r.g.at[first : first + count, span(h * 2 * band + p * band, band, 16), :]

        def begin(mine):
            p = parity if mine else 1 - parity
            copies[mine] = pair(piece(1 - near, p), got_y.at[1 if mine else 0], y_peer)

        def value(mine):
            copies[mine].wait_recv()
            return piece(near, parity if mine else 1 - parity)[...].astype(F32) + got_y[1 if mine else 0].astype(F32)

        def forward():
            got_y[0] = value(False).astype(BF16)
            copies["one"] = pair(got_y.at[0], one, one_peer)

        def again():
            total = value(True)
            copies["one"].wait_recv()
            total = total + one[...].astype(F32)
            upper = total[:, :owned].reshape(count * owned, width)
            lower = total[:, owned:].reshape(count * owned, width)
            return last_step(
                number, jnp.where(high == 0, upper, lower), jnp.where(high == 0, lower, upper), two_peer
            )

        return begin, forward, again

    own_rows = span(index * quarter, quarter, 16)

    def turn(slot, value):
        r.turned[slot] = value.T
        return r.turned[slot, own_rows, :]

    co_begin, co_forward, co_again = y_first(0)
    so_begin, so_forward, so_again = y_first(1)
    late_begin, late_forward, late_again = y_first(2)
    k_forward, k_again, k_finish = line_first(3)
    v_forward, v_again, v_finish = line_first(4)

    ratio = jnp.exp(rows_of(r.o_stat)[:, :LANES] - rows_of(r.log_total))
    dmixed = nt(rows_of(r.dcross), matrix(CO)).astype(BF16)
    dots = head_sums(dmixed.astype(F32) * rows_of(r.mixc).astype(F32))
    for number in range(pairs):
        cross_backward(
            number, r.qc, dmixed, r.key, r.val, r.c_probs, ratio, dots, r.dq_part
        )
    q_first = pair(r.dq_part.at[:, 1 - core], r.dq_core, c_peer)
    r.key[...] = r.c_probs[:, :LANES].reshape(width, -1).T
    q_first.wait_recv()
    r.dq_to[...] = (r.dq_part[1 - side, core].astype(F32) + r.dq_core[1 - side].astype(F32)).astype(BF16)
    q_second = pair(r.dq_to, r.dq_x, x_peer)
    r.c_probs[:, :LANES] = r.enc_here[...].T.reshape(pairs, LANES, -1)
    kv_other, kv_own = span((1 - core) * quarter, quarter, 16), span(core * quarter, quarter, 16)

    def kv_first(part, ref):
        for cols in column_tiles(width):
            product = nn(r.c_probs[:, :LANES].reshape(width, -1), ref[:, cols])
            r.gkv[part, :, :, cols] = product.astype(BF16).reshape(2, 2 * quarter, -1)
        return pair(r.gkv.at[part, :, kv_other, :], r.kv_core.at[part], c_peer)

    def kv_second(part, copy):
        copy.wait_recv()
        total = r.gkv[part, 1 - side, kv_own, :].astype(F32) + r.kv_core[part, 1 - side].astype(F32)
        r.kv_to[part] = total.astype(BF16)
        return pair(r.kv_to.at[part], r.kv_x.at[part], x_peer)

    def kv_third(part, copy):
        copy.wait_recv()
        total = r.gkv[part, side, kv_own, :].astype(F32) + r.kv_core[part, side].astype(F32)
        r.g[CK + part] = ordered(total + r.kv_x[part].astype(F32), False)

    f_second(f_piece(places[2])[...].astype(F32))
    k_copy = kv_first(0, r.key)
    q_second.wait_recv()
    dq_rows = (
        r.dq_part[side, core].astype(F32) + r.dq_core[side].astype(F32) + r.dq_x[...].astype(F32)
    ).astype(BF16)
    r.dqc[side, core] = dq_rows
    upstream = nt(dq_rows, matrix(CQ))
    y = r.after[my_rows, :]
    factor = rms_factor(y)
    gain_two = jnp.sum(upstream * y * factor, 0, keepdims=True)
    grad = r.grad_rows[...] + norm_back(y, factor, r.gains[1:2], upstream)
    low = grad.astype(BF16)
    r.dself[side, core] = low
    dself_then = spread4(r.dself)
    r.dself_rest[side, core] = (grad - low.astype(F32)).astype(BF16)
    dqc_then = spread4(r.dqc)
    r.g[CO] = ordered(nn(turn(0, rows_of(r.mixc)), rows_of(r.dcross)), True)
    co_begin(False)
    co_begin(True)
    r.val[...] = r.c_probs[:, LANES:].reshape(width, -1).T
    dself_end = dself_then()
    k_copy = kv_second(0, k_copy)
    v_copy = kv_first(1, r.val)
    dself_end()
    dqc_end = dqc_then()

    dself = rows_of(r.dself)
    r.g[SO] = ordered(nn(turn(1, r.mix[...]), dself), True)
    dmixed = nt(dself, matrix(SO)).astype(BF16)
    dqc_end()
    r.g[CQ] = ordered(nn(turn(2, r.n2[...]), rows_of(r.dqc)), True)
    so_begin(False)
    v_copy = kv_second(1, v_copy)
    rest_then = spread4(r.dself_rest)
    self_backward(dmixed, r.q, r.k, r.v, r.s_probs, r.dq, r.dk, r.dv)
    co_forward()
    kv_third(0, k_copy)
    k_forward()
    normed = turn(3, r.n1[...])
    for number, ref in ((SQ, r.dq), (SK, r.dk), (SV, r.dv)):
        r.g[number] = ordered(nn(normed, ref[...]), True)
    late_begin(False)
    so_begin(True)
    co_end = co_again()
    so_forward()
    late_begin(True)

    f_total(f_piece(far)[...].astype(F32), r.f_sum)
    both = r.f_sum[...]
    upper, lower = both[:, :fan], both[:, fan:]
    r.f_swap[...] = jnp.where(near == 0, lower, upper).astype(BF16)
    f_copy = pair(r.f_swap, r.f_swapped, y_peer)
    kept = jnp.where(near == 0, upper, lower)
    r.g_in_here[:, own_cols] = kept[0]
    r.g_out_here[:, own_cols] = kept[1]

    upstream = nt(r.dq[...], matrix(SQ)) + nt(r.dk[...], matrix(SK)) + nt(r.dv[...], matrix(SV))
    kv_third(1, v_copy)
    k_again()
    v_forward()
    late_forward()
    rest_then()()
    x = r.res[...]
    factor = rms_factor(x)
    grad = dself.astype(F32) + rows_of(r.dself_rest).astype(F32) + norm_back(x, factor, r.gains[0:1], upstream)
    r.grad_dec_here[...] = grad
    store(r.grad_dec_here, r.grad_dec)
    mine = lax.broadcasted_iota(jnp.int32, (tokens, 1), 0) // share == index
    task = jnp.sum(jnp.where(mine, grad, 0.0), 0, keepdims=True)
    r.t_buf[0, 0:3] = jnp.concatenate([task * jnp.where(chosen == i, 1.0, 0.0).astype(F32) for i in range(3)], 0)
    r.t_buf[0, 3:4] = jnp.sum(jnp.where(mine, upstream * x * factor, 0.0), 0, keepdims=True)
    r.t_buf[0, 4:5] = gain_two
    r.t_buf[0, 5:6] = gain_three
    r.t_buf[0, 6:8] = jnp.zeros((2, width), F32)
    t_first, t_second, t_third, t_fourth, t_last = ladder(r.t_buf, r.t_recv, r.t_sems)
    t_copy = t_first()
    so_end = so_again()
    hidden = hp_last()
    r.block_here[side, core] = (r.after_rows[...] + hidden).astype(BF16)
    out_then = spread4(r.block_here)
    t_copy = t_second(t_copy)
    def encoded_columns(cols):
        r.grad_enc_here[:, cols] = nt(r.key[...], matrix(CK)[cols]) + nt(r.val[...], matrix(CV)[cols])

    tiles = column_tiles(width)
    encoded_columns(tiles[0])
    t_copy = t_third(t_copy)
    out_end = out_then()
    v_again()
    k_end = k_finish()
    t_fourth(t_copy)
    for cols in tiles[1:-1]:
        encoded_columns(cols)
    late_end = late_again()
    encoded_columns(tiles[-1])
    store(r.grad_enc_here, r.grad_enc)
    co_end()
    so_end()
    v_end = v_finish()
    out_end()
    for p in range(psg):
        store(r.block_here.at[p // 2, p % 2], r.block_out.at[p])
    f_copy.wait_recv()
    r.g_in_here[:, other_cols] = r.f_swapped[0].astype(F32)
    r.g_out_here[:, other_cols] = r.f_swapped[1].astype(F32)
    store(r.g_in_here, r.g_in)
    store(r.g_out_here, r.g_out)
    r.g_vec_here[...] = lax.dot_general(
        t_last(), place.astype(F32), (((1,), (1,)), ((), ())), precision=lax.Precision.HIGHEST
    )
    store(r.g_vec_here, r.g_vec)
    k_end()
    v_end()
    late_end()
    for copy in stores:
        copy.wait()
    for run in range(len(GATHER)):
        sent_of(run)
    for copy in sent + leaving[-LEAVING:]:
        copy.wait_send()


def settle_kernel(block_out, grad_dec, grad_enc, g_attn, g_in, g_out, g_vec, *rest):
    outs, vectors, here, sems = rest[:13], rest[13:17], rest[17:23], rest[23]
    rows = grad_enc.shape[0] // ENCODED_PARTS
    parts = [pl.ds(number * rows, rows) for number in range(ENCODED_PARTS)]
    moves = [(grad_enc.at[part], here[0].at[part], [outs[2].at[part]]) for part in parts]
    moves += [
        (block_out, here[1], [outs[0]]),
        (grad_dec, here[2], [outs[1]]),
        (g_in, here[4], [outs[11]]),
        (g_out, here[5], [outs[12]]),
        (g_attn, here[3], outs[3:11]),
    ]
    arrivals = [
        pltpu.make_async_copy(source, spot, sems.at[0, number]) for number, (source, spot, _) in enumerate(moves)
    ]
    for copy in arrivals:
        copy.start()
    first = 0
    for out in vectors:
        out[...] = g_vec[first : first + out.shape[0]]
        first += out.shape[0]
    departures = []
    for copy, (_, spot, places) in zip(arrivals, moves, strict=True):
        copy.wait()
        for number, out in enumerate(places):
            source = spot if len(places) == 1 else spot.at[number]
            departures.append(pltpu.make_async_copy(source, out, sems.at[1, len(departures)]))
            departures[-1].start()
    for copy in departures:
        copy.wait()


def regular(owned, psg, batch, tokens, width):
    return psg == 4 and batch == 2 * SPANS and owned % 8 == 0 and tokens % 128 == 0 and (width // 2) % LANES == 0


def fused(psg, batch, decoder_in, encoded, cotangent, task_ids, task_embed, gain_self, self_query, self_key, self_value,
          self_output, gain_cross, cross_query, cross_key, cross_value, cross_output, gain_hidden, hidden_in, hidden_out):
    _, tokens, width = decoder_in.shape
    length = encoded.shape[1]
    groups, owned = task_embed.shape
    hidden = hidden_in.shape[1]
    scratch = buffers(psg, batch, tokens, length, width, owned, hidden)
    names = INPUTS + OUTPUTS + list(scratch)
    vmem = pl.BlockSpec(memory_space=pltpu.VMEM)
    hbm = pl.BlockSpec(memory_space=pl.ANY)
    block_out, grad_decoder, grad_encoded, g_attn, g_in, g_out, g_vec = pl.pallas_call(
        functools.partial(block_kernel, names, psg, batch),
        out_shape=(
            jax.ShapeDtypeStruct((psg,) + (tokens // psg, width), BF16),
            jax.ShapeDtypeStruct((tokens, width), F32),
            jax.ShapeDtypeStruct((length, width), F32),
            jax.ShapeDtypeStruct((8, owned, width), F32),
            jax.ShapeDtypeStruct((width // batch, hidden), F32),
            jax.ShapeDtypeStruct((width // batch, hidden), F32),
            jax.ShapeDtypeStruct((8, owned), F32),
        ),
        in_specs=[pl.BlockSpec(memory_space=pltpu.SMEM)] + [hbm] * 3 + [vmem] * (len(INPUTS) - 4),
        out_specs=[hbm] * len(OUTPUTS),
        scratch_shapes=list(scratch.values()),
        compiler_params=pltpu.CompilerParams(collective_id=0, has_side_effects=True, vmem_limit_bytes=56 * MIB),
        name="decoder_block",
    )(task_ids, decoder_in[0], cotangent[0], encoded[0], task_embed, gain_self[None],
      gain_cross[None], gain_hidden[None], self_query, self_key, self_value, self_output,
      cross_query, cross_output, cross_key, cross_value, hidden_in, hidden_out.T)
    shapes = [(tokens, width), (tokens, width), (length, width)] + [(owned, width)] * 8 + [(width // batch, hidden)] * 2
    small = [(groups, owned)] + [(1, owned)] * 3
    outs = pl.pallas_call(
        settle_kernel,
        out_shape=tuple(
            jax.ShapeDtypeStruct(shape, F32 if number else BF16) for number, shape in enumerate(shapes + small)
        ),
        in_specs=[hbm] * 6 + [vmem],
        out_specs=[hbm] * len(shapes) + [vmem] * len(small),
        scratch_shapes=[
            pltpu.VMEM((length, width), F32),
            pltpu.VMEM((tokens, width), BF16),
            pltpu.VMEM((tokens, width), F32),
            pltpu.VMEM((8, owned, width), F32),
            pltpu.VMEM((width // batch, hidden), F32),
            pltpu.VMEM((width // batch, hidden), F32),
            pltpu.SemaphoreType.DMA((2, len(shapes) + ENCODED_PARTS)),
        ],
        compiler_params=pltpu.CompilerParams(vmem_limit_bytes=60 * MIB),
        name="settle",
    )(block_out.reshape(tokens, width), grad_decoder, grad_encoded, g_attn, g_in, g_out, g_vec)
    block_out, grad_decoder, grad_encoded = outs[:3]
    g_attn, (g_in, g_out) = outs[3:11], outs[11:13]
    table, gain_one, gain_two, gain_three = outs[13:]
    return (
        block_out[None],
        grad_decoder[None],
        grad_encoded[None],
        table,
        gain_one[0],
        g_attn[SQ],
        g_attn[SK],
        g_attn[SV],
        g_attn[SO],
        gain_two[0],
        g_attn[CQ],
        g_attn[CK],
        g_attn[CV],
        g_attn[CO],
        gain_three[0],
        g_in,
        g_out.T,
    )


def rms_norm(values, scales):
    factor = lax.rsqrt(jnp.mean(values * values, -1, keepdims=True) + EPSILON)
    return (values * factor * scales, factor)


def rms_back(values, factor, scales, grad_out):
    scaled = grad_out * scales
    cubed = factor * factor * factor
    lower = factor * scaled - values * cubed * jnp.mean(scaled * values, -1, keepdims=True)
    return (lower, grad_out * values * factor)


def gelu_tanh(values):
    return jax.nn.gelu(values, approximate=True)


def matmul(former, latter):
    return jnp.dot(former, latter, preferred_element_type=jnp.float32)


def inner_rows(former, latter):
    return lax.dot_general(
        former, latter, (((0,), (0,)), ((), ())), preferred_element_type=jnp.float32
    )


def outer_cols(former, latter):
    return lax.dot_general(
        former, latter, (((1,), (1,)), ((), ())), preferred_element_type=jnp.float32
    )


def split_heads(values, questions):
    return values.reshape(questions, values.shape[0] // questions, HEADS, values.shape[1] // HEADS)


def key_blocks(values):
    questions, length, width = values.shape
    shaped = values.reshape(questions, length // PASS_LEN, PASS_LEN, HEADS, width // HEADS)
    return jnp.moveaxis(shaped, 1, 0)


def block_scores(queries, key_block):
    scale = queries.shape[-1] ** (-0.5)
    return (
        jnp.einsum("bqhe,bkhe->bhqk", queries, key_block, preferred_element_type=jnp.float32)
        * scale
    )


def score_stats(queries, keys):
    questions, tokens, heads, width = queries.shape
    initial = (
        jnp.full((questions, heads, tokens), -1e30, jnp.float32),
        jnp.zeros((questions, heads, tokens), jnp.float32),
    )

    def score_advance(running, key_block):
        scores = block_scores(queries, key_block)
        highest = jnp.maximum(running[0], jnp.max(scores, -1))
        totals = running[1] * jnp.exp(running[0] - highest) + jnp.sum(
            jnp.exp(scores - highest[..., None]), -1
        )
        return ((highest, totals), None)

    return lax.scan(score_advance, initial, key_blocks(keys))[0]


def weighted_values(queries, keys, values, log_total):

    def weighted_advance(running, blocks):
        chances = jnp.exp(block_scores(queries, blocks[0]) - log_total[..., None]).astype(
            jnp.bfloat16
        )
        return (
            running
            + jnp.einsum("bhqk,bkhe->bqhe", chances, blocks[1], preferred_element_type=jnp.float32),
            None,
        )

    return lax.scan(
        weighted_advance,
        jnp.zeros(queries.shape, jnp.float32),
        (key_blocks(keys), key_blocks(values)),
    )[0]


def grad_dots(queries, keys, values, log_total, grad_out):
    questions, tokens, heads, width = queries.shape

    def grad_advance(running, blocks):
        chances = jnp.exp(block_scores(queries, blocks[0]) - log_total[..., None])
        dchance = jnp.einsum(
            "bqhe,bkhe->bhqk", grad_out, blocks[1], preferred_element_type=jnp.float32
        )
        return (running + jnp.sum(chances * dchance, -1), None)

    initial = jnp.zeros((questions, heads, tokens), jnp.float32)
    return lax.scan(grad_advance, initial, (key_blocks(keys), key_blocks(values)))[0]


def cross_back(queries, keys, values, log_total, dots, grad_out, with_keys):
    scale = queries.shape[-1] ** (-0.5)

    def cross_advance(running, blocks):
        chances = jnp.exp(block_scores(queries, blocks[0]) - log_total[..., None])
        dchance = jnp.einsum(
            "bqhe,bkhe->bhqk", grad_out, blocks[1], preferred_element_type=jnp.float32
        )
        dscore = (chances * (dchance - dots[..., None])).astype(jnp.bfloat16)
        running = (
            running
            + jnp.einsum("bhqk,bkhe->bqhe", dscore, blocks[0], preferred_element_type=jnp.float32)
            * scale
        )
        if with_keys:
            dkey = (
                jnp.einsum("bhqk,bqhe->bkhe", dscore, queries, preferred_element_type=jnp.float32)
                * scale
            ).astype(jnp.bfloat16)
            dvalue = jnp.einsum(
                "bhqk,bqhe->bkhe",
                chances.astype(jnp.bfloat16),
                grad_out,
                preferred_element_type=jnp.float32,
            ).astype(jnp.bfloat16)
            return (running, (dkey, dvalue))
        return (running, None)

    query_grad, pieces = lax.scan(
        cross_advance, jnp.zeros(queries.shape, jnp.float32), (key_blocks(keys), key_blocks(values))
    )
    if not with_keys:
        return (query_grad, None)
    questions, length, width = keys.shape
    key_grad = jnp.moveaxis(pieces[0], 0, 1).reshape(questions, length, width)
    value_grad = jnp.moveaxis(pieces[1], 0, 1).reshape(questions, length, width)
    return (query_grad, (key_grad, value_grad))


def general(
    decoder_in,
    encoded,
    cotangent,
    task_ids,
    task_embed,
    gain_self,
    self_query,
    self_key,
    self_value,
    self_output,
    gain_cross,
    cross_query,
    cross_key,
    cross_value,
    cross_output,
    gain_hidden,
    hidden_in,
    hidden_out,
):
    gathered = (
        lax.all_gather(task_embed, ("psg", "batch"), axis=1, tiled=True),
        lax.all_gather(gain_self, ("psg", "batch"), axis=0, tiled=True),
        lax.all_gather(self_query, ("psg", "batch"), axis=0, tiled=True),
        lax.all_gather(self_key, ("psg", "batch"), axis=0, tiled=True),
        lax.all_gather(self_value, ("psg", "batch"), axis=0, tiled=True),
        lax.all_gather(self_output, ("psg", "batch"), axis=0, tiled=True),
        lax.all_gather(gain_cross, ("psg", "batch"), axis=0, tiled=True),
        lax.all_gather(cross_query, ("psg", "batch"), axis=0, tiled=True),
        lax.all_gather(cross_key, ("psg", "batch"), axis=0, tiled=True),
        lax.all_gather(cross_value, ("psg", "batch"), axis=0, tiled=True),
        lax.all_gather(cross_output, ("psg", "batch"), axis=0, tiled=True),
        lax.all_gather(gain_hidden, ("psg", "batch"), axis=0, tiled=True),
    )
    (
        wide_table,
        wide_gain_self,
        wide_self_query,
        wide_self_key,
        wide_self_value,
        wide_self_output,
        wide_gain_cross,
        wide_cross_query,
        wide_cross_key,
        wide_cross_value,
        wide_cross_output,
        wide_gain_hidden,
    ) = gathered
    pieces = (
        lax.all_gather(hidden_in, "batch", axis=0, tiled=True),
        lax.all_gather(hidden_out, "batch", axis=1, tiled=True),
    )
    wide_in, wide_out = (
        lax.all_gather(pieces[0], "psg", axis=1, tiled=True),
        lax.all_gather(pieces[1], "psg", axis=0, tiled=True),
    )
    questions, tokens, width = decoder_in.shape
    rows = questions * tokens
    groups = task_embed.shape[0]
    onehot = (task_ids[:, None] == jnp.arange(groups, dtype=jnp.int32)[None, :]).astype(jnp.float32)
    embed_rows = jnp.dot(onehot, wide_table.astype(jnp.float32), precision=lax.Precision.HIGHEST)
    residual_in = (decoder_in.astype(jnp.float32) + embed_rows[:, None, :]).reshape(rows, width)
    gain_one = wide_gain_self.astype(jnp.float32)
    gain_two = wide_gain_cross.astype(jnp.float32)
    gain_three = wide_gain_hidden.astype(jnp.float32)
    normed_value, factor_one = rms_norm(residual_in, gain_one)
    normed_self = normed_value.astype(jnp.bfloat16)
    query_self = split_heads(matmul(normed_self, wide_self_query).astype(jnp.bfloat16), questions)
    key_self = split_heads(matmul(normed_self, wide_self_key).astype(jnp.bfloat16), questions)
    value_self = split_heads(matmul(normed_self, wide_self_value).astype(jnp.bfloat16), questions)
    causal = jnp.arange(tokens)[:, None] >= jnp.arange(tokens)[None, :]
    scores_self = jnp.where(causal, block_scores(query_self, key_self), MASKED)
    expo = jnp.exp(scores_self - jnp.max(scores_self, -1, keepdims=True))
    chances_self = expo / jnp.sum(expo, -1, keepdims=True)
    chances_low = chances_self.astype(jnp.bfloat16)
    mixed_self = (
        jnp.einsum("bhqk,bkhe->bqhe", chances_low, value_self, preferred_element_type=jnp.float32)
        .astype(jnp.bfloat16)
        .reshape(rows, width)
    )
    after_self = residual_in + matmul(mixed_self, wide_self_output)
    normed_value, factor_two = rms_norm(after_self, gain_two)
    normed_cross = normed_value.astype(jnp.bfloat16)
    query_cross = split_heads(
        matmul(normed_cross, wide_cross_query).astype(jnp.bfloat16), questions
    )
    encoder_rows = encoded.reshape(-1, width)
    key_cross = matmul(encoder_rows, wide_cross_key).astype(jnp.bfloat16).reshape(encoded.shape)
    value_cross = matmul(encoder_rows, wide_cross_value).astype(jnp.bfloat16).reshape(encoded.shape)
    length = encoded.shape[1]
    all_keys, all_values = (
        lax.all_gather(key_cross, "psg", axis=1, tiled=True),
        lax.all_gather(value_cross, "psg", axis=1, tiled=True),
    )
    highest, totals = score_stats(query_cross, all_keys)
    log_total = highest + jnp.log(totals)
    mixed = weighted_values(query_cross, all_keys, all_values, log_total)
    mixed_cross = mixed.astype(jnp.bfloat16).reshape(rows, width)
    after_cross = after_self + matmul(mixed_cross, wide_cross_output)
    normed_value, factor_three = rms_norm(after_cross, gain_three)
    normed_hidden = normed_value.astype(jnp.bfloat16)
    pre_act = matmul(normed_hidden, wide_in)
    activation, gelu_pull = jax.vjp(gelu_tanh, pre_act)
    act_low = activation.astype(jnp.bfloat16)
    hidden_part = matmul(act_low, wide_out)
    result = after_cross + hidden_part
    block_out = result.astype(jnp.bfloat16).reshape(decoder_in.shape)
    psg_count = lax.axis_size("psg")
    row_share = rows // psg_count
    first_row = lax.axis_index("psg") * row_share

    def own(values):
        return lax.dynamic_slice_in_dim(values, first_row, row_share, 0)

    grad_top = cotangent.reshape(rows, width)
    dhidden = outer_cols(grad_top, wide_out)
    dpre = gelu_pull(dhidden)[0].astype(jnp.bfloat16)
    term_out = inner_rows(own(act_low), own(grad_top))
    term_in = inner_rows(own(normed_hidden), own(dpre))
    dnorm_hidden = outer_cols(dpre, wide_in)
    lower, gterm_three = rms_back(after_cross, factor_three, gain_three, dnorm_hidden)
    grad_after_cross = grad_top.astype(jnp.float32) + lower
    dcross = grad_after_cross.astype(jnp.bfloat16)
    term_cross_output = inner_rows(own(mixed_cross), own(dcross))
    dmixed_cross = split_heads(
        outer_cols(dcross, wide_cross_output).astype(jnp.bfloat16), questions
    )
    dots_cross = grad_dots(query_cross, all_keys, all_values, log_total, dmixed_cross)
    query_own, key_pair = cross_back(
        query_cross, key_cross, value_cross, log_total, dots_cross, dmixed_cross, True
    )
    begin = (lax.axis_index("psg") + 1) * length
    span = (psg_count - 1) * length
    other_keys = lax.dynamic_slice_in_dim(jnp.concatenate([all_keys, all_keys], 1), begin, span, 1)
    other_values = lax.dynamic_slice_in_dim(
        jnp.concatenate([all_values, all_values], 1), begin, span, 1
    )
    query_rest = cross_back(
        query_cross, other_keys, other_values, log_total, dots_cross, dmixed_cross, False
    )[0]
    query_grad = query_own + query_rest
    dquery_cross = query_grad.astype(jnp.bfloat16).reshape(rows, width)
    dkey_rows = key_pair[0].reshape(-1, width)
    dvalue_rows = key_pair[1].reshape(-1, width)
    grad_encoded = (
        outer_cols(dkey_rows, wide_cross_key) + outer_cols(dvalue_rows, wide_cross_value)
    ).reshape(encoded.shape)
    term_cross_key = inner_rows(encoder_rows, dkey_rows)
    term_cross_value = inner_rows(encoder_rows, dvalue_rows)
    term_cross_query = inner_rows(own(normed_cross), own(dquery_cross))
    dnorm_cross = outer_cols(dquery_cross, wide_cross_query)
    lower, gterm_two = rms_back(after_self, factor_two, gain_two, dnorm_cross)
    grad_after_self = grad_after_cross + lower
    dself = grad_after_self.astype(jnp.bfloat16)
    term_self_output = inner_rows(own(mixed_self), own(dself))
    dmixed_self = split_heads(outer_cols(dself, wide_self_output).astype(jnp.bfloat16), questions)
    dchance = jnp.einsum(
        "bqhe,bkhe->bhqk", dmixed_self, value_self, preferred_element_type=jnp.float32
    )
    dots_self = jnp.sum(chances_self * dchance, -1, keepdims=True)
    dscore = (chances_self * (dchance - dots_self)).astype(jnp.bfloat16)
    scale = query_self.shape[-1] ** (-0.5)
    dquery_self = (
        (
            jnp.einsum("bhqk,bkhe->bqhe", dscore, key_self, preferred_element_type=jnp.float32)
            * scale
        )
        .astype(jnp.bfloat16)
        .reshape(rows, width)
    )
    dkey_self = (
        (
            jnp.einsum("bhqk,bqhe->bkhe", dscore, query_self, preferred_element_type=jnp.float32)
            * scale
        )
        .astype(jnp.bfloat16)
        .reshape(rows, width)
    )
    dvalue_self = (
        jnp.einsum("bhqk,bqhe->bkhe", chances_low, dmixed_self, preferred_element_type=jnp.float32)
        .astype(jnp.bfloat16)
        .reshape(rows, width)
    )
    dnorm_self = (
        outer_cols(dquery_self, wide_self_query)
        + outer_cols(dkey_self, wide_self_key)
        + outer_cols(dvalue_self, wide_self_value)
    )
    normed_own = own(normed_self)
    term_self_query = inner_rows(normed_own, own(dquery_self))
    term_self_key = inner_rows(normed_own, own(dkey_self))
    term_self_value = inner_rows(normed_own, own(dvalue_self))
    lower, gterm_one = rms_back(residual_in, factor_one, gain_one, dnorm_self)
    grad_decoder = grad_after_self + lower
    row_hot = jnp.repeat(onehot, tokens, 0)
    term_table = lax.dot_general(
        own(row_hot), own(grad_decoder), (((0,), (0,)), ((), ())), precision=lax.Precision.HIGHEST
    )
    sums = (
        lax.psum_scatter(term_table, ("psg", "batch"), scatter_dimension=1, tiled=True),
        lax.psum_scatter(
            jnp.sum(own(gterm_one), 0), ("psg", "batch"), scatter_dimension=0, tiled=True
        ),
        lax.psum_scatter(term_self_query, ("psg", "batch"), scatter_dimension=0, tiled=True),
        lax.psum_scatter(term_self_key, ("psg", "batch"), scatter_dimension=0, tiled=True),
        lax.psum_scatter(term_self_value, ("psg", "batch"), scatter_dimension=0, tiled=True),
        lax.psum_scatter(term_self_output, ("psg", "batch"), scatter_dimension=0, tiled=True),
        lax.psum_scatter(
            jnp.sum(own(gterm_two), 0), ("psg", "batch"), scatter_dimension=0, tiled=True
        ),
        lax.psum_scatter(term_cross_query, ("psg", "batch"), scatter_dimension=0, tiled=True),
        lax.psum_scatter(term_cross_key, ("psg", "batch"), scatter_dimension=0, tiled=True),
        lax.psum_scatter(term_cross_value, ("psg", "batch"), scatter_dimension=0, tiled=True),
        lax.psum_scatter(term_cross_output, ("psg", "batch"), scatter_dimension=0, tiled=True),
        lax.psum_scatter(
            jnp.sum(own(gterm_three), 0), ("psg", "batch"), scatter_dimension=0, tiled=True
        ),
    )
    hidden_pair = (
        lax.psum_scatter(
            term_in.astype(jnp.bfloat16), "psg", scatter_dimension=1, tiled=True
        ).astype(jnp.float32),
        lax.psum_scatter(
            term_out.astype(jnp.bfloat16), "psg", scatter_dimension=0, tiled=True
        ).astype(jnp.float32),
    )
    hidden_grads = (
        lax.psum_scatter(hidden_pair[0], "batch", scatter_dimension=0, tiled=True),
        lax.psum_scatter(hidden_pair[1], "batch", scatter_dimension=1, tiled=True),
    )
    return (
        block_out,
        grad_decoder.reshape(decoder_in.shape),
        grad_encoded,
        sums[0],
        sums[1],
        sums[2],
        sums[3],
        sums[4],
        sums[5],
        sums[6],
        sums[7],
        sums[8],
        sums[9],
        sums[10],
        sums[11],
        hidden_grads[0],
        hidden_grads[1],
    )


def local(psg, batch, *arrays):
    decoder_in, gain = arrays[0], arrays[5]
    if regular(gain.shape[0], psg, batch, decoder_in.shape[1], decoder_in.shape[2]) and decoder_in.shape[0] == 1:
        return fused(psg, batch, *arrays)
    return general(*arrays)


def solution(mesh):
    line, spread = P("batch", None, None), P("batch", "psg", None)
    flat, rows = P(("psg", "batch")), P(("psg", "batch"), None)
    table, wide, tall = P(None, ("psg", "batch")), P("batch", "psg"), P("psg", "batch")
    return jax.shard_map(
        functools.partial(local, mesh.shape["psg"], mesh.shape["batch"]),
        mesh=mesh,
        in_specs=(line, spread, line, P("batch"), table) + ((flat,) + (rows,) * 4) * 2 + (flat, wide, tall),
        out_specs=(line, line, spread, table) + ((flat,) + (rows,) * 4) * 2 + (flat, wide, tall),
        check_vma=False,
    )
```

```python
import functools
import types

import jax
import jax.numpy as jnp
from jax import lax
from jax.experimental import pallas as pl
from jax.experimental.pallas import tpu as pltpu
from jax.sharding import PartitionSpec as P

SPANS = 4
HEADS = 12
PASS_LEN = 192
EPSILON = 1e-06
MASKED = -1000000000.0
LANES = 128
MIB = 2**20
ENCODED_PARTS = 3
PAIRS = 80
LEAVING = 24

F32 = jnp.float32
BF16 = jnp.bfloat16
ID = pl.DeviceIdType.MESH

CK, CV, CO, CQ, SO, SK, SQ, SV = range(8)
GATHER = ((CK, 2, False), (SK, 3, False), (SO, 1, True), (CQ, 1, True), (CO, 1, True))
REDUCE = ((CO, 1, True), (CQ, 2, True), (SK, 3, True), (CK, 1, False), (CV, 1, False))


def nn(former, latter):
    return jnp.dot(former, latter, preferred_element_type=F32)


def nt(former, latter):
    return lax.dot_general(former, latter, (((1,), (1,)), ((), ())), preferred_element_type=F32)


def rms_factor(values):
    return lax.rsqrt(jnp.mean(values * values, -1, keepdims=True) + EPSILON)


def norm_back(values, factor, scales, grad_out):
    scaled = grad_out * scales
    cubed = factor * factor * factor
    return factor * scaled - values * cubed * jnp.mean(scaled * values, -1, keepdims=True)


def lane_is_low():
    return lax.broadcasted_iota(jnp.int32, (1, LANES), 1) < LANES // 2


def stack_heads(pair):
    low = lane_is_low()
    zero = jnp.zeros_like(pair)
    return jnp.concatenate([jnp.where(low, pair, zero), jnp.where(low, zero, pair)], 0)


def merge_heads(stacked):
    half = stacked.shape[0] // 2
    return jnp.where(lane_is_low(), stacked[:half], stacked[half:])


def stack_stat(stats, pair):
    return jnp.concatenate([stats[:, 2 * pair : 2 * pair + 1], stats[:, 2 * pair + 1 : 2 * pair + 2]], 0)


def spread_stat(stats, pair):
    return jnp.where(
        lane_is_low(), stats[:, 2 * pair : 2 * pair + 1], stats[:, 2 * pair + 1 : 2 * pair + 2]
    )


def column_tiles(width, size=256):
    return [slice(first, min(first + size, width)) for first in range(0, width, size)]


def pair_lanes(pair):
    return slice(pair * LANES, (pair + 1) * LANES)


def self_forward(dec, row, g1, wq, wk, wv, wo, g2, res, n1, q, k, v, probs, mix, after, n2):
    x = dec + row
    res[...] = x
    normed = (x * rms_factor(x) * g1).astype(BF16)
    n1[...] = normed
    q[...] = nn(normed, wq).astype(BF16)
    k[...] = nn(normed, wk).astype(BF16)
    v[...] = nn(normed, wv).astype(BF16)
    tokens, width = x.shape
    scale = (width // HEADS) ** (-0.5)
    rows = lax.broadcasted_iota(jnp.int32, (2 * tokens, tokens), 0) % tokens
    causal = rows >= lax.broadcasted_iota(jnp.int32, (2 * tokens, tokens), 1)
    for pair in range(HEADS // 2):
        cols = pair_lanes(pair)
        scores = jnp.where(causal, nt(stack_heads(q[:, cols]), k[:, cols]) * scale, MASKED)
        expo = jnp.exp(scores - jnp.max(scores, -1, keepdims=True))
        chances = expo * (1.0 / jnp.sum(expo, -1, keepdims=True))
        probs[pair] = chances
        mix[:, cols] = merge_heads(nn(chances.astype(BF16), v[:, cols])).astype(BF16)
    y = x + nn(mix[...], wo)
    after[...] = y
    n2[...] = (y * rms_factor(y) * g2).astype(BF16)


def cross_attend(qc, key, val, probs, stat, part):
    tokens, width = qc.shape
    share = tokens // 4
    scale = (width // HEADS) ** (-0.5)
    lane = lax.broadcasted_iota(jnp.int32, (tokens, LANES), 1)
    tops = jnp.zeros((tokens, LANES), F32)
    sums = jnp.ones((tokens, LANES), F32)
    for pair in range(HEADS // 2):
        cols = pair_lanes(pair)
        scores = nt(stack_heads(qc[:, cols]), key[:, cols]) * scale
        top = jnp.max(scores, -1, keepdims=True)
        expo = jnp.exp(scores - top)
        total = jnp.sum(expo, -1, keepdims=True)
        low = expo.astype(BF16)
        probs[pair] = low
        mixed = merge_heads(nn(low, val[:, cols]) * (1.0 / total)).astype(BF16)
        for p in range(4):
            part[p // 2, p % 2, :, cols] = mixed[p * share : (p + 1) * share]
        for half in range(2):
            rows = slice(half * tokens, (half + 1) * tokens)
            here = lane == 2 * pair + half
            tops = jnp.where(here, top[rows], tops)
            sums = jnp.where(here, total[rows], sums)
    for p in range(4):
        rows = slice(p * share, (p + 1) * share)
        stat[p // 2, p % 2, :, :LANES] = tops[rows]
        stat[p // 2, p % 2, :, LANES:] = sums[rows]


def join_parts(o_a, s_a, o_b, s_b, out, stat):
    top_a, top_b = s_a[:, :LANES], s_b[:, :LANES]
    top = jnp.maximum(top_a, top_b)
    w_a = jnp.exp(top_a - top) * s_a[:, LANES:]
    w_b = jnp.exp(top_b - top) * s_b[:, LANES:]
    total = w_a + w_b
    inverse = 1.0 / total
    w_a, w_b = w_a * inverse, w_b * inverse
    for pair in range(HEADS // 2):
        cols = pair_lanes(pair)
        mixed = spread_stat(w_a, pair) * o_a[:, cols].astype(F32) + spread_stat(w_b, pair) * o_b[:, cols].astype(F32)
        out[:, cols] = mixed.astype(out.dtype)
    stat[:, :LANES] = top
    stat[:, LANES:] = total


def feed_forward(x, top, w_in, w_out):
    pre = nn(x, w_in)
    root = (2.0 / jnp.pi) ** 0.5
    square = pre * pre
    bend = jnp.tanh(root * (pre + 0.044715 * (square * pre)))
    act = (0.5 * pre * (1.0 + bend)).astype(BF16)
    slope = 0.5 * (1.0 + bend) + 0.5 * pre * (1.0 - bend * bend) * (root * (1.0 + 3 * 0.044715 * square))
    dpre = (nn(top, w_out) * slope).astype(BF16)
    return act, dpre


def head_sums(product):
    lane = lax.broadcasted_iota(jnp.int32, (product.shape[0], LANES), 1)
    sums = jnp.zeros(lane.shape, F32)
    low = lane_is_low()
    for pair in range(HEADS // 2):
        here = product[:, pair_lanes(pair)]
        sums = jnp.where(lane == 2 * pair, jnp.sum(jnp.where(low, here, 0.0), -1, keepdims=True), sums)
        sums = jnp.where(lane == 2 * pair + 1, jnp.sum(jnp.where(low, 0.0, here), -1, keepdims=True), sums)
    return sums


def cross_backward(pair, qc, dmixed, key, val, probs, ratio, dots, part):
    tokens, width = qc.shape
    share = tokens // 4
    scale = (width // HEADS) ** (-0.5)
    cols = pair_lanes(pair)
    q2 = stack_heads(qc[:, cols])
    d2 = stack_heads(dmixed[:, cols])
    chances = probs[pair].astype(F32) * stack_stat(ratio, pair)
    dchance = nt(d2, val[:, cols])
    dscore = (chances * (dchance - stack_stat(dots, pair))).astype(BF16)
    dquery = (merge_heads(nn(dscore, key[:, cols])) * scale).astype(BF16)
    for p in range(4):
        part[p // 2, p % 2, :, cols] = dquery[p * share : (p + 1) * share]
    probs[pair, :LANES] = (nn(q2.T, dscore) * scale).astype(BF16)
    probs[pair, LANES:] = nn(d2.T, chances.astype(BF16)).astype(BF16)


def self_backward(dmixed, q, k, v, probs, dq, dk, dv):
    width = q.shape[1]
    scale = (width // HEADS) ** (-0.5)
    for pair in range(HEADS // 2):
        cols = pair_lanes(pair)
        q2 = stack_heads(q[:, cols])
        d2 = stack_heads(dmixed[:, cols])
        chances = probs[pair]
        dchance = nt(d2, v[:, cols])
        dscore = chances * (dchance - jnp.sum(chances * dchance, -1, keepdims=True))
        low = dscore.astype(BF16)
        dq[:, cols] = (merge_heads(nn(low, k[:, cols])) * scale).astype(BF16)
        dk[:, cols] = (nn(low.T, q2) * scale).astype(BF16)
        dv[:, cols] = nn(chances.astype(BF16).T, d2).astype(BF16)


INPUTS = ["tid", "dec", "cot", "enc", "table", "g_one", "g_two", "g_three", "sq", "sk", "sv", "so", "cq", "co", "ck", "cv", "h_in", "h_out"]
OUTPUTS = ["block_out", "grad_dec", "grad_enc", "g_attn", "g_in", "g_out", "g_vec"]


def buffers(psg, batch, tokens, length, width, owned, hidden):
    spans, pairs, share, half = batch // 2, HEADS // 2, tokens // psg, width // 2
    dma = pltpu.SemaphoreType.DMA
    whole = (tokens, width)
    quad = (2, 2, share)
    band = 2 * owned
    runs = len(GATHER)

    def low(*shape):
        return pltpu.VMEM(shape, BF16)

    def full(*shape):
        return pltpu.VMEM(shape, F32)

    out = dict(
        w=low(8, 2, 2 * batch * owned, width),
        f=low(2, width, hidden // 2),
        m_send=low(4, band, half),
        m_recv=low(4, band, half),
        v_buf=full(4, 8, width),
        v_recv=full(3 + spans, 8, width),
        cots=low(2, tokens, width),
        dec_here=low(tokens, width),
        enc_here=low(length, width),
        block_here=low(*quad, width),
        grad_dec_here=full(*whole),
        grad_enc_here=full(length, width),
        g_attn_here=full(8, owned, width),
        g_in_here=full(width // batch, hidden),
        g_out_here=full(width // batch, hidden),
        g_vec_here=full(8, owned),
        load=dma((3,)),
        store=dma((16,)),
        key=low(length, width),
        val=low(length, width),
        c_probs=low(pairs, 2 * tokens, length),
        s_probs=full(pairs, 2 * tokens, tokens),
        res=full(*whole),
        after=full(*whole),
        n1=low(*whole),
        n2=low(*whole),
        q=low(*whole),
        k=low(*whole),
        v=low(*whole),
        mix=low(*whole),
        qc=low(*whole),
        o_part=low(*quad, width),
        o_stat=full(*quad, 2 * LANES),
        o_core=low(2, share, width),
        o_core_stat=full(2, share, 2 * LANES),
        o_to=low(share, width),
        o_to_stat=full(share, 2 * LANES),
        o_mid=full(share, width),
        o_mid_stat=full(share, 2 * LANES),
        o_x=low(share, width),
        o_x_stat=full(share, 2 * LANES),
        mixed_rows=full(share, width),
        stat_rows=full(share, 2 * LANES),
        after_rows=full(share, width),
        n3=low(2, *quad, width),
        mixc=low(*quad, width),
        log_total=full(*quad, LANES),
        dn=low(2, *quad, width),
        dn_core=low(2, 2, share, width),
        dn_to=low(3, share, width),
        dn_got=low(3, share, width),
        hp=low(2, *quad, width),
        hp_core=low(2, 2, share, width),
        hp_to=low(3, share, width),
        hp_got=low(3, share, width),
        grad_rows=full(share, width),
        dcross=low(*quad, width),
        dq_part=low(*quad, width),
        dq_core=low(2, share, width),
        dq_to=low(share, width),
        dq_x=low(share, width),
        dqc=low(*quad, width),
        dself=low(*quad, width),
        dself_rest=low(*quad, width),
        dq=low(*whole),
        dk=low(*whole),
        dv=low(*whole),
        turned=low(4, width, tokens),
        gf=low(2, width, hidden // 2),
        gkv=low(2, 2, 2 * batch * owned, width),
        kv_core=low(2, 2, batch * owned, width),
        kv_to=low(2, batch * owned, width),
        kv_x=low(2, batch * owned, width),
        g=low(8, batch * owned, width),
        gains=full(8, width),
        t_buf=full(4, 8, width),
        t_recv=full(3 + spans, 8, width),
        f_swap=low(2, width // batch, hidden // 2),
        f_swapped=low(2, width // batch, hidden // 2),
        f_came=low(3, 2, width // spans, hidden // 2),
        f_sum=full(2, width // spans, hidden // 2),
        one_send=dma((LEAVING,)),
        one_recv=dma((PAIRS,)),
        a_recv=dma((runs, 2 * batch)),
        a_send=dma((runs, 4)),
        a_core=dma((runs,)),
        w_recv=dma((spans,)),
        w_send=dma((3,)),
        v_sems=dma((2, spans)),
        t_sems=dma((2, spans)),
        f_line=dma((6,)),
    )
    for number, (_, count, y_first) in enumerate(REDUCE):
        rows = -(-count * owned // 16) * 16
        if y_first:
            out[f"r{number}_y"] = low(2, count, band, width)
            out[f"r{number}_one"] = low(count, band, width)
            out[f"r{number}_own"] = full(count * owned, width)
        else:
            out[f"r{number}_one"] = low(2 * band, width)
            out[f"r{number}_two_to"] = low(band, width)
            out[f"r{number}_two"] = low(band, width)
            out[f"r{number}_own"] = full(band, width)
        out[f"r{number}_last_to"] = low(rows, width)
        out[f"r{number}_last"] = low(rows, width)
    return out


def block_kernel(names, psg, batch, *refs):
    r = types.SimpleNamespace(**dict(zip(names, refs, strict=True)))
    index, question = lax.axis_index("psg"), lax.axis_index("batch")
    far, near = question // 2, question % 2
    side, core = index // 2, index % 2
    x_peer = ((1 - side) * 2 + core, question)
    c_peer = (side * 2 + 1 - core, question)
    y_peer = (index, far * 2 + 1 - near)
    d_peer = ((1 - side) * 2 + core, far * 2 + 1 - near)
    places = [far, far + 1 - 2 * (far % 2), lax.rem(far + 2, SPANS), SPANS - 1 - far]
    column = [(index, z * 2 + near) for z in places[1:]]
    one_peer, two_peer = column[0], column[1]
    tokens, width = r.dec_here.shape
    owned = r.sq.shape[0]
    band, quarter, half = 2 * owned, batch * owned, width // 2
    share = tokens // psg
    fan = width // batch
    shards = (r.ck, r.cv, r.co, r.cq, r.so, r.sk, r.sq, r.sv)
    pairs = HEADS // 2

    def aligned(value, to):
        return value if isinstance(value, int) else pl.multiple_of(value, to)

    def span(start, size, to):
        return pl.ds(aligned(start, to), size)

    def lanes(h):
        return span(h * half, half, LANES)

    sent = []

    def go(copy):
        copy.start()
        sent.append(copy)

    def remote(src, dst, send, recv, device):
        return pltpu.make_async_remote_copy(
            src_ref=src, dst_ref=dst, send_sem=send, recv_sem=recv, device_id=device, device_id_type=ID
        )

    numbers = iter(range(PAIRS))
    leaving = []

    def pair(src, dst, device):
        number = next(numbers)
        if number >= LEAVING:
            leaving[number - LEAVING].wait_send()
        copy = remote(src, dst, r.one_send.at[number % LEAVING], r.one_recv.at[number], device)
        copy.start()
        leaving.append(copy)
        return copy

    loads = [
        pltpu.make_async_copy(r.cot, r.cots.at[near], r.load.at[0]),
        pltpu.make_async_copy(r.dec, r.dec_here, r.load.at[1]),
        pltpu.make_async_copy(r.enc, r.enc_here, r.load.at[2]),
    ]
    for copy in loads:
        copy.start()
    stores = []

    def store(src, dst):
        copy = pltpu.make_async_copy(src, dst, r.store.at[len(stores)])
        copy.start()
        stores.append(copy)

    barrier = pltpu.get_barrier_semaphore()
    greeted = column + [y_peer, x_peer, c_peer, d_peer]
    for other in greeted:
        pl.semaphore_signal(barrier, inc=1, device_id=other, device_id_type=ID)
    pl.semaphore_wait(barrier, len(greeted))

    def pack(number):
        first, second = shards[2 * number], shards[2 * number + 1]
        both = jnp.concatenate([first[:, lanes(1 - near)].astype(F32), second[:, lanes(1 - near)].astype(F32)], 0)
        r.m_send[number] = both.astype(BF16)

    def exchange(first, count):
        for number in range(first, first + count):
            pack(number)
        return pair(r.m_send.at[first : first + count], r.m_recv.at[first : first + count], y_peer)

    row = core * quarter + far * band

    def join(number):
        other = r.m_recv[number].astype(F32)
        for part in range(2):
            mine = shards[2 * number + part][:, lanes(near)].astype(F32)
            theirs = other[part * owned : (part + 1) * owned]
            block = jnp.where(near == 0, jnp.concatenate([mine, theirs], 0), jnp.concatenate([theirs, mine], 0))
            r.w[2 * number + part, side, span(row, band, 16), lanes(near)] = block.astype(BF16)

    def unit(run, x, c, z, h):
        first, count, joined = GATHER[run]
        rows = span(c * quarter + z * band, band, 16)
        return r.w.at[first : first + count, slice(None) if joined else x, rows, lanes(h)]

    def landing(run, x, c, z, h):
        return r.a_recv.at[run, (0 if GATHER[run][2] else x) * batch + z * 2 + h]

    def hand(run, x, c, z, h, kind, device, recv=None):
        spot = unit(run, x, c, z, h)
        remote(spot, spot, r.a_send.at[run, kind], landing(run, x, c, z, h) if recv is None else recv, device).start()

    def landed(run, x, c, z, h):
        spot = unit(run, x, c, z, h)
        remote(spot, spot, r.a_send.at[run, 0], landing(run, x, c, z, h), c_peer).wait_recv()

    held = []

    def wide(run, z, h, hold=False):
        to_x = functools.partial(hand, run, side, core, z, h, 2, x_peer)
        if hold:
            held.append(to_x)
        elif not GATHER[run][2]:
            to_x()
        hand(run, side, core, z, h, 3, c_peer, r.a_core.at[run])

    def offer(run):
        hand(run, side, core, far, near, 0, two_peer)
        hand(run, side, core, far, near, 0, one_peer)
        hand(run, side, core, far, near, 1, y_peer)
        wide(run, far, near)

    def from_y(run, step, hold=False):
        landed(run, side, core, places[step], 1 - near)
        wide(run, places[step], 1 - near, hold)

    def from_line(run, step, hold=False):
        z = places[step]
        landed(run, side, core, z, near)
        if step == 2:
            hand(run, side, core, z, near, 0, one_peer)
        hand(run, side, core, z, near, 1, y_peer)
        wide(run, z, near, hold)

    def from_x(run, step):
        z = places[step]
        for h in (near, 1 - near):
            landed(run, 1 - side, core, z, h)
            hand(run, 1 - side, core, z, h, 3, c_peer, r.a_core.at[run])

    def sent_of(run):
        first, count, joined = GATHER[run]
        lower = r.w.at[first : first + count, slice(None) if joined else 0]
        quarters = (slice(None),) * (2 if joined else 1)
        sizes = [
            lower.at[(*quarters, pl.ds(0, 3 * band), pl.ds(0, half))],
            lower.at[(*quarters, pl.ds(0, quarter), pl.ds(0, half))],
            None if joined else lower.at[(*quarters, pl.ds(0, quarter), slice(None))],
            r.w.at[first : first + count, :, pl.ds(0, quarter), :],
        ]
        for kind, size in enumerate(sizes):
            if size is not None:
                remote(size, size, r.a_send.at[run, kind], r.a_core.at[run], c_peer).wait_send()

    def complete(run):
        first, count, _ = GATHER[run]
        all_of = r.w.at[first : first + count, :, span((1 - core) * quarter, quarter, 16), :]
        remote(all_of, all_of, r.a_send.at[run, 0], r.a_core.at[run], c_peer).wait_recv()

    def matrix(number):
        return r.w[number].reshape(width, width)

    m_kv = exchange(0, 1)
    m_self = exchange(2, 2)
    m_tail = exchange(1, 1)

    def ladder(buf, recv, sems):
        def first():
            return pair(buf.at[0], recv.at[0], c_peer)

        def second(copy):
            copy.wait_recv()
            buf[1] = (buf[0].astype(F32) + recv[0].astype(F32)).astype(buf.dtype)
            return pair(buf.at[1], recv.at[1], x_peer)

        def third(copy):
            copy.wait_recv()
            buf[2] = (buf[1].astype(F32) + recv[1].astype(F32)).astype(buf.dtype)
            return pair(buf.at[2], recv.at[2], y_peer)

        def fourth(copy):
            copy.wait_recv()
            buf[3] = (buf[2].astype(F32) + recv[2].astype(F32)).astype(buf.dtype)
            for z in places[1:]:
                go(remote(buf.at[3], recv.at[3 + far], sems.at[0, z], sems.at[1, far], (index, z * 2 + near)))

        def last():
            total = buf[3].astype(F32)
            for z in places[1:]:
                remote(buf.at[3], recv.at[3 + z], sems.at[0, z], sems.at[1, z], c_peer).wait_recv()
                total = total + recv[3 + z].astype(F32)
            return total

        return first, second, third, fourth, last

    device = index * batch + question
    place = jnp.where(
        lax.broadcasted_iota(jnp.int32, (owned, width), 1)
        == lax.broadcasted_iota(jnp.int32, (owned, width), 0) + device * owned,
        1.0,
        0.0,
    ).astype(BF16)
    r.v_buf[0, 0:3] = nn(r.table[...], place)
    for number, gain in enumerate((r.g_one, r.g_two, r.g_three)):
        r.v_buf[0, 3 + number : 4 + number] = nn(gain[...], place)
    r.v_buf[0, 6:8] = jnp.zeros((2, width), F32)
    v_first, v_second, v_third, v_fourth, v_last = ladder(r.v_buf, r.v_recv, r.v_sems)
    v_copy = v_first()

    m_kv.wait_recv()
    join(0)
    offer(0)
    m_self.wait_recv()
    join(2)
    join(3)
    offer(1)
    m_tail.wait_recv()
    join(1)
    own_tail = r.w.at[CO : CO + 3, side, span(row, band, 16), lanes(near)]
    x_tail = pair(own_tail, own_tail, x_peer)
    v_copy = v_second(v_copy)

    cut = r.f.shape[2]
    other_cols = span((1 - near) * cut, cut, LANES)
    own_cols = span(near * cut, cut, LANES)
    own_fan = span(question * fan, fan, 16)
    r.f[0, own_fan] = r.h_in[:, own_cols]
    r.f[1, own_fan] = r.h_out[:, own_cols]

    def f_unit(z):
        return r.f.at[:, span(z * 2 * fan, 2 * fan, 16), :]

    def f_hand(z, sem, device):
        go(remote(f_unit(z), f_unit(z), sem, r.w_recv.at[z], device))

    def f_landed(step):
        z = places[step]
        remote(f_unit(z), f_unit(z), r.w_send.at[0], r.w_recv.at[z], c_peer).wait_recv()
        if step == 2:
            f_hand(z, r.w_send.at[2], one_peer)

    def near_units(run, hold=False):
        from_y(run, 0, hold)
        from_line(run, 2, hold)
        from_line(run, 1, hold)

    def far_units(run):
        from_line(run, 3)
        from_y(run, 1)
        from_y(run, 2)

    near_units(0)
    far_units(0)
    near_units(1, True)
    x_tail.wait_recv()
    offer(2)
    from_y(0, 3)
    for to_x in held:
        to_x()
    far_units(1)
    near_units(2)
    offer(3)
    v_copy = v_third(v_copy)
    for step in range(3):
        from_x(0, step)
    from_y(1, 3)
    h_copies = [
        pair(r.h_in.at[:, other_cols], r.f.at[0, own_fan], y_peer),
        pair(r.h_out.at[:, other_cols], r.f.at[1, own_fan], y_peer),
    ]
    far_units(2)
    from_x(1, 0)
    offer(4)
    from_x(0, 3)
    near_units(3)
    complete(0)
    loads[2].wait()
    for cols in column_tiles(width):
        r.key[:, cols] = nn(r.enc_here[...], r.w[CK, :, :, cols].reshape(width, -1)).astype(BF16)
        r.val[:, cols] = nn(r.enc_here[...], r.w[CV, :, :, cols].reshape(width, -1)).astype(BF16)
    v_fourth(v_copy)
    from_y(2, 3)
    far_units(3)
    from_x(1, 1)
    from_x(1, 2)
    near_units(4)
    from_y(3, 3)
    from_x(1, 3)
    for copy in h_copies:
        copy.wait_recv()
    f_hand(far, r.w_send.at[0], two_peer)
    f_hand(far, r.w_send.at[1], one_peer)
    loads[0].wait()
    loads[1].wait()
    complete(1)
    complete(2)
    vectors = v_last()

    gains = [vectors[3 + i : 4 + i] for i in range(3)]
    chosen = r.tid[0]
    row_embed = functools.reduce(
        jnp.add, [vectors[i : i + 1] * jnp.where(chosen == i, 1.0, 0.0).astype(F32) for i in range(3)]
    )
    r.gains[0:3] = vectors[3:6]
    self_forward(
        r.dec_here[...].astype(F32), row_embed, gains[0], matrix(SQ), matrix(SK), matrix(SV), matrix(SO), gains[1],
        r.res, r.n1, r.q, r.k, r.v, r.s_probs, r.mix, r.after, r.n2,
    )
    far_units(4)
    cot_copy = pair(r.cots.at[near], r.cots.at[near], y_peer)
    complete(3)
    r.qc[...] = nn(r.n2[...], matrix(CQ)).astype(BF16)

    cross_attend(r.qc, r.key, r.val, r.c_probs, r.o_stat, r.o_part)
    first = [pair(r.o_part.at[:, 1 - core], r.o_core, c_peer), pair(r.o_stat.at[:, 1 - core], r.o_core_stat, c_peer)]
    from_y(4, 3)
    for copy in first:
        copy.wait_recv()
    join_parts(
        r.o_part[1 - side, core], r.o_stat[1 - side, core], r.o_core[1 - side], r.o_core_stat[1 - side],
        r.o_to, r.o_to_stat,
    )
    second = [pair(r.o_to, r.o_x, x_peer), pair(r.o_to_stat, r.o_x_stat, x_peer)]
    join_parts(
        r.o_part[side, core], r.o_stat[side, core], r.o_core[side], r.o_core_stat[side], r.o_mid, r.o_mid_stat
    )
    f_landed(2)
    f_landed(1)
    complete(4)
    for copy in second:
        copy.wait_recv()
    join_parts(r.o_mid[...], r.o_mid_stat[...], r.o_x[...], r.o_x_stat[...], r.mixed_rows, r.stat_rows)
    my_rows = span(index * share, share, 16)
    r.log_total[side, core] = r.stat_rows[:, :LANES] + jnp.log(r.stat_rows[:, LANES:])
    mixed_low = r.mixed_rows[...].astype(BF16)
    r.mixc[side, core] = mixed_low
    y = r.after[my_rows, :] + nn(mixed_low, matrix(CO))
    r.after_rows[...] = y
    r.n3[near, side, core] = (y * rms_factor(y) * r.gains[2:3]).astype(BF16)

    def block8(h, x, c):
        return r.n3.at[h, x, c]

    def spread4(buf):
        spot = buf.at[side, core]
        over_x, over_c = pair(spot, spot, x_peer), pair(spot, spot, c_peer)

        def then():
            over_x.wait_recv()
            onward = buf.at[1 - side, core]
            last = pair(onward, onward, c_peer)

            def end():
                over_c.wait_recv()
                last.wait_recv()

            return end

        return then

    mine = block8(near, side, core)
    to_y, to_x, to_d, to_c = [pair(mine, mine, peer) for peer in (y_peer, x_peer, d_peer, c_peer)]
    onward = [to_c]
    for copy, h, x in ((to_y, 1 - near, side), (to_x, near, 1 - side), (to_d, 1 - near, 1 - side)):
        copy.wait_recv()
        onward.append(pair(block8(h, x, core), block8(h, x, core), c_peer))
    f_landed(3)
    cot_copy.wait_recv()
    for copy in onward:
        copy.wait_recv()

    log_then = spread4(r.log_total)
    mixc_then = spread4(r.mixc)
    x = r.n3[...].reshape(2 * tokens, width)
    top = r.cots[...].reshape(2 * tokens, width)
    act, dpre = feed_forward(x, top, r.f[0], r.f[1])
    r.dn[...] = nt(dpre, r.f[0]).astype(BF16).reshape(r.dn.shape)

    def shrink8(part, got_c, to, got):
        over_c = pair(part.at[:, :, 1 - core], got_c, c_peer)

        def second():
            over_c.wait_recv()

            def total(h, x):
                return part[h, x, core].astype(F32) + got_c[h, x].astype(F32)

            copies = []
            for slot, (h, x, peer) in enumerate(
                ((1 - near, 1 - side, d_peer), (near, 1 - side, x_peer), (1 - near, side, y_peer))
            ):
                to[slot] = total(h, x).astype(BF16)
                copies.append(pair(to.at[slot], got.at[slot], peer))

            def last():
                out = total(near, side)
                for slot, copy in enumerate(copies):
                    copy.wait_recv()
                    out = out + got[slot].astype(F32)
                return out

            return last

        return second

    dn_second = shrink8(r.dn, r.dn_core, r.dn_to, r.dn_got)
    r.hp[...] = nt(act, r.f[1]).astype(BF16).reshape(r.hp.shape)
    dn_last = dn_second()
    hp_second = shrink8(r.hp, r.hp_core, r.hp_to, r.hp_got)
    r.gf[0] = nn(x.T, dpre).astype(BF16)
    r.gf[1] = nn(top.T, act).astype(BF16)

    def line_kit(came, src, sems):
        def over_pair(step):
            slot = step // 2
            return remote(src(places[step]), came.at[slot], sems.at[slot], sems.at[3 + slot], one_peer)

        def over_pairs():
            return remote(src(places[2]), came.at[2], sems.at[2], sems.at[5], two_peer)

        def first():
            go(over_pair(3))
            go(over_pair(1))

        def second(value):
            over_pair(3).wait_recv()
            src(places[2])[...] = (value + came[1].astype(F32)).astype(BF16)
            go(over_pairs())

        def total(value, out):
            over_pair(1).wait_recv()
            both = value + came[0].astype(F32)
            over_pairs().wait_recv()
            out[...] = both + came[2].astype(F32)

        return first, second, total

    def f_piece(z):
        return r.gf.at[:, span(z * 2 * fan, 2 * fan, 16), :]

    f_first, f_second, f_total = line_kit(r.f_came, f_piece, r.f_line)
    f_first()
    log_end = log_then()
    mixc_end = mixc_then()

    upstream = dn_last()
    y = r.after_rows[...]
    factor = rms_factor(y)
    scales = r.gains[2:3]
    gain_three = jnp.sum(upstream * y * factor, 0, keepdims=True)
    grad = r.cots[near, my_rows, :].astype(F32) + norm_back(y, factor, scales, upstream)
    r.grad_rows[...] = grad
    low = grad.astype(BF16)
    r.dcross[side, core] = low
    dcross_then = spread4(r.dcross)
    log_end()
    mixc_end()
    dcross_end = dcross_then()
    dcross_end()
    hp_last = hp_second()

    def rows_of(ref):
        return ref[...].reshape(tokens, ref.shape[-1])

    parity, high = far % 2, far // 2

    def ordered(value, y_first):
        blocks = [(z, h) for z in range(SPANS) for h in range(2)]
        if y_first:
            blocks.sort(key=lambda block: (block[1], block[0] % 2, block[0] // 2))
        else:
            blocks.sort(key=lambda block: (block[0] % 2, block[0] // 2, block[1]))
        parts = [value[(z * 2 + h) * owned : (z * 2 + h + 1) * owned] for z, h in blocks]
        return jnp.concatenate(parts, 0).astype(BF16)

    def last_step(number, mine, theirs, peer):
        first, count, _ = REDUCE[number]
        to, got = getattr(r, f"r{number}_last_to"), getattr(r, f"r{number}_last")
        if to.shape[0] > theirs.shape[0]:
            theirs = jnp.concatenate([theirs, jnp.zeros((to.shape[0] - theirs.shape[0], width), F32)], 0)
        to[...] = theirs.astype(BF16)
        copy = pair(to, got, peer)
        r.g_attn_here[first : first + count] = mine.reshape(count, owned, width)

        def end():
            copy.wait_recv()
            more = got[...].astype(F32)[: count * owned]
            r.g_attn_here[first : first + count] = r.g_attn_here[first : first + count] + more.reshape(count, owned, width)
            store(r.g_attn_here.at[first : first + count], r.g_attn.at[first : first + count])

        return end

    def line_first(number):
        m = REDUCE[number][0]
        one, two_to, two, own = [getattr(r, f"r{number}_{name}") for name in ("one", "two_to", "two", "own")]
        copies = []

        def forward():
            copies.append(pair(r.g.at[m, span((1 - parity) * 2 * band, 2 * band, 16), :], one, one_peer))

        def again():
            copies[0].wait_recv()
            total = r.g[m, span(parity * 2 * band, 2 * band, 16), :].astype(F32) + one[...].astype(F32)
            upper, lower = total[:band], total[band:]
            two_to[...] = jnp.where(high == 0, lower, upper).astype(BF16)
            copies.append(pair(two_to, two, two_peer))
            own[...] = jnp.where(high == 0, upper, lower)

        def finish():
            copies[1].wait_recv()
            total = own[...] + two[...].astype(F32)
            upper, lower = total[:owned], total[owned:]
            return last_step(
                number, jnp.where(near == 0, upper, lower), jnp.where(near == 0, lower, upper), y_peer
            )

        return forward, again, finish

    def y_first(number):
        first, count, _ = REDUCE[number]
        got_y, one = getattr(r, f"r{number}_y"), getattr(r, f"r{number}_one")
        copies = {}

        def piece(h, p):
            return r.g.at[first : first + count, span(h * 2 * band + p * band, band, 16), :]

        def begin(mine):
            p = parity if mine else 1 - parity
            copies[mine] = pair(piece(1 - near, p), got_y.at[1 if mine else 0], y_peer)

        def value(mine):
            copies[mine].wait_recv()
            return piece(near, parity if mine else 1 - parity)[...].astype(F32) + got_y[1 if mine else 0].astype(F32)

        def forward():
            got_y[0] = value(False).astype(BF16)
            copies["one"] = pair(got_y.at[0], one, one_peer)

        def again():
            total = value(True)
            copies["one"].wait_recv()
            total = total + one[...].astype(F32)
            upper = total[:, :owned].reshape(count * owned, width)
            lower = total[:, owned:].reshape(count * owned, width)
            return last_step(
                number, jnp.where(high == 0, upper, lower), jnp.where(high == 0, lower, upper), two_peer
            )

        return begin, forward, again

    own_rows = span(index * quarter, quarter, 16)

    def turn(slot, value):
        r.turned[slot] = value.T
        return r.turned[slot, own_rows, :]

    co_begin, co_forward, co_again = y_first(0)
    so_begin, so_forward, so_again = y_first(1)
    late_begin, late_forward, late_again = y_first(2)
    k_forward, k_again, k_finish = line_first(3)
    v_forward, v_again, v_finish = line_first(4)

    ratio = jnp.exp(rows_of(r.o_stat)[:, :LANES] - rows_of(r.log_total))
    dmixed = nt(rows_of(r.dcross), matrix(CO)).astype(BF16)
    dots = head_sums(dmixed.astype(F32) * rows_of(r.mixc).astype(F32))
    for number in range(pairs):
        cross_backward(
            number, r.qc, dmixed, r.key, r.val, r.c_probs, ratio, dots, r.dq_part
        )
    q_first = pair(r.dq_part.at[:, 1 - core], r.dq_core, c_peer)
    r.g[CO] = ordered(nn(turn(0, rows_of(r.mixc)), rows_of(r.dcross)), True)
    co_begin(False)
    co_begin(True)
    r.key[...] = r.c_probs[:, :LANES].reshape(width, -1).T
    q_first.wait_recv()
    r.dq_to[...] = (r.dq_part[1 - side, core].astype(F32) + r.dq_core[1 - side].astype(F32)).astype(BF16)
    q_second = pair(r.dq_to, r.dq_x, x_peer)
    r.c_probs[:, :LANES] = r.enc_here[...].T.reshape(pairs, LANES, -1)
    kv_other, kv_own = span((1 - core) * quarter, quarter, 16), span(core * quarter, quarter, 16)

    def kv_first(part, ref):
        for cols in column_tiles(width):
            product = nn(r.c_probs[:, :LANES].reshape(width, -1), ref[:, cols])
            r.gkv[part, :, :, cols] = product.astype(BF16).reshape(2, 2 * quarter, -1)
        return pair(r.gkv.at[part, :, kv_other, :], r.kv_core.at[part], c_peer)

    def kv_second(part, copy):
        copy.wait_recv()
        total = r.gkv[part, 1 - side, kv_own, :].astype(F32) + r.kv_core[part, 1 - side].astype(F32)
        r.kv_to[part] = total.astype(BF16)
        return pair(r.kv_to.at[part], r.kv_x.at[part], x_peer)

    def kv_third(part, copy):
        copy.wait_recv()
        total = r.gkv[part, side, kv_own, :].astype(F32) + r.kv_core[part, side].astype(F32)
        r.g[CK + part] = ordered(total + r.kv_x[part].astype(F32), False)

    f_second(f_piece(places[2])[...].astype(F32))
    k_copy = kv_first(0, r.key)
    q_second.wait_recv()
    dq_rows = (
        r.dq_part[side, core].astype(F32) + r.dq_core[side].astype(F32) + r.dq_x[...].astype(F32)
    ).astype(BF16)
    r.dqc[side, core] = dq_rows
    upstream = nt(dq_rows, matrix(CQ))
    y = r.after[my_rows, :]
    factor = rms_factor(y)
    gain_two = jnp.sum(upstream * y * factor, 0, keepdims=True)
    grad = r.grad_rows[...] + norm_back(y, factor, r.gains[1:2], upstream)
    low = grad.astype(BF16)
    r.dself[side, core] = low
    dself_then = spread4(r.dself)
    r.dself_rest[side, core] = (grad - low.astype(F32)).astype(BF16)
    dqc_then = spread4(r.dqc)
    r.val[...] = r.c_probs[:, LANES:].reshape(width, -1).T
    dself_end = dself_then()
    co_forward()
    k_copy = kv_second(0, k_copy)
    v_copy = kv_first(1, r.val)
    dself_end()
    dqc_end = dqc_then()

    dself = rows_of(r.dself)
    r.g[SO] = ordered(nn(turn(1, r.mix[...]), dself), True)
    dmixed = nt(dself, matrix(SO)).astype(BF16)
    dqc_end()
    r.g[CQ] = ordered(nn(turn(2, r.n2[...]), rows_of(r.dqc)), True)
    so_begin(False)
    v_copy = kv_second(1, v_copy)
    rest_then = spread4(r.dself_rest)
    co_end = co_again()
    self_backward(dmixed, r.q, r.k, r.v, r.s_probs, r.dq, r.dk, r.dv)
    kv_third(0, k_copy)
    k_forward()
    normed = turn(3, r.n1[...])
    for number, ref in ((SQ, r.dq), (SK, r.dk), (SV, r.dv)):
        r.g[number] = ordered(nn(normed, ref[...]), True)
    late_begin(False)
    so_begin(True)
    so_forward()
    late_begin(True)

    f_total(f_piece(far)[...].astype(F32), r.f_sum)
    both = r.f_sum[...]
    upper, lower = both[:, :fan], both[:, fan:]
    r.f_swap[...] = jnp.where(near == 0, lower, upper).astype(BF16)
    f_copy = pair(r.f_swap, r.f_swapped, y_peer)
    kept = jnp.where(near == 0, upper, lower)
    r.g_in_here[:, own_cols] = kept[0]
    r.g_out_here[:, own_cols] = kept[1]

    upstream = nt(r.dq[...], matrix(SQ)) + nt(r.dk[...], matrix(SK)) + nt(r.dv[...], matrix(SV))
    kv_third(1, v_copy)
    k_again()
    v_forward()
    late_forward()
    rest_then()()
    x = r.res[...]
    factor = rms_factor(x)
    grad = dself.astype(F32) + rows_of(r.dself_rest).astype(F32) + norm_back(x, factor, r.gains[0:1], upstream)
    r.grad_dec_here[...] = grad
    store(r.grad_dec_here, r.grad_dec)
    mine = lax.broadcasted_iota(jnp.int32, (tokens, 1), 0) // share == index
    task = jnp.sum(jnp.where(mine, grad, 0.0), 0, keepdims=True)
    r.t_buf[0, 0:3] = jnp.concatenate([task * jnp.where(chosen == i, 1.0, 0.0).astype(F32) for i in range(3)], 0)
    r.t_buf[0, 3:4] = jnp.sum(jnp.where(mine, upstream * x * factor, 0.0), 0, keepdims=True)
    r.t_buf[0, 4:5] = gain_two
    r.t_buf[0, 5:6] = gain_three
    r.t_buf[0, 6:8] = jnp.zeros((2, width), F32)
    t_first, t_second, t_third, t_fourth, t_last = ladder(r.t_buf, r.t_recv, r.t_sems)
    t_copy = t_first()
    so_end = so_again()
    hidden = hp_last()
    r.block_here[side, core] = (r.after_rows[...] + hidden).astype(BF16)
    out_then = spread4(r.block_here)
    t_copy = t_second(t_copy)
    def encoded_columns(cols):
        r.grad_enc_here[:, cols] = nt(r.key[...], matrix(CK)[cols]) + nt(r.val[...], matrix(CV)[cols])

    tiles = column_tiles(width)
    encoded_columns(tiles[0])
    t_copy = t_third(t_copy)
    out_end = out_then()
    v_again()
    k_end = k_finish()
    t_fourth(t_copy)
    for cols in tiles[1:-1]:
        encoded_columns(cols)
    late_end = late_again()
    v_end = v_finish()
    encoded_columns(tiles[-1])
    store(r.grad_enc_here, r.grad_enc)
    co_end()
    so_end()
    out_end()
    for p in range(psg):
        store(r.block_here.at[p // 2, p % 2], r.block_out.at[p])
    f_copy.wait_recv()
    r.g_in_here[:, other_cols] = r.f_swapped[0].astype(F32)
    r.g_out_here[:, other_cols] = r.f_swapped[1].astype(F32)
    store(r.g_in_here, r.g_in)
    store(r.g_out_here, r.g_out)
    r.g_vec_here[...] = lax.dot_general(
        t_last(), place.astype(F32), (((1,), (1,)), ((), ())), precision=lax.Precision.HIGHEST
    )
    store(r.g_vec_here, r.g_vec)
    k_end()
    v_end()
    late_end()
    for copy in stores:
        copy.wait()
    for run in range(len(GATHER)):
        sent_of(run)
    for copy in sent + leaving[-LEAVING:]:
        copy.wait_send()


def settle_kernel(block_out, grad_dec, grad_enc, g_attn, g_in, g_out, g_vec, *rest):
    outs, vectors, here, sems = rest[:13], rest[13:17], rest[17:23], rest[23]
    rows = grad_enc.shape[0] // ENCODED_PARTS
    parts = [pl.ds(number * rows, rows) for number in range(ENCODED_PARTS)]
    moves = [(grad_enc.at[part], here[0].at[part], [outs[2].at[part]]) for part in parts]
    moves += [
        (block_out, here[1], [outs[0]]),
        (grad_dec, here[2], [outs[1]]),
        (g_in, here[4], [outs[11]]),
        (g_out, here[5], [outs[12]]),
        (g_attn, here[3], outs[3:11]),
    ]
    arrivals = [
        pltpu.make_async_copy(source, spot, sems.at[0, number]) for number, (source, spot, _) in enumerate(moves)
    ]
    for copy in arrivals:
        copy.start()
    first = 0
    for out in vectors:
        out[...] = g_vec[first : first + out.shape[0]]
        first += out.shape[0]
    departures = []
    for copy, (_, spot, places) in zip(arrivals, moves, strict=True):
        copy.wait()
        for number, out in enumerate(places):
            source = spot if len(places) == 1 else spot.at[number]
            departures.append(pltpu.make_async_copy(source, out, sems.at[1, len(departures)]))
            departures[-1].start()
    for copy in departures:
        copy.wait()


def regular(owned, psg, batch, tokens, width):
    return psg == 4 and batch == 2 * SPANS and owned % 8 == 0 and tokens % 128 == 0 and (width // 2) % LANES == 0


def fused(psg, batch, decoder_in, encoded, cotangent, task_ids, task_embed, gain_self, self_query, self_key, self_value,
          self_output, gain_cross, cross_query, cross_key, cross_value, cross_output, gain_hidden, hidden_in, hidden_out):
    _, tokens, width = decoder_in.shape
    length = encoded.shape[1]
    groups, owned = task_embed.shape
    hidden = hidden_in.shape[1]
    scratch = buffers(psg, batch, tokens, length, width, owned, hidden)
    names = INPUTS + OUTPUTS + list(scratch)
    vmem = pl.BlockSpec(memory_space=pltpu.VMEM)
    hbm = pl.BlockSpec(memory_space=pl.ANY)
    block_out, grad_decoder, grad_encoded, g_attn, g_in, g_out, g_vec = pl.pallas_call(
        functools.partial(block_kernel, names, psg, batch),
        out_shape=(
            jax.ShapeDtypeStruct((psg,) + (tokens // psg, width), BF16),
            jax.ShapeDtypeStruct((tokens, width), F32),
            jax.ShapeDtypeStruct((length, width), F32),
            jax.ShapeDtypeStruct((8, owned, width), F32),
            jax.ShapeDtypeStruct((width // batch, hidden), F32),
            jax.ShapeDtypeStruct((width // batch, hidden), F32),
            jax.ShapeDtypeStruct((8, owned), F32),
        ),
        in_specs=[pl.BlockSpec(memory_space=pltpu.SMEM)] + [hbm] * 3 + [vmem] * (len(INPUTS) - 4),
        out_specs=[hbm] * len(OUTPUTS),
        scratch_shapes=list(scratch.values()),
        compiler_params=pltpu.CompilerParams(collective_id=0, has_side_effects=True, vmem_limit_bytes=56 * MIB),
        name="decoder_block",
    )(task_ids, decoder_in[0], cotangent[0], encoded[0], task_embed, gain_self[None],
      gain_cross[None], gain_hidden[None], self_query, self_key, self_value, self_output,
      cross_query, cross_output, cross_key, cross_value, hidden_in, hidden_out.T)
    shapes = [(tokens, width), (tokens, width), (length, width)] + [(owned, width)] * 8 + [(width // batch, hidden)] * 2
    small = [(groups, owned)] + [(1, owned)] * 3
    outs = pl.pallas_call(
        settle_kernel,
        out_shape=tuple(
            jax.ShapeDtypeStruct(shape, F32 if number else BF16) for number, shape in enumerate(shapes + small)
        ),
        in_specs=[hbm] * 6 + [vmem],
        out_specs=[hbm] * len(shapes) + [vmem] * len(small),
        scratch_shapes=[
            pltpu.VMEM((length, width), F32),
            pltpu.VMEM((tokens, width), BF16),
            pltpu.VMEM((tokens, width), F32),
            pltpu.VMEM((8, owned, width), F32),
            pltpu.VMEM((width // batch, hidden), F32),
            pltpu.VMEM((width // batch, hidden), F32),
            pltpu.SemaphoreType.DMA((2, len(shapes) + ENCODED_PARTS)),
        ],
        compiler_params=pltpu.CompilerParams(vmem_limit_bytes=60 * MIB),
        name="settle",
    )(block_out.reshape(tokens, width), grad_decoder, grad_encoded, g_attn, g_in, g_out, g_vec)
    block_out, grad_decoder, grad_encoded = outs[:3]
    g_attn, (g_in, g_out) = outs[3:11], outs[11:13]
    table, gain_one, gain_two, gain_three = outs[13:]
    return (
        block_out[None],
        grad_decoder[None],
        grad_encoded[None],
        table,
        gain_one[0],
        g_attn[SQ],
        g_attn[SK],
        g_attn[SV],
        g_attn[SO],
        gain_two[0],
        g_attn[CQ],
        g_attn[CK],
        g_attn[CV],
        g_attn[CO],
        gain_three[0],
        g_in,
        g_out.T,
    )


def rms_norm(values, scales):
    factor = lax.rsqrt(jnp.mean(values * values, -1, keepdims=True) + EPSILON)
    return (values * factor * scales, factor)


def rms_back(values, factor, scales, grad_out):
    scaled = grad_out * scales
    cubed = factor * factor * factor
    lower = factor * scaled - values * cubed * jnp.mean(scaled * values, -1, keepdims=True)
    return (lower, grad_out * values * factor)


def gelu_tanh(values):
    return jax.nn.gelu(values, approximate=True)


def matmul(former, latter):
    return jnp.dot(former, latter, preferred_element_type=jnp.float32)


def inner_rows(former, latter):
    return lax.dot_general(
        former, latter, (((0,), (0,)), ((), ())), preferred_element_type=jnp.float32
    )


def outer_cols(former, latter):
    return lax.dot_general(
        former, latter, (((1,), (1,)), ((), ())), preferred_element_type=jnp.float32
    )


def split_heads(values, questions):
    return values.reshape(questions, values.shape[0] // questions, HEADS, values.shape[1] // HEADS)


def key_blocks(values):
    questions, length, width = values.shape
    shaped = values.reshape(questions, length // PASS_LEN, PASS_LEN, HEADS, width // HEADS)
    return jnp.moveaxis(shaped, 1, 0)


def block_scores(queries, key_block):
    scale = queries.shape[-1] ** (-0.5)
    return (
        jnp.einsum("bqhe,bkhe->bhqk", queries, key_block, preferred_element_type=jnp.float32)
        * scale
    )


def score_stats(queries, keys):
    questions, tokens, heads, width = queries.shape
    initial = (
        jnp.full((questions, heads, tokens), -1e30, jnp.float32),
        jnp.zeros((questions, heads, tokens), jnp.float32),
    )

    def score_advance(running, key_block):
        scores = block_scores(queries, key_block)
        highest = jnp.maximum(running[0], jnp.max(scores, -1))
        totals = running[1] * jnp.exp(running[0] - highest) + jnp.sum(
            jnp.exp(scores - highest[..., None]), -1
        )
        return ((highest, totals), None)

    return lax.scan(score_advance, initial, key_blocks(keys))[0]


def weighted_values(queries, keys, values, log_total):

    def weighted_advance(running, blocks):
        chances = jnp.exp(block_scores(queries, blocks[0]) - log_total[..., None]).astype(
            jnp.bfloat16
        )
        return (
            running
            + jnp.einsum("bhqk,bkhe->bqhe", chances, blocks[1], preferred_element_type=jnp.float32),
            None,
        )

    return lax.scan(
        weighted_advance,
        jnp.zeros(queries.shape, jnp.float32),
        (key_blocks(keys), key_blocks(values)),
    )[0]


def grad_dots(queries, keys, values, log_total, grad_out):
    questions, tokens, heads, width = queries.shape

    def grad_advance(running, blocks):
        chances = jnp.exp(block_scores(queries, blocks[0]) - log_total[..., None])
        dchance = jnp.einsum(
            "bqhe,bkhe->bhqk", grad_out, blocks[1], preferred_element_type=jnp.float32
        )
        return (running + jnp.sum(chances * dchance, -1), None)

    initial = jnp.zeros((questions, heads, tokens), jnp.float32)
    return lax.scan(grad_advance, initial, (key_blocks(keys), key_blocks(values)))[0]


def cross_back(queries, keys, values, log_total, dots, grad_out, with_keys):
    scale = queries.shape[-1] ** (-0.5)

    def cross_advance(running, blocks):
        chances = jnp.exp(block_scores(queries, blocks[0]) - log_total[..., None])
        dchance = jnp.einsum(
            "bqhe,bkhe->bhqk", grad_out, blocks[1], preferred_element_type=jnp.float32
        )
        dscore = (chances * (dchance - dots[..., None])).astype(jnp.bfloat16)
        running = (
            running
            + jnp.einsum("bhqk,bkhe->bqhe", dscore, blocks[0], preferred_element_type=jnp.float32)
            * scale
        )
        if with_keys:
            dkey = (
                jnp.einsum("bhqk,bqhe->bkhe", dscore, queries, preferred_element_type=jnp.float32)
                * scale
            ).astype(jnp.bfloat16)
            dvalue = jnp.einsum(
                "bhqk,bqhe->bkhe",
                chances.astype(jnp.bfloat16),
                grad_out,
                preferred_element_type=jnp.float32,
            ).astype(jnp.bfloat16)
            return (running, (dkey, dvalue))
        return (running, None)

    query_grad, pieces = lax.scan(
        cross_advance, jnp.zeros(queries.shape, jnp.float32), (key_blocks(keys), key_blocks(values))
    )
    if not with_keys:
        return (query_grad, None)
    questions, length, width = keys.shape
    key_grad = jnp.moveaxis(pieces[0], 0, 1).reshape(questions, length, width)
    value_grad = jnp.moveaxis(pieces[1], 0, 1).reshape(questions, length, width)
    return (query_grad, (key_grad, value_grad))


def general(
    decoder_in,
    encoded,
    cotangent,
    task_ids,
    task_embed,
    gain_self,
    self_query,
    self_key,
    self_value,
    self_output,
    gain_cross,
    cross_query,
    cross_key,
    cross_value,
    cross_output,
    gain_hidden,
    hidden_in,
    hidden_out,
):
    gathered = (
        lax.all_gather(task_embed, ("psg", "batch"), axis=1, tiled=True),
        lax.all_gather(gain_self, ("psg", "batch"), axis=0, tiled=True),
        lax.all_gather(self_query, ("psg", "batch"), axis=0, tiled=True),
        lax.all_gather(self_key, ("psg", "batch"), axis=0, tiled=True),
        lax.all_gather(self_value, ("psg", "batch"), axis=0, tiled=True),
        lax.all_gather(self_output, ("psg", "batch"), axis=0, tiled=True),
        lax.all_gather(gain_cross, ("psg", "batch"), axis=0, tiled=True),
        lax.all_gather(cross_query, ("psg", "batch"), axis=0, tiled=True),
        lax.all_gather(cross_key, ("psg", "batch"), axis=0, tiled=True),
        lax.all_gather(cross_value, ("psg", "batch"), axis=0, tiled=True),
        lax.all_gather(cross_output, ("psg", "batch"), axis=0, tiled=True),
        lax.all_gather(gain_hidden, ("psg", "batch"), axis=0, tiled=True),
    )
    (
        wide_table,
        wide_gain_self,
        wide_self_query,
        wide_self_key,
        wide_self_value,
        wide_self_output,
        wide_gain_cross,
        wide_cross_query,
        wide_cross_key,
        wide_cross_value,
        wide_cross_output,
        wide_gain_hidden,
    ) = gathered
    pieces = (
        lax.all_gather(hidden_in, "batch", axis=0, tiled=True),
        lax.all_gather(hidden_out, "batch", axis=1, tiled=True),
    )
    wide_in, wide_out = (
        lax.all_gather(pieces[0], "psg", axis=1, tiled=True),
        lax.all_gather(pieces[1], "psg", axis=0, tiled=True),
    )
    questions, tokens, width = decoder_in.shape
    rows = questions * tokens
    groups = task_embed.shape[0]
    onehot = (task_ids[:, None] == jnp.arange(groups, dtype=jnp.int32)[None, :]).astype(jnp.float32)
    embed_rows = jnp.dot(onehot, wide_table.astype(jnp.float32), precision=lax.Precision.HIGHEST)
    residual_in = (decoder_in.astype(jnp.float32) + embed_rows[:, None, :]).reshape(rows, width)
    gain_one = wide_gain_self.astype(jnp.float32)
    gain_two = wide_gain_cross.astype(jnp.float32)
    gain_three = wide_gain_hidden.astype(jnp.float32)
    normed_value, factor_one = rms_norm(residual_in, gain_one)
    normed_self = normed_value.astype(jnp.bfloat16)
    query_self = split_heads(matmul(normed_self, wide_self_query).astype(jnp.bfloat16), questions)
    key_self = split_heads(matmul(normed_self, wide_self_key).astype(jnp.bfloat16), questions)
    value_self = split_heads(matmul(normed_self, wide_self_value).astype(jnp.bfloat16), questions)
    causal = jnp.arange(tokens)[:, None] >= jnp.arange(tokens)[None, :]
    scores_self = jnp.where(causal, block_scores(query_self, key_self), MASKED)
    expo = jnp.exp(scores_self - jnp.max(scores_self, -1, keepdims=True))
    chances_self = expo / jnp.sum(expo, -1, keepdims=True)
    chances_low = chances_self.astype(jnp.bfloat16)
    mixed_self = (
        jnp.einsum("bhqk,bkhe->bqhe", chances_low, value_self, preferred_element_type=jnp.float32)
        .astype(jnp.bfloat16)
        .reshape(rows, width)
    )
    after_self = residual_in + matmul(mixed_self, wide_self_output)
    normed_value, factor_two = rms_norm(after_self, gain_two)
    normed_cross = normed_value.astype(jnp.bfloat16)
    query_cross = split_heads(
        matmul(normed_cross, wide_cross_query).astype(jnp.bfloat16), questions
    )
    encoder_rows = encoded.reshape(-1, width)
    key_cross = matmul(encoder_rows, wide_cross_key).astype(jnp.bfloat16).reshape(encoded.shape)
    value_cross = matmul(encoder_rows, wide_cross_value).astype(jnp.bfloat16).reshape(encoded.shape)
    length = encoded.shape[1]
    all_keys, all_values = (
        lax.all_gather(key_cross, "psg", axis=1, tiled=True),
        lax.all_gather(value_cross, "psg", axis=1, tiled=True),
    )
    highest, totals = score_stats(query_cross, all_keys)
    log_total = highest + jnp.log(totals)
    mixed = weighted_values(query_cross, all_keys, all_values, log_total)
    mixed_cross = mixed.astype(jnp.bfloat16).reshape(rows, width)
    after_cross = after_self + matmul(mixed_cross, wide_cross_output)
    normed_value, factor_three = rms_norm(after_cross, gain_three)
    normed_hidden = normed_value.astype(jnp.bfloat16)
    pre_act = matmul(normed_hidden, wide_in)
    activation, gelu_pull = jax.vjp(gelu_tanh, pre_act)
    act_low = activation.astype(jnp.bfloat16)
    hidden_part = matmul(act_low, wide_out)
    result = after_cross + hidden_part
    block_out = result.astype(jnp.bfloat16).reshape(decoder_in.shape)
    psg_count = lax.axis_size("psg")
    row_share = rows // psg_count
    first_row = lax.axis_index("psg") * row_share

    def own(values):
        return lax.dynamic_slice_in_dim(values, first_row, row_share, 0)

    grad_top = cotangent.reshape(rows, width)
    dhidden = outer_cols(grad_top, wide_out)
    dpre = gelu_pull(dhidden)[0].astype(jnp.bfloat16)
    term_out = inner_rows(own(act_low), own(grad_top))
    term_in = inner_rows(own(normed_hidden), own(dpre))
    dnorm_hidden = outer_cols(dpre, wide_in)
    lower, gterm_three = rms_back(after_cross, factor_three, gain_three, dnorm_hidden)
    grad_after_cross = grad_top.astype(jnp.float32) + lower
    dcross = grad_after_cross.astype(jnp.bfloat16)
    term_cross_output = inner_rows(own(mixed_cross), own(dcross))
    dmixed_cross = split_heads(
        outer_cols(dcross, wide_cross_output).astype(jnp.bfloat16), questions
    )
    dots_cross = grad_dots(query_cross, all_keys, all_values, log_total, dmixed_cross)
    query_own, key_pair = cross_back(
        query_cross, key_cross, value_cross, log_total, dots_cross, dmixed_cross, True
    )
    begin = (lax.axis_index("psg") + 1) * length
    span = (psg_count - 1) * length
    other_keys = lax.dynamic_slice_in_dim(jnp.concatenate([all_keys, all_keys], 1), begin, span, 1)
    other_values = lax.dynamic_slice_in_dim(
        jnp.concatenate([all_values, all_values], 1), begin, span, 1
    )
    query_rest = cross_back(
        query_cross, other_keys, other_values, log_total, dots_cross, dmixed_cross, False
    )[0]
    query_grad = query_own + query_rest
    dquery_cross = query_grad.astype(jnp.bfloat16).reshape(rows, width)
    dkey_rows = key_pair[0].reshape(-1, width)
    dvalue_rows = key_pair[1].reshape(-1, width)
    grad_encoded = (
        outer_cols(dkey_rows, wide_cross_key) + outer_cols(dvalue_rows, wide_cross_value)
    ).reshape(encoded.shape)
    term_cross_key = inner_rows(encoder_rows, dkey_rows)
    term_cross_value = inner_rows(encoder_rows, dvalue_rows)
    term_cross_query = inner_rows(own(normed_cross), own(dquery_cross))
    dnorm_cross = outer_cols(dquery_cross, wide_cross_query)
    lower, gterm_two = rms_back(after_self, factor_two, gain_two, dnorm_cross)
    grad_after_self = grad_after_cross + lower
    dself = grad_after_self.astype(jnp.bfloat16)
    term_self_output = inner_rows(own(mixed_self), own(dself))
    dmixed_self = split_heads(outer_cols(dself, wide_self_output).astype(jnp.bfloat16), questions)
    dchance = jnp.einsum(
        "bqhe,bkhe->bhqk", dmixed_self, value_self, preferred_element_type=jnp.float32
    )
    dots_self = jnp.sum(chances_self * dchance, -1, keepdims=True)
    dscore = (chances_self * (dchance - dots_self)).astype(jnp.bfloat16)
    scale = query_self.shape[-1] ** (-0.5)
    dquery_self = (
        (
            jnp.einsum("bhqk,bkhe->bqhe", dscore, key_self, preferred_element_type=jnp.float32)
            * scale
        )
        .astype(jnp.bfloat16)
        .reshape(rows, width)
    )
    dkey_self = (
        (
            jnp.einsum("bhqk,bqhe->bkhe", dscore, query_self, preferred_element_type=jnp.float32)
            * scale
        )
        .astype(jnp.bfloat16)
        .reshape(rows, width)
    )
    dvalue_self = (
        jnp.einsum("bhqk,bqhe->bkhe", chances_low, dmixed_self, preferred_element_type=jnp.float32)
        .astype(jnp.bfloat16)
        .reshape(rows, width)
    )
    dnorm_self = (
        outer_cols(dquery_self, wide_self_query)
        + outer_cols(dkey_self, wide_self_key)
        + outer_cols(dvalue_self, wide_self_value)
    )
    normed_own = own(normed_self)
    term_self_query = inner_rows(normed_own, own(dquery_self))
    term_self_key = inner_rows(normed_own, own(dkey_self))
    term_self_value = inner_rows(normed_own, own(dvalue_self))
    lower, gterm_one = rms_back(residual_in, factor_one, gain_one, dnorm_self)
    grad_decoder = grad_after_self + lower
    row_hot = jnp.repeat(onehot, tokens, 0)
    term_table = lax.dot_general(
        own(row_hot), own(grad_decoder), (((0,), (0,)), ((), ())), precision=lax.Precision.HIGHEST
    )
    sums = (
        lax.psum_scatter(term_table, ("psg", "batch"), scatter_dimension=1, tiled=True),
        lax.psum_scatter(
            jnp.sum(own(gterm_one), 0), ("psg", "batch"), scatter_dimension=0, tiled=True
        ),
        lax.psum_scatter(term_self_query, ("psg", "batch"), scatter_dimension=0, tiled=True),
        lax.psum_scatter(term_self_key, ("psg", "batch"), scatter_dimension=0, tiled=True),
        lax.psum_scatter(term_self_value, ("psg", "batch"), scatter_dimension=0, tiled=True),
        lax.psum_scatter(term_self_output, ("psg", "batch"), scatter_dimension=0, tiled=True),
        lax.psum_scatter(
            jnp.sum(own(gterm_two), 0), ("psg", "batch"), scatter_dimension=0, tiled=True
        ),
        lax.psum_scatter(term_cross_query, ("psg", "batch"), scatter_dimension=0, tiled=True),
        lax.psum_scatter(term_cross_key, ("psg", "batch"), scatter_dimension=0, tiled=True),
        lax.psum_scatter(term_cross_value, ("psg", "batch"), scatter_dimension=0, tiled=True),
        lax.psum_scatter(term_cross_output, ("psg", "batch"), scatter_dimension=0, tiled=True),
        lax.psum_scatter(
            jnp.sum(own(gterm_three), 0), ("psg", "batch"), scatter_dimension=0, tiled=True
        ),
    )
    hidden_pair = (
        lax.psum_scatter(
            term_in.astype(jnp.bfloat16), "psg", scatter_dimension=1, tiled=True
        ).astype(jnp.float32),
        lax.psum_scatter(
            term_out.astype(jnp.bfloat16), "psg", scatter_dimension=0, tiled=True
        ).astype(jnp.float32),
    )
    hidden_grads = (
        lax.psum_scatter(hidden_pair[0], "batch", scatter_dimension=0, tiled=True),
        lax.psum_scatter(hidden_pair[1], "batch", scatter_dimension=1, tiled=True),
    )
    return (
        block_out,
        grad_decoder.reshape(decoder_in.shape),
        grad_encoded,
        sums[0],
        sums[1],
        sums[2],
        sums[3],
        sums[4],
        sums[5],
        sums[6],
        sums[7],
        sums[8],
        sums[9],
        sums[10],
        sums[11],
        hidden_grads[0],
        hidden_grads[1],
    )


def local(psg, batch, *arrays):
    decoder_in, gain = arrays[0], arrays[5]
    if regular(gain.shape[0], psg, batch, decoder_in.shape[1], decoder_in.shape[2]) and decoder_in.shape[0] == 1:
        return fused(psg, batch, *arrays)
    return general(*arrays)


def solution(mesh):
    line, spread = P("batch", None, None), P("batch", "psg", None)
    flat, rows = P(("psg", "batch")), P(("psg", "batch"), None)
    table, wide, tall = P(None, ("psg", "batch")), P("batch", "psg"), P("psg", "batch")
    return jax.shard_map(
        functools.partial(local, mesh.shape["psg"], mesh.shape["batch"]),
        mesh=mesh,
        in_specs=(line, spread, line, P("batch"), table) + ((flat,) + (rows,) * 4) * 2 + (flat, wide, tall),
        out_specs=(line, line, spread, table) + ((flat,) + (rows,) * 4) * 2 + (flat, wide, tall),
        check_vma=False,
    )
```

```python
import functools
import types

import jax
import jax.numpy as jnp
from jax import lax
from jax.experimental import pallas as pl
from jax.experimental.pallas import tpu as pltpu
from jax.sharding import PartitionSpec as P

SPANS = 4
HEADS = 12
PASS_LEN = 192
EPSILON = 1e-06
MASKED = -1000000000.0
LANES = 128
MIB = 2**20
ENCODED_PARTS = 3
PAIRS = 78
LEAVING = 16

F32 = jnp.float32
BF16 = jnp.bfloat16
ID = pl.DeviceIdType.MESH

CK, CV, CO, CQ, SO, SK, SQ, SV = range(8)
GATHER = ((CK, 2, False), (SK, 3, False), (SO, 1, True), (CQ, 1, True), (CO, 1, True))
REDUCE = ((CO, 1, True), (CQ, 2, True), (SK, 3, True), (CK, 1, False), (CV, 1, False))


def nn(former, latter):
    return jnp.dot(former, latter, preferred_element_type=F32)


def nt(former, latter):
    return lax.dot_general(former, latter, (((1,), (1,)), ((), ())), preferred_element_type=F32)


def rms_factor(values):
    return lax.rsqrt(jnp.mean(values * values, -1, keepdims=True) + EPSILON)


def norm_back(values, factor, scales, grad_out):
    scaled = grad_out * scales
    cubed = factor * factor * factor
    return factor * scaled - values * cubed * jnp.mean(scaled * values, -1, keepdims=True)


def lane_is_low():
    return lax.broadcasted_iota(jnp.int32, (1, LANES), 1) < LANES // 2


def stack_heads(pair):
    low = lane_is_low()
    zero = jnp.zeros_like(pair)
    return jnp.concatenate([jnp.where(low, pair, zero), jnp.where(low, zero, pair)], 0)


def merge_heads(stacked):
    half = stacked.shape[0] // 2
    return jnp.where(lane_is_low(), stacked[:half], stacked[half:])


def stack_stat(stats, pair):
    return jnp.concatenate([stats[:, 2 * pair : 2 * pair + 1], stats[:, 2 * pair + 1 : 2 * pair + 2]], 0)


def spread_stat(stats, pair):
    return jnp.where(
        lane_is_low(), stats[:, 2 * pair : 2 * pair + 1], stats[:, 2 * pair + 1 : 2 * pair + 2]
    )


def column_tiles(width, size=256):
    return [slice(first, min(first + size, width)) for first in range(0, width, size)]


def pair_lanes(pair):
    return slice(pair * LANES, (pair + 1) * LANES)


def self_forward(dec, row, g1, wq, wk, wv, wo, g2, res, n1, q, k, v, probs, mix, after, n2):
    x = dec + row
    res[...] = x
    normed = (x * rms_factor(x) * g1).astype(BF16)
    n1[...] = normed
    q[...] = nn(normed, wq).astype(BF16)
    k[...] = nn(normed, wk).astype(BF16)
    v[...] = nn(normed, wv).astype(BF16)
    tokens, width = x.shape
    scale = (width // HEADS) ** (-0.5)
    rows = lax.broadcasted_iota(jnp.int32, (2 * tokens, tokens), 0) % tokens
    causal = rows >= lax.broadcasted_iota(jnp.int32, (2 * tokens, tokens), 1)
    for pair in range(HEADS // 2):
        cols = pair_lanes(pair)
        scores = jnp.where(causal, nt(stack_heads(q[:, cols]), k[:, cols]) * scale, MASKED)
        expo = jnp.exp(scores - jnp.max(scores, -1, keepdims=True))
        chances = expo * (1.0 / jnp.sum(expo, -1, keepdims=True))
        probs[pair] = chances
        mix[:, cols] = merge_heads(nn(chances.astype(BF16), v[:, cols])).astype(BF16)
    y = x + nn(mix[...], wo)
    after[...] = y
    n2[...] = (y * rms_factor(y) * g2).astype(BF16)


def cross_attend(qc, key, val, probs, stat, part):
    tokens, width = qc.shape
    share = tokens // 4
    scale = (width // HEADS) ** (-0.5)
    lane = lax.broadcasted_iota(jnp.int32, (tokens, LANES), 1)
    tops = jnp.zeros((tokens, LANES), F32)
    sums = jnp.ones((tokens, LANES), F32)
    for pair in range(HEADS // 2):
        cols = pair_lanes(pair)
        scores = nt(stack_heads(qc[:, cols] * scale), key[:, cols])
        top = jnp.max(scores, -1, keepdims=True)
        expo = jnp.exp(scores - top)
        total = jnp.sum(expo, -1, keepdims=True)
        low = expo.astype(BF16)
        probs[pair] = low
        mixed = merge_heads(nn(low, val[:, cols]) * (1.0 / total)).astype(BF16)
        for p in range(4):
            part[p // 2, p % 2, :, cols] = mixed[p * share : (p + 1) * share]
        for half in range(2):
            rows = slice(half * tokens, (half + 1) * tokens)
            here = lane == 2 * pair + half
            tops = jnp.where(here, top[rows], tops)
            sums = jnp.where(here, total[rows], sums)
    for p in range(4):
        rows = slice(p * share, (p + 1) * share)
        stat[p // 2, p % 2, :, :LANES] = tops[rows]
        stat[p // 2, p % 2, :, LANES:] = sums[rows]


def join_parts(o_a, s_a, o_b, s_b, out, stat):
    top_a, top_b = s_a[:, :LANES], s_b[:, :LANES]
    top = jnp.maximum(top_a, top_b)
    w_a = jnp.exp(top_a - top) * s_a[:, LANES:]
    w_b = jnp.exp(top_b - top) * s_b[:, LANES:]
    total = w_a + w_b
    inverse = 1.0 / total
    w_a, w_b = w_a * inverse, w_b * inverse
    for pair in range(HEADS // 2):
        cols = pair_lanes(pair)
        mixed = spread_stat(w_a, pair) * o_a[:, cols].astype(F32) + spread_stat(w_b, pair) * o_b[:, cols].astype(F32)
        out[:, cols] = mixed.astype(out.dtype)
    stat[:, :LANES] = top
    stat[:, LANES:] = total


def feed_forward(x, top, w_in, w_out):
    pre = nn(x, w_in)
    root = (2.0 / jnp.pi) ** 0.5
    square = pre * pre
    bend = jnp.tanh(root * (pre + 0.044715 * (square * pre)))
    act = (0.5 * pre * (1.0 + bend)).astype(BF16)
    slope = 0.5 * (1.0 + bend) + 0.5 * pre * (1.0 - bend * bend) * (root * (1.0 + 3 * 0.044715 * square))
    dpre = (nn(top, w_out) * slope).astype(BF16)
    return act, dpre


def head_sums(product):
    lane = lax.broadcasted_iota(jnp.int32, (product.shape[0], LANES), 1)
    sums = jnp.zeros(lane.shape, F32)
    low = lane_is_low()
    for pair in range(HEADS // 2):
        here = product[:, pair_lanes(pair)]
        sums = jnp.where(lane == 2 * pair, jnp.sum(jnp.where(low, here, 0.0), -1, keepdims=True), sums)
        sums = jnp.where(lane == 2 * pair + 1, jnp.sum(jnp.where(low, 0.0, here), -1, keepdims=True), sums)
    return sums


def cross_backward(pair, qc, dmixed, key, val, probs, ratio, dots, part):
    tokens, width = qc.shape
    share = tokens // 4
    scale = (width // HEADS) ** (-0.5)
    cols = pair_lanes(pair)
    q2 = stack_heads(qc[:, cols])
    d2 = stack_heads(dmixed[:, cols])
    chances = probs[pair].astype(F32) * stack_stat(ratio, pair)
    dchance = nt(d2, val[:, cols])
    dscore = (chances * (dchance - stack_stat(dots, pair))).astype(BF16)
    dquery = (merge_heads(nn(dscore, key[:, cols])) * scale).astype(BF16)
    for p in range(4):
        part[p // 2, p % 2, :, cols] = dquery[p * share : (p + 1) * share]
    probs[pair, :LANES] = (nn(q2.T, dscore) * scale).astype(BF16)
    probs[pair, LANES:] = nn(d2.T, chances.astype(BF16)).astype(BF16)


def self_backward(dmixed, q, k, v, probs, dq, dk, dv):
    width = q.shape[1]
    scale = (width // HEADS) ** (-0.5)
    for pair in range(HEADS // 2):
        cols = pair_lanes(pair)
        q2 = stack_heads(q[:, cols])
        d2 = stack_heads(dmixed[:, cols])
        chances = probs[pair]
        dchance = nt(d2, v[:, cols])
        dscore = chances * (dchance - jnp.sum(chances * dchance, -1, keepdims=True))
        low = dscore.astype(BF16)
        dq[:, cols] = (merge_heads(nn(low, k[:, cols])) * scale).astype(BF16)
        dk[:, cols] = (nn(low.T, q2) * scale).astype(BF16)
        dv[:, cols] = nn(chances.astype(BF16).T, d2).astype(BF16)


INPUTS = ["tid", "dec", "cot", "enc", "table", "g_one", "g_two", "g_three", "sq", "sk", "sv", "so", "cq", "co", "ck", "cv", "h_in", "h_out"]
OUTPUTS = ["block_out", "grad_dec", "grad_enc", "g_attn", "g_in", "g_out", "g_vec"]


def buffers(psg, batch, tokens, length, width, owned, hidden):
    spans, pairs, share, half = batch // 2, HEADS // 2, tokens // psg, width // 2
    dma = pltpu.SemaphoreType.DMA
    whole = (tokens, width)
    quad = (2, 2, share)
    band = 2 * owned
    runs = len(GATHER)

    def low(*shape):
        return pltpu.VMEM(shape, BF16)

    def full(*shape):
        return pltpu.VMEM(shape, F32)

    out = dict(
        w=low(8, 2, 2 * batch * owned, width),
        f=low(2, width, hidden // 2),
        m_send=low(4, band, half),
        m_recv=low(4, band, half),
        v_buf=full(4, 8, width),
        v_recv=full(3 + spans, 8, width),
        cots=low(2, tokens, width),
        dec_here=low(tokens, width),
        enc_here=low(length, width),
        block_here=low(*quad, width),
        grad_dec_here=full(*whole),
        grad_enc_here=full(length, width),
        g_attn_here=full(8, owned, width),
        g_in_here=full(width // batch, hidden),
        g_out_here=full(width // batch, hidden),
        g_vec_here=full(8, owned),
        load=dma((3,)),
        store=dma((14,)),
        key=low(length, width),
        val=low(length, width),
        c_probs=low(pairs, 2 * tokens, length),
        s_probs=full(pairs, 2 * tokens, tokens),
        res=full(*whole),
        after=full(*whole),
        n1=low(*whole),
        n2=low(*whole),
        q=low(*whole),
        k=low(*whole),
        v=low(*whole),
        mix=low(*whole),
        qc=low(*whole),
        o_part=low(*quad, width),
        o_stat=full(*quad, 2 * LANES),
        o_core=low(2, share, width),
        o_core_stat=full(2, share, 2 * LANES),
        o_to=low(share, width),
        o_to_stat=full(share, 2 * LANES),
        o_mid=full(share, width),
        o_mid_stat=full(share, 2 * LANES),
        o_x=low(share, width),
        o_x_stat=full(share, 2 * LANES),
        mixed_rows=full(share, width),
        stat_rows=full(share, 2 * LANES),
        after_rows=full(share, width),
        n3=low(2, *quad, width),
        mixc=low(*quad, width),
        log_total=full(*quad, LANES),
        dn=low(2, *quad, width),
        dn_core=low(2, 2, share, width),
        dn_to=low(3, share, width),
        dn_got=low(3, share, width),
        hp=low(2, *quad, width),
        hp_core=low(2, 2, share, width),
        hp_to=low(3, share, width),
        hp_got=low(3, share, width),
        grad_rows=full(share, width),
        dcross=low(*quad, width),
        dq_part=low(*quad, width),
        dq_core=low(2, share, width),
        dq_to=low(share, width),
        dq_x=low(share, width),
        dqc=low(*quad, width),
        dself=low(*quad, width),
        dself_rest=low(*quad, width),
        dq=low(*whole),
        dk=low(*whole),
        dv=low(*whole),
        turned=low(4, width, tokens),
        gf=low(2, width, hidden // 2),
        gkv=low(2, 2, 2 * batch * owned, width),
        kv_core=low(2, 2, batch * owned, width),
        kv_to=low(2, batch * owned, width),
        kv_x=low(2, batch * owned, width),
        g=low(8, batch * owned, width),
        gains=full(8, width),
        t_buf=full(4, 8, width),
        t_recv=full(3 + spans, 8, width),
        f_swap=low(2, width // batch, hidden // 2),
        f_swapped=low(2, width // batch, hidden // 2),
        f_came=low(3, 2, width // spans, hidden // 2),
        f_sum=full(2, width // spans, hidden // 2),
        one_send=dma((LEAVING,)),
        one_recv=dma((PAIRS,)),
        a_recv=dma((sum(1 if joined else 2 for _, _, joined in GATHER) * batch,)),
        a_send=dma((runs, 4)),
        a_core=dma((runs,)),
        w_recv=dma((spans,)),
        w_send=dma((3,)),
        v_sems=dma((2, spans)),
        t_sems=dma((2, spans)),
        f_line=dma((6,)),
    )
    for number, (_, count, y_first) in enumerate(REDUCE):
        rows = -(-count * owned // 16) * 16
        if y_first:
            out[f"r{number}_y"] = low(2, count, band, width)
            out[f"r{number}_one"] = low(count, band, width)
            out[f"r{number}_own"] = full(count * owned, width)
        else:
            out[f"r{number}_one"] = low(2 * band, width)
            out[f"r{number}_two_to"] = low(band, width)
            out[f"r{number}_two"] = low(band, width)
            out[f"r{number}_own"] = full(band, width)
        out[f"r{number}_last_to"] = low(rows, width)
        out[f"r{number}_last"] = low(rows, width)
    return out


def block_kernel(names, psg, batch, *refs):
    r = types.SimpleNamespace(**dict(zip(names, refs, strict=True)))
    index, question = lax.axis_index("psg"), lax.axis_index("batch")
    far, near = question // 2, question % 2
    side, core = index // 2, index % 2
    x_peer = ((1 - side) * 2 + core, question)
    c_peer = (side * 2 + 1 - core, question)
    y_peer = (index, far * 2 + 1 - near)
    d_peer = ((1 - side) * 2 + core, far * 2 + 1 - near)
    places = [far, far + 1 - 2 * (far % 2), lax.rem(far + 2, SPANS), SPANS - 1 - far]
    column = [(index, z * 2 + near) for z in places[1:]]
    one_peer, two_peer = column[0], column[1]
    tokens, width = r.dec_here.shape
    owned = r.sq.shape[0]
    band, quarter, half = 2 * owned, batch * owned, width // 2
    share = tokens // psg
    fan = width // batch
    shards = (r.ck, r.cv, r.co, r.cq, r.so, r.sk, r.sq, r.sv)
    pairs = HEADS // 2

    def aligned(value, to):
        return value if isinstance(value, int) else pl.multiple_of(value, to)

    def span(start, size, to):
        return pl.ds(aligned(start, to), size)

    def lanes(h):
        return span(h * half, half, LANES)

    sent = []

    def go(copy):
        copy.start()
        sent.append(copy)

    def remote(src, dst, send, recv, device):
        return pltpu.make_async_remote_copy(
            src_ref=src, dst_ref=dst, send_sem=send, recv_sem=recv, device_id=device, device_id_type=ID
        )

    numbers = iter(range(PAIRS))
    leaving = []

    def pair(src, dst, device):
        number = next(numbers)
        if number >= LEAVING:
            leaving[number - LEAVING].wait_send()
        copy = remote(src, dst, r.one_send.at[number % LEAVING], r.one_recv.at[number], device)
        copy.start()
        leaving.append(copy)
        return copy

    loads = [
        pltpu.make_async_copy(r.cot, r.cots.at[near], r.load.at[0]),
        pltpu.make_async_copy(r.dec, r.dec_here, r.load.at[1]),
        pltpu.make_async_copy(r.enc, r.enc_here, r.load.at[2]),
    ]
    for copy in loads:
        copy.start()
    stores = []

    def store(src, dst):
        copy = pltpu.make_async_copy(src, dst, r.store.at[len(stores)])
        copy.start()
        stores.append(copy)

    barrier = pltpu.get_barrier_semaphore()
    greeted = column + [y_peer, x_peer, c_peer, d_peer]
    for other in greeted:
        pl.semaphore_signal(barrier, inc=1, device_id=other, device_id_type=ID)
    pl.semaphore_wait(barrier, len(greeted))

    def pack(number):
        first, second = shards[2 * number], shards[2 * number + 1]
        both = jnp.concatenate([first[:, lanes(1 - near)].astype(F32), second[:, lanes(1 - near)].astype(F32)], 0)
        r.m_send[number] = both.astype(BF16)

    def exchange(first, count):
        for number in range(first, first + count):
            pack(number)
        return pair(r.m_send.at[first : first + count], r.m_recv.at[first : first + count], y_peer)

    row = core * quarter + far * band

    def join(number):
        other = r.m_recv[number].astype(F32)
        for part in range(2):
            mine = shards[2 * number + part][:, lanes(near)].astype(F32)
            theirs = other[part * owned : (part + 1) * owned]
            block = jnp.where(near == 0, jnp.concatenate([mine, theirs], 0), jnp.concatenate([theirs, mine], 0))
            r.w[2 * number + part, side, span(row, band, 16), lanes(near)] = block.astype(BF16)

    def unit(run, x, c, z, h):
        first, count, joined = GATHER[run]
        rows = span(c * quarter + z * band, band, 16)
        return r.w.at[first : first + count, slice(None) if joined else x, rows, lanes(h)]

    def landing(run, x, c, z, h):
        return r.a_recv.at[sum(1 if joined else 2 for _, _, joined in GATHER[:run]) * batch + (0 if GATHER[run][2] else x) * batch + z * 2 + h]

    def hand(run, x, c, z, h, kind, device, recv=None):
        spot = unit(run, x, c, z, h)
        remote(spot, spot, r.a_send.at[run, kind], landing(run, x, c, z, h) if recv is None else recv, device).start()

    def landed(run, x, c, z, h):
        spot = unit(run, x, c, z, h)
        remote(spot, spot, r.a_send.at[run, 0], landing(run, x, c, z, h), c_peer).wait_recv()

    held = []

    def wide(run, z, h, hold=False):
        to_x = functools.partial(hand, run, side, core, z, h, 2, x_peer)
        if hold:
            held.append(to_x)
        elif not GATHER[run][2]:
            to_x()
        hand(run, side, core, z, h, 3, c_peer, r.a_core.at[run])

    def offer(run):
        hand(run, side, core, far, near, 0, two_peer)
        hand(run, side, core, far, near, 0, one_peer)
        hand(run, side, core, far, near, 1, y_peer)
        wide(run, far, near)

    def from_y(run, step, hold=False):
        landed(run, side, core, places[step], 1 - near)
        wide(run, places[step], 1 - near, hold)

    def from_line(run, step, hold=False):
        z = places[step]
        landed(run, side, core, z, near)
        if step == 2:
            hand(run, side, core, z, near, 0, one_peer)
        hand(run, side, core, z, near, 1, y_peer)
        wide(run, z, near, hold)

    def from_x(run, step):
        z = places[step]
        for h in (near, 1 - near):
            landed(run, 1 - side, core, z, h)
            hand(run, 1 - side, core, z, h, 3, c_peer, r.a_core.at[run])

    def sent_of(run):
        first, count, joined = GATHER[run]
        lower = r.w.at[first : first + count, slice(None) if joined else 0]
        quarters = (slice(None),) * (2 if joined else 1)
        sizes = [
            lower.at[(*quarters, pl.ds(0, 3 * band), pl.ds(0, half))],
            lower.at[(*quarters, pl.ds(0, quarter), pl.ds(0, half))],
            None if joined else lower.at[(*quarters, pl.ds(0, quarter), slice(None))],
            r.w.at[first : first + count, :, pl.ds(0, quarter), :],
        ]
        for kind, size in enumerate(sizes):
            if size is not None:
                remote(size, size, r.a_send.at[run, kind], r.a_core.at[run], c_peer).wait_send()

    def complete(run):
        first, count, _ = GATHER[run]
        all_of = r.w.at[first : first + count, :, span((1 - core) * quarter, quarter, 16), :]
        remote(all_of, all_of, r.a_send.at[run, 0], r.a_core.at[run], c_peer).wait_recv()

    def matrix(number):
        return r.w[number].reshape(width, width)

    m_kv = exchange(0, 1)
    m_self = exchange(2, 2)
    m_tail = exchange(1, 1)

    def ladder(buf, recv, sems):
        def first():
            return pair(buf.at[0], recv.at[0], c_peer)

        def second(copy):
            copy.wait_recv()
            buf[1] = (buf[0].astype(F32) + recv[0].astype(F32)).astype(buf.dtype)
            return pair(buf.at[1], recv.at[1], x_peer)

        def third(copy):
            copy.wait_recv()
            buf[2] = (buf[1].astype(F32) + recv[1].astype(F32)).astype(buf.dtype)
            return pair(buf.at[2], recv.at[2], y_peer)

        def fourth(copy):
            copy.wait_recv()
            buf[3] = (buf[2].astype(F32) + recv[2].astype(F32)).astype(buf.dtype)
            for z in places[1:]:
                go(remote(buf.at[3], recv.at[3 + far], sems.at[0, z], sems.at[1, far], (index, z * 2 + near)))

        def last():
            total = buf[3].astype(F32)
            for z in places[1:]:
                remote(buf.at[3], recv.at[3 + z], sems.at[0, z], sems.at[1, z], c_peer).wait_recv()
                total = total + recv[3 + z].astype(F32)
            return total

        return first, second, third, fourth, last

    device = index * batch + question
    place = jnp.where(
        lax.broadcasted_iota(jnp.int32, (owned, width), 1)
        == lax.broadcasted_iota(jnp.int32, (owned, width), 0) + device * owned,
        1.0,
        0.0,
    ).astype(BF16)
    r.v_buf[0, 0:3] = nn(r.table[...], place)
    for number, gain in enumerate((r.g_one, r.g_two, r.g_three)):
        r.v_buf[0, 3 + number : 4 + number] = nn(gain[...], place)
    r.v_buf[0, 6:8] = jnp.zeros((2, width), F32)
    v_first, v_second, v_third, v_fourth, v_last = ladder(r.v_buf, r.v_recv, r.v_sems)
    v_copy = v_first()

    m_kv.wait_recv()
    join(0)
    offer(0)
    m_self.wait_recv()
    join(2)
    join(3)
    offer(1)
    m_tail.wait_recv()
    join(1)
    own_tail = r.w.at[CO : CO + 3, side, span(row, band, 16), lanes(near)]
    x_tail = pair(own_tail, own_tail, x_peer)
    v_copy = v_second(v_copy)

    cut = r.f.shape[2]
    other_cols = span((1 - near) * cut, cut, LANES)
    own_cols = span(near * cut, cut, LANES)
    own_fan = span(question * fan, fan, 16)
    r.f[0, own_fan] = r.h_in[:, own_cols]
    r.f[1, own_fan] = r.h_out[:, own_cols]

    def f_unit(z):
        return r.f.at[:, span(z * 2 * fan, 2 * fan, 16), :]

    def f_hand(z, sem, device):
        go(remote(f_unit(z), f_unit(z), sem, r.w_recv.at[z], device))

    def f_landed(step):
        z = places[step]
        remote(f_unit(z), f_unit(z), r.w_send.at[0], r.w_recv.at[z], c_peer).wait_recv()
        if step == 2:
            f_hand(z, r.w_send.at[2], one_peer)

    def near_units(run, hold=False):
        from_y(run, 0, hold)
        from_line(run, 2, hold)
        from_line(run, 1, hold)

    def far_units(run):
        from_line(run, 3)
        from_y(run, 1)
        from_y(run, 2)

    near_units(0)
    far_units(0)
    near_units(1, True)
    x_tail.wait_recv()
    offer(2)
    from_y(0, 3)
    for to_x in held:
        to_x()
    far_units(1)
    near_units(2)
    offer(3)
    v_copy = v_third(v_copy)
    for step in range(3):
        from_x(0, step)
    from_y(1, 3)
    h_copies = [
        pair(r.h_in.at[:, other_cols], r.f.at[0, own_fan], y_peer),
        pair(r.h_out.at[:, other_cols], r.f.at[1, own_fan], y_peer),
    ]
    far_units(2)
    from_x(1, 0)
    offer(4)
    from_x(0, 3)
    near_units(3)
    complete(0)
    loads[2].wait()
    for cols in column_tiles(width):
        r.key[:, cols] = nn(r.enc_here[...], r.w[CK, :, :, cols].reshape(width, -1)).astype(BF16)
        r.val[:, cols] = nn(r.enc_here[...], r.w[CV, :, :, cols].reshape(width, -1)).astype(BF16)
    v_fourth(v_copy)
    from_y(2, 3)
    far_units(3)
    from_x(1, 1)
    from_x(1, 2)
    near_units(4)
    from_y(3, 3)
    from_x(1, 3)
    for copy in h_copies:
        copy.wait_recv()
    f_hand(far, r.w_send.at[0], two_peer)
    f_hand(far, r.w_send.at[1], one_peer)
    loads[0].wait()
    loads[1].wait()
    complete(1)
    complete(2)
    vectors = v_last()

    gains = [vectors[3 + i : 4 + i] for i in range(3)]
    chosen = r.tid[0]
    row_embed = functools.reduce(
        jnp.add, [vectors[i : i + 1] * jnp.where(chosen == i, 1.0, 0.0).astype(F32) for i in range(3)]
    )
    r.gains[0:3] = vectors[3:6]
    self_forward(
        r.dec_here[...].astype(F32), row_embed, gains[0], matrix(SQ), matrix(SK), matrix(SV), matrix(SO), gains[1],
        r.res, r.n1, r.q, r.k, r.v, r.s_probs, r.mix, r.after, r.n2,
    )
    far_units(4)
    cot_copy = pair(r.cots.at[near], r.cots.at[near], y_peer)
    complete(3)
    r.qc[...] = nn(r.n2[...], matrix(CQ)).astype(BF16)

    cross_attend(r.qc, r.key, r.val, r.c_probs, r.o_stat, r.o_part)
    first = [pair(r.o_part.at[:, 1 - core], r.o_core, c_peer), pair(r.o_stat.at[:, 1 - core], r.o_core_stat, c_peer)]
    from_y(4, 3)
    for copy in first:
        copy.wait_recv()
    join_parts(
        r.o_part[1 - side, core], r.o_stat[1 - side, core], r.o_core[1 - side], r.o_core_stat[1 - side],
        r.o_to, r.o_to_stat,
    )
    second = [pair(r.o_to, r.o_x, x_peer), pair(r.o_to_stat, r.o_x_stat, x_peer)]
    join_parts(
        r.o_part[side, core], r.o_stat[side, core], r.o_core[side], r.o_core_stat[side], r.o_mid, r.o_mid_stat
    )
    f_landed(2)
    f_landed(1)
    complete(4)
    for copy in second:
        copy.wait_recv()
    join_parts(r.o_mid[...], r.o_mid_stat[...], r.o_x[...], r.o_x_stat[...], r.mixed_rows, r.stat_rows)
    my_rows = span(index * share, share, 16)
    r.log_total[side, core] = r.stat_rows[:, :LANES] + jnp.log(r.stat_rows[:, LANES:])
    mixed_low = r.mixed_rows[...].astype(BF16)
    r.mixc[side, core] = mixed_low
    y = r.after[my_rows, :] + nn(mixed_low, matrix(CO))
    r.after_rows[...] = y
    r.n3[near, side, core] = (y * rms_factor(y) * r.gains[2:3]).astype(BF16)

    def block8(h, x, c):
        return r.n3.at[h, x, c]

    def spread4(buf):
        spot = buf.at[side, core]
        over_x, over_c = pair(spot, spot, x_peer), pair(spot, spot, c_peer)

        def then():
            over_x.wait_recv()
            onward = buf.at[1 - side, core]
            last = pair(onward, onward, c_peer)

            def end():
                over_c.wait_recv()
                last.wait_recv()

            return end

        return then

    mine = block8(near, side, core)
    to_y, to_x, to_d, to_c = [pair(mine, mine, peer) for peer in (y_peer, x_peer, d_peer, c_peer)]
    onward = [to_c]
    for copy, h, x in ((to_y, 1 - near, side), (to_x, near, 1 - side), (to_d, 1 - near, 1 - side)):
        copy.wait_recv()
        onward.append(pair(block8(h, x, core), block8(h, x, core), c_peer))
    f_landed(3)
    cot_copy.wait_recv()
    for copy in onward:
        copy.wait_recv()

    log_then = spread4(r.log_total)
    mixc_then = spread4(r.mixc)
    x = r.n3[...].reshape(2 * tokens, width)
    top = r.cots[...].reshape(2 * tokens, width)
    act, dpre = feed_forward(x, top, r.f[0], r.f[1])
    r.dn[...] = nt(dpre, r.f[0]).astype(BF16).reshape(r.dn.shape)

    def shrink8(part, got_c, to, got):
        over_c = pair(part.at[:, :, 1 - core], got_c, c_peer)

        def second():
            over_c.wait_recv()

            def total(h, x):
                return part[h, x, core].astype(F32) + got_c[h, x].astype(F32)

            copies = []
            for slot, (h, x, peer) in enumerate(
                ((1 - near, 1 - side, d_peer), (near, 1 - side, x_peer), (1 - near, side, y_peer))
            ):
                to[slot] = total(h, x).astype(BF16)
                copies.append(pair(to.at[slot], got.at[slot], peer))

            def last():
                out = total(near, side)
                for slot, copy in enumerate(copies):
                    copy.wait_recv()
                    out = out + got[slot].astype(F32)
                return out

            return last

        return second

    dn_second = shrink8(r.dn, r.dn_core, r.dn_to, r.dn_got)
    r.hp[...] = nt(act, r.f[1]).astype(BF16).reshape(r.hp.shape)
    dn_last = dn_second()
    hp_second = shrink8(r.hp, r.hp_core, r.hp_to, r.hp_got)
    r.gf[0] = nn(x.T, dpre).astype(BF16)
    r.gf[1] = nn(top.T, act).astype(BF16)

    def line_kit(came, src, sems):
        def over_pair(step):
            slot = step // 2
            return remote(src(places[step]), came.at[slot], sems.at[slot], sems.at[3 + slot], one_peer)

        def over_pairs():
            return remote(src(places[2]), came.at[2], sems.at[2], sems.at[5], two_peer)

        def first():
            go(over_pair(3))
            go(over_pair(1))

        def second(value):
            over_pair(3).wait_recv()
            src(places[2])[...] = (value + came[1].astype(F32)).astype(BF16)
            go(over_pairs())

        def total(value, out):
            over_pair(1).wait_recv()
            both = value + came[0].astype(F32)
            over_pairs().wait_recv()
            out[...] = both + came[2].astype(F32)

        return first, second, total

    def f_piece(z):
        return r.gf.at[:, span(z * 2 * fan, 2 * fan, 16), :]

    f_first, f_second, f_total = line_kit(r.f_came, f_piece, r.f_line)
    f_first()
    log_end = log_then()
    mixc_end = mixc_then()

    upstream = dn_last()
    y = r.after_rows[...]
    factor = rms_factor(y)
    scales = r.gains[2:3]
    gain_three = jnp.sum(upstream * y * factor, 0, keepdims=True)
    grad = r.cots[near, my_rows, :].astype(F32) + norm_back(y, factor, scales, upstream)
    r.grad_rows[...] = grad
    low = grad.astype(BF16)
    r.dcross[side, core] = low
    dcross_then = spread4(r.dcross)
    log_end()
    mixc_end()
    dcross_end = dcross_then()
    dcross_end()
    hp_last = hp_second()

    def rows_of(ref):
        return ref[...].reshape(tokens, ref.shape[-1])

    parity, high = far % 2, far // 2

    def ordered(value, y_first):
        blocks = [(z, h) for z in range(SPANS) for h in range(2)]
        if y_first:
            blocks.sort(key=lambda block: (block[1], block[0] % 2, block[0] // 2))
        else:
            blocks.sort(key=lambda block: (block[0] % 2, block[0] // 2, block[1]))
        parts = [value[(z * 2 + h) * owned : (z * 2 + h + 1) * owned] for z, h in blocks]
        return jnp.concatenate(parts, 0).astype(BF16)

    def last_step(number, mine, theirs, peer):
        first, count, _ = REDUCE[number]
        to, got = getattr(r, f"r{number}_last_to"), getattr(r, f"r{number}_last")
        if to.shape[0] > theirs.shape[0]:
            theirs = jnp.concatenate([theirs, jnp.zeros((to.shape[0] - theirs.shape[0], width), F32)], 0)
        to[...] = theirs.astype(BF16)
        copy = pair(to, got, peer)
        r.g_attn_here[first : first + count] = mine.reshape(count, owned, width)

        def end():
            copy.wait_recv()
            more = got[...].astype(F32)[: count * owned]
            r.g_attn_here[first : first + count] = r.g_attn_here[first : first + count] + more.reshape(count, owned, width)
            store(r.g_attn_here.at[first : first + count], r.g_attn.at[first : first + count])

        return end

    def line_first(number):
        m = REDUCE[number][0]
        one, two_to, two, own = [getattr(r, f"r{number}_{name}") for name in ("one", "two_to", "two", "own")]
        copies = []

        def forward():
            copies.append(pair(r.g.at[m, span((1 - parity) * 2 * band, 2 * band, 16), :], one, one_peer))

        def again():
            copies[0].wait_recv()
            total = r.g[m, span(parity * 2 * band, 2 * band, 16), :].astype(F32) + one[...].astype(F32)
            upper, lower = total[:band], total[band:]
            two_to[...] = jnp.where(high == 0, lower, upper).astype(BF16)
            copies.append(pair(two_to, two, two_peer))
            own[...] = jnp.where(high == 0, upper, lower)

        def finish():
            copies[1].wait_recv()
            total = own[...] + two[...].astype(F32)
            upper, lower = total[:owned], total[owned:]
            return last_step(
                number, jnp.where(near == 0, upper, lower), jnp.where(near == 0, lower, upper), y_peer
            )

        return forward, again, finish

    def y_first(number):
        first, count, _ = REDUCE[number]
        got_y, one = getattr(r, f"r{number}_y"), getattr(r, f"r{number}_one")
        copies = {}

        def piece(h, p):
            return r.g.at[first : first + count, span(h * 2 * band + p * band, band, 16), :]

        def begin(mine):
            p = parity if mine else 1 - parity
            copies[mine] = pair(piece(1 - near, p), got_y.at[1 if mine else 0], y_peer)

        def value(mine):
            copies[mine].wait_recv()
            return piece(near, parity if mine else 1 - parity)[...].astype(F32) + got_y[1 if mine else 0].astype(F32)

        def forward():
            got_y[0] = value(False).astype(BF16)
            copies["one"] = pair(got_y.at[0], one, one_peer)

        def again():
            total = value(True)
            copies["one"].wait_recv()
            total = total + one[...].astype(F32)
            upper = total[:, :owned].reshape(count * owned, width)
            lower = total[:, owned:].reshape(count * owned, width)
            return last_step(
                number, jnp.where(high == 0, upper, lower), jnp.where(high == 0, lower, upper), two_peer
            )

        return begin, forward, again

    own_rows = span(index * quarter, quarter, 16)

    def turn(slot, value):
        r.turned[slot] = value.T
        return r.turned[slot, own_rows, :]

    co_begin, co_forward, co_again = y_first(0)
    so_begin, so_forward, so_again = y_first(1)
    late_begin, late_forward, late_again = y_first(2)
    k_forward, k_again, k_finish = line_first(3)
    v_forward, v_again, v_finish = line_first(4)

    ratio = jnp.exp(rows_of(r.o_stat)[:, :LANES] - rows_of(r.log_total))
    dmixed = nt(rows_of(r.dcross), matrix(CO)).astype(BF16)
    dots = head_sums(dmixed.astype(F32) * rows_of(r.mixc).astype(F32))
    for number in range(pairs):
        cross_backward(
            number, r.qc, dmixed, r.key, r.val, r.c_probs, ratio, dots, r.dq_part
        )
    q_first = pair(r.dq_part.at[:, 1 - core], r.dq_core, c_peer)
    r.g[CO] = ordered(nn(turn(0, rows_of(r.mixc)), rows_of(r.dcross)), True)
    co_begin(False)
    co_begin(True)
    r.key[...] = r.c_probs[:, :LANES].reshape(width, -1).T
    q_first.wait_recv()
    r.dq_to[...] = (r.dq_part[1 - side, core].astype(F32) + r.dq_core[1 - side].astype(F32)).astype(BF16)
    q_second = pair(r.dq_to, r.dq_x, x_peer)
    r.c_probs[:, :LANES] = r.enc_here[...].T.reshape(pairs, LANES, -1)
    kv_other, kv_own = span((1 - core) * quarter, quarter, 16), span(core * quarter, quarter, 16)

    def kv_first(part, ref):
        for cols in column_tiles(width):
            product = nn(r.c_probs[:, :LANES].reshape(width, -1), ref[:, cols])
            r.gkv[part, :, :, cols] = product.astype(BF16).reshape(2, 2 * quarter, -1)
        return pair(r.gkv.at[part, :, kv_other, :], r.kv_core.at[part], c_peer)

    def kv_second(part, copy):
        copy.wait_recv()
        total = r.gkv[part, 1 - side, kv_own, :].astype(F32) + r.kv_core[part, 1 - side].astype(F32)
        r.kv_to[part] = total.astype(BF16)
        return pair(r.kv_to.at[part], r.kv_x.at[part], x_peer)

    def kv_third(part, copy):
        copy.wait_recv()
        total = r.gkv[part, side, kv_own, :].astype(F32) + r.kv_core[part, side].astype(F32)
        r.g[CK + part] = ordered(total + r.kv_x[part].astype(F32), False)

    f_second(f_piece(places[2])[...].astype(F32))
    k_copy = kv_first(0, r.key)
    q_second.wait_recv()
    dq_rows = (
        r.dq_part[side, core].astype(F32) + r.dq_core[side].astype(F32) + r.dq_x[...].astype(F32)
    ).astype(BF16)
    r.dqc[side, core] = dq_rows
    upstream = nt(dq_rows, matrix(CQ))
    y = r.after[my_rows, :]
    factor = rms_factor(y)
    gain_two = jnp.sum(upstream * y * factor, 0, keepdims=True)
    grad = r.grad_rows[...] + norm_back(y, factor, r.gains[1:2], upstream)
    low = grad.astype(BF16)
    r.dself[side, core] = low
    dself_then = spread4(r.dself)
    r.dself_rest[side, core] = (grad - low.astype(F32)).astype(BF16)
    dqc_then = spread4(r.dqc)
    r.val[...] = r.c_probs[:, LANES:].reshape(width, -1).T
    dself_end = dself_then()
    co_forward()
    k_copy = kv_second(0, k_copy)
    v_copy = kv_first(1, r.val)
    dself_end()
    dqc_end = dqc_then()

    dself = rows_of(r.dself)
    r.g[SO] = ordered(nn(turn(1, r.mix[...]), dself), True)
    dmixed = nt(dself, matrix(SO)).astype(BF16)
    dqc_end()
    r.g[CQ] = ordered(nn(turn(2, r.n2[...]), rows_of(r.dqc)), True)
    so_begin(False)
    v_copy = kv_second(1, v_copy)
    rest_then = spread4(r.dself_rest)
    co_end = co_again()
    self_backward(dmixed, r.q, r.k, r.v, r.s_probs, r.dq, r.dk, r.dv)
    kv_third(0, k_copy)
    k_forward()
    normed = turn(3, r.n1[...])
    for number, ref in ((SQ, r.dq), (SK, r.dk), (SV, r.dv)):
        r.g[number] = ordered(nn(normed, ref[...]), True)
    late_begin(False)
    so_begin(True)
    so_forward()
    late_begin(True)

    f_total(f_piece(far)[...].astype(F32), r.f_sum)
    both = r.f_sum[...]
    upper, lower = both[:, :fan], both[:, fan:]
    r.f_swap[...] = jnp.where(near == 0, lower, upper).astype(BF16)
    f_copy = pair(r.f_swap, r.f_swapped, y_peer)
    kept = jnp.where(near == 0, upper, lower)
    r.g_in_here[:, own_cols] = kept[0]
    r.g_out_here[:, own_cols] = kept[1]

    upstream = nt(r.dq[...], matrix(SQ)) + nt(r.dk[...], matrix(SK)) + nt(r.dv[...], matrix(SV))
    kv_third(1, v_copy)
    k_again()
    v_forward()
    late_forward()
    rest_then()()
    x = r.res[...]
    factor = rms_factor(x)
    grad = dself.astype(F32) + rows_of(r.dself_rest).astype(F32) + norm_back(x, factor, r.gains[0:1], upstream)
    r.grad_dec_here[...] = grad
    store(r.grad_dec_here, r.grad_dec)
    mine = lax.broadcasted_iota(jnp.int32, (tokens, 1), 0) // share == index
    task = jnp.sum(jnp.where(mine, grad, 0.0), 0, keepdims=True)
    r.t_buf[0, 0:3] = jnp.concatenate([task * jnp.where(chosen == i, 1.0, 0.0).astype(F32) for i in range(3)], 0)
    r.t_buf[0, 3:4] = jnp.sum(jnp.where(mine, upstream * x * factor, 0.0), 0, keepdims=True)
    r.t_buf[0, 4:5] = gain_two
    r.t_buf[0, 5:6] = gain_three
    r.t_buf[0, 6:8] = jnp.zeros((2, width), F32)
    t_first, t_second, t_third, t_fourth, t_last = ladder(r.t_buf, r.t_recv, r.t_sems)
    t_copy = t_first()
    so_end = so_again()
    hidden = hp_last()
    r.block_here[side, core] = (r.after_rows[...] + hidden).astype(BF16)
    out_then = spread4(r.block_here)
    t_copy = t_second(t_copy)
    def encoded_columns(cols):
        r.grad_enc_here[:, cols] = nt(r.key[...], matrix(CK)[cols]) + nt(r.val[...], matrix(CV)[cols])

    tiles = column_tiles(width)
    encoded_columns(tiles[0])
    t_copy = t_third(t_copy)
    out_end = out_then()
    v_again()
    k_end = k_finish()
    t_fourth(t_copy)
    for cols in tiles[1:-1]:
        encoded_columns(cols)
    late_end = late_again()
    v_end = v_finish()
    encoded_columns(tiles[-1])
    store(r.grad_enc_here, r.grad_enc)
    co_end()
    so_end()
    out_end()
    for p in range(psg):
        store(r.block_here.at[p // 2, p % 2], r.block_out.at[p])
    f_copy.wait_recv()
    r.g_in_here[:, other_cols] = r.f_swapped[0].astype(F32)
    r.g_out_here[:, other_cols] = r.f_swapped[1].astype(F32)
    store(r.g_in_here, r.g_in)
    store(r.g_out_here, r.g_out)
    r.g_vec_here[...] = lax.dot_general(
        t_last(), place.astype(F32), (((1,), (1,)), ((), ())), precision=lax.Precision.HIGHEST
    )
    store(r.g_vec_here, r.g_vec)
    k_end()
    v_end()
    late_end()
    for copy in stores:
        copy.wait()
    for run in range(len(GATHER)):
        sent_of(run)
    for copy in sent + leaving[-LEAVING:]:
        copy.wait_send()


def settle_kernel(block_out, grad_dec, grad_enc, g_attn, g_in, g_out, g_vec, *rest):
    outs, vectors, here, sems = rest[:13], rest[13:17], rest[17:23], rest[23]
    rows = grad_enc.shape[0] // ENCODED_PARTS
    parts = [pl.ds(number * rows, rows) for number in range(ENCODED_PARTS)]
    moves = [(grad_enc.at[part], here[0].at[part], [outs[2].at[part]]) for part in parts]
    moves += [
        (block_out, here[1], [outs[0]]),
        (grad_dec, here[2], [outs[1]]),
        (g_in, here[4], [outs[11]]),
        (g_out, here[5], [outs[12]]),
        (g_attn, here[3], outs[3:11]),
    ]
    arrivals = [
        pltpu.make_async_copy(source, spot, sems.at[0, number]) for number, (source, spot, _) in enumerate(moves)
    ]
    for copy in arrivals:
        copy.start()
    first = 0
    for out in vectors:
        out[...] = g_vec[first : first + out.shape[0]]
        first += out.shape[0]
    departures = []
    for copy, (_, spot, places) in zip(arrivals, moves, strict=True):
        copy.wait()
        for number, out in enumerate(places):
            source = spot if len(places) == 1 else spot.at[number]
            departures.append(pltpu.make_async_copy(source, out, sems.at[1, len(departures)]))
            departures[-1].start()
    for copy in departures:
        copy.wait()


def regular(owned, psg, batch, tokens, width):
    return psg == 4 and batch == 2 * SPANS and owned % 8 == 0 and tokens % 128 == 0 and (width // 2) % LANES == 0


def fused(psg, batch, decoder_in, encoded, cotangent, task_ids, task_embed, gain_self, self_query, self_key, self_value,
          self_output, gain_cross, cross_query, cross_key, cross_value, cross_output, gain_hidden, hidden_in, hidden_out):
    _, tokens, width = decoder_in.shape
    length = encoded.shape[1]
    groups, owned = task_embed.shape
    hidden = hidden_in.shape[1]
    scratch = buffers(psg, batch, tokens, length, width, owned, hidden)
    names = INPUTS + OUTPUTS + list(scratch)
    vmem = pl.BlockSpec(memory_space=pltpu.VMEM)
    hbm = pl.BlockSpec(memory_space=pl.ANY)
    block_out, grad_decoder, grad_encoded, g_attn, g_in, g_out, g_vec = pl.pallas_call(
        functools.partial(block_kernel, names, psg, batch),
        out_shape=(
            jax.ShapeDtypeStruct((psg,) + (tokens // psg, width), BF16),
            jax.ShapeDtypeStruct((tokens, width), F32),
            jax.ShapeDtypeStruct((length, width), F32),
            jax.ShapeDtypeStruct((8, owned, width), F32),
            jax.ShapeDtypeStruct((width // batch, hidden), F32),
            jax.ShapeDtypeStruct((width // batch, hidden), F32),
            jax.ShapeDtypeStruct((8, owned), F32),
        ),
        in_specs=[pl.BlockSpec(memory_space=pltpu.SMEM)] + [hbm] * 3 + [vmem] * (len(INPUTS) - 4),
        out_specs=[hbm] * len(OUTPUTS),
        scratch_shapes=list(scratch.values()),
        compiler_params=pltpu.CompilerParams(collective_id=0, has_side_effects=True, vmem_limit_bytes=56 * MIB),
        name="decoder_block",
    )(task_ids, decoder_in[0], cotangent[0], encoded[0], task_embed, gain_self[None],
      gain_cross[None], gain_hidden[None], self_query, self_key, self_value, self_output,
      cross_query, cross_output, cross_key, cross_value, hidden_in, hidden_out.T)
    shapes = [(tokens, width), (tokens, width), (length, width)] + [(owned, width)] * 8 + [(width // batch, hidden)] * 2
    small = [(groups, owned)] + [(1, owned)] * 3
    outs = pl.pallas_call(
        settle_kernel,
        out_shape=tuple(
            jax.ShapeDtypeStruct(shape, F32 if number else BF16) for number, shape in enumerate(shapes + small)
        ),
        in_specs=[hbm] * 6 + [vmem],
        out_specs=[hbm] * len(shapes) + [vmem] * len(small),
        scratch_shapes=[
            pltpu.VMEM((length, width), F32),
            pltpu.VMEM((tokens, width), BF16),
            pltpu.VMEM((tokens, width), F32),
            pltpu.VMEM((8, owned, width), F32),
            pltpu.VMEM((width // batch, hidden), F32),
            pltpu.VMEM((width // batch, hidden), F32),
            pltpu.SemaphoreType.DMA((2, len(shapes) + ENCODED_PARTS)),
        ],
        compiler_params=pltpu.CompilerParams(vmem_limit_bytes=60 * MIB),
        name="settle",
    )(block_out.reshape(tokens, width), grad_decoder, grad_encoded, g_attn, g_in, g_out, g_vec)
    block_out, grad_decoder, grad_encoded = outs[:3]
    g_attn, (g_in, g_out) = outs[3:11], outs[11:13]
    table, gain_one, gain_two, gain_three = outs[13:]
    return (
        block_out[None],
        grad_decoder[None],
        grad_encoded[None],
        table,
        gain_one[0],
        g_attn[SQ],
        g_attn[SK],
        g_attn[SV],
        g_attn[SO],
        gain_two[0],
        g_attn[CQ],
        g_attn[CK],
        g_attn[CV],
        g_attn[CO],
        gain_three[0],
        g_in,
        g_out.T,
    )


def rms_norm(values, scales):
    factor = lax.rsqrt(jnp.mean(values * values, -1, keepdims=True) + EPSILON)
    return (values * factor * scales, factor)


def rms_back(values, factor, scales, grad_out):
    scaled = grad_out * scales
    cubed = factor * factor * factor
    lower = factor * scaled - values * cubed * jnp.mean(scaled * values, -1, keepdims=True)
    return (lower, grad_out * values * factor)


def gelu_tanh(values):
    return jax.nn.gelu(values, approximate=True)


def matmul(former, latter):
    return jnp.dot(former, latter, preferred_element_type=jnp.float32)


def inner_rows(former, latter):
    return lax.dot_general(
        former, latter, (((0,), (0,)), ((), ())), preferred_element_type=jnp.float32
    )


def outer_cols(former, latter):
    return lax.dot_general(
        former, latter, (((1,), (1,)), ((), ())), preferred_element_type=jnp.float32
    )


def split_heads(values, questions):
    return values.reshape(questions, values.shape[0] // questions, HEADS, values.shape[1] // HEADS)


def key_blocks(values):
    questions, length, width = values.shape
    shaped = values.reshape(questions, length // PASS_LEN, PASS_LEN, HEADS, width // HEADS)
    return jnp.moveaxis(shaped, 1, 0)


def block_scores(queries, key_block):
    scale = queries.shape[-1] ** (-0.5)
    return (
        jnp.einsum("bqhe,bkhe->bhqk", queries, key_block, preferred_element_type=jnp.float32)
        * scale
    )


def score_stats(queries, keys):
    questions, tokens, heads, width = queries.shape
    initial = (
        jnp.full((questions, heads, tokens), -1e30, jnp.float32),
        jnp.zeros((questions, heads, tokens), jnp.float32),
    )

    def score_advance(running, key_block):
        scores = block_scores(queries, key_block)
        highest = jnp.maximum(running[0], jnp.max(scores, -1))
        totals = running[1] * jnp.exp(running[0] - highest) + jnp.sum(
            jnp.exp(scores - highest[..., None]), -1
        )
        return ((highest, totals), None)

    return lax.scan(score_advance, initial, key_blocks(keys))[0]


def weighted_values(queries, keys, values, log_total):

    def weighted_advance(running, blocks):
        chances = jnp.exp(block_scores(queries, blocks[0]) - log_total[..., None]).astype(
            jnp.bfloat16
        )
        return (
            running
            + jnp.einsum("bhqk,bkhe->bqhe", chances, blocks[1], preferred_element_type=jnp.float32),
            None,
        )

    return lax.scan(
        weighted_advance,
        jnp.zeros(queries.shape, jnp.float32),
        (key_blocks(keys), key_blocks(values)),
    )[0]


def grad_dots(queries, keys, values, log_total, grad_out):
    questions, tokens, heads, width = queries.shape

    def grad_advance(running, blocks):
        chances = jnp.exp(block_scores(queries, blocks[0]) - log_total[..., None])
        dchance = jnp.einsum(
            "bqhe,bkhe->bhqk", grad_out, blocks[1], preferred_element_type=jnp.float32
        )
        return (running + jnp.sum(chances * dchance, -1), None)

    initial = jnp.zeros((questions, heads, tokens), jnp.float32)
    return lax.scan(grad_advance, initial, (key_blocks(keys), key_blocks(values)))[0]


def cross_back(queries, keys, values, log_total, dots, grad_out, with_keys):
    scale = queries.shape[-1] ** (-0.5)

    def cross_advance(running, blocks):
        chances = jnp.exp(block_scores(queries, blocks[0]) - log_total[..., None])
        dchance = jnp.einsum(
            "bqhe,bkhe->bhqk", grad_out, blocks[1], preferred_element_type=jnp.float32
        )
        dscore = (chances * (dchance - dots[..., None])).astype(jnp.bfloat16)
        running = (
            running
            + jnp.einsum("bhqk,bkhe->bqhe", dscore, blocks[0], preferred_element_type=jnp.float32)
            * scale
        )
        if with_keys:
            dkey = (
                jnp.einsum("bhqk,bqhe->bkhe", dscore, queries, preferred_element_type=jnp.float32)
                * scale
            ).astype(jnp.bfloat16)
            dvalue = jnp.einsum(
                "bhqk,bqhe->bkhe",
                chances.astype(jnp.bfloat16),
                grad_out,
                preferred_element_type=jnp.float32,
            ).astype(jnp.bfloat16)
            return (running, (dkey, dvalue))
        return (running, None)

    query_grad, pieces = lax.scan(
        cross_advance, jnp.zeros(queries.shape, jnp.float32), (key_blocks(keys), key_blocks(values))
    )
    if not with_keys:
        return (query_grad, None)
    questions, length, width = keys.shape
    key_grad = jnp.moveaxis(pieces[0], 0, 1).reshape(questions, length, width)
    value_grad = jnp.moveaxis(pieces[1], 0, 1).reshape(questions, length, width)
    return (query_grad, (key_grad, value_grad))


def general(
    decoder_in,
    encoded,
    cotangent,
    task_ids,
    task_embed,
    gain_self,
    self_query,
    self_key,
    self_value,
    self_output,
    gain_cross,
    cross_query,
    cross_key,
    cross_value,
    cross_output,
    gain_hidden,
    hidden_in,
    hidden_out,
):
    gathered = (
        lax.all_gather(task_embed, ("psg", "batch"), axis=1, tiled=True),
        lax.all_gather(gain_self, ("psg", "batch"), axis=0, tiled=True),
        lax.all_gather(self_query, ("psg", "batch"), axis=0, tiled=True),
        lax.all_gather(self_key, ("psg", "batch"), axis=0, tiled=True),
        lax.all_gather(self_value, ("psg", "batch"), axis=0, tiled=True),
        lax.all_gather(self_output, ("psg", "batch"), axis=0, tiled=True),
        lax.all_gather(gain_cross, ("psg", "batch"), axis=0, tiled=True),
        lax.all_gather(cross_query, ("psg", "batch"), axis=0, tiled=True),
        lax.all_gather(cross_key, ("psg", "batch"), axis=0, tiled=True),
        lax.all_gather(cross_value, ("psg", "batch"), axis=0, tiled=True),
        lax.all_gather(cross_output, ("psg", "batch"), axis=0, tiled=True),
        lax.all_gather(gain_hidden, ("psg", "batch"), axis=0, tiled=True),
    )
    (
        wide_table,
        wide_gain_self,
        wide_self_query,
        wide_self_key,
        wide_self_value,
        wide_self_output,
        wide_gain_cross,
        wide_cross_query,
        wide_cross_key,
        wide_cross_value,
        wide_cross_output,
        wide_gain_hidden,
    ) = gathered
    pieces = (
        lax.all_gather(hidden_in, "batch", axis=0, tiled=True),
        lax.all_gather(hidden_out, "batch", axis=1, tiled=True),
    )
    wide_in, wide_out = (
        lax.all_gather(pieces[0], "psg", axis=1, tiled=True),
        lax.all_gather(pieces[1], "psg", axis=0, tiled=True),
    )
    questions, tokens, width = decoder_in.shape
    rows = questions * tokens
    groups = task_embed.shape[0]
    onehot = (task_ids[:, None] == jnp.arange(groups, dtype=jnp.int32)[None, :]).astype(jnp.float32)
    embed_rows = jnp.dot(onehot, wide_table.astype(jnp.float32), precision=lax.Precision.HIGHEST)
    residual_in = (decoder_in.astype(jnp.float32) + embed_rows[:, None, :]).reshape(rows, width)
    gain_one = wide_gain_self.astype(jnp.float32)
    gain_two = wide_gain_cross.astype(jnp.float32)
    gain_three = wide_gain_hidden.astype(jnp.float32)
    normed_value, factor_one = rms_norm(residual_in, gain_one)
    normed_self = normed_value.astype(jnp.bfloat16)
    query_self = split_heads(matmul(normed_self, wide_self_query).astype(jnp.bfloat16), questions)
    key_self = split_heads(matmul(normed_self, wide_self_key).astype(jnp.bfloat16), questions)
    value_self = split_heads(matmul(normed_self, wide_self_value).astype(jnp.bfloat16), questions)
    causal = jnp.arange(tokens)[:, None] >= jnp.arange(tokens)[None, :]
    scores_self = jnp.where(causal, block_scores(query_self, key_self), MASKED)
    expo = jnp.exp(scores_self - jnp.max(scores_self, -1, keepdims=True))
    chances_self = expo / jnp.sum(expo, -1, keepdims=True)
    chances_low = chances_self.astype(jnp.bfloat16)
    mixed_self = (
        jnp.einsum("bhqk,bkhe->bqhe", chances_low, value_self, preferred_element_type=jnp.float32)
        .astype(jnp.bfloat16)
        .reshape(rows, width)
    )
    after_self = residual_in + matmul(mixed_self, wide_self_output)
    normed_value, factor_two = rms_norm(after_self, gain_two)
    normed_cross = normed_value.astype(jnp.bfloat16)
    query_cross = split_heads(
        matmul(normed_cross, wide_cross_query).astype(jnp.bfloat16), questions
    )
    encoder_rows = encoded.reshape(-1, width)
    key_cross = matmul(encoder_rows, wide_cross_key).astype(jnp.bfloat16).reshape(encoded.shape)
    value_cross = matmul(encoder_rows, wide_cross_value).astype(jnp.bfloat16).reshape(encoded.shape)
    length = encoded.shape[1]
    all_keys, all_values = (
        lax.all_gather(key_cross, "psg", axis=1, tiled=True),
        lax.all_gather(value_cross, "psg", axis=1, tiled=True),
    )
    highest, totals = score_stats(query_cross, all_keys)
    log_total = highest + jnp.log(totals)
    mixed = weighted_values(query_cross, all_keys, all_values, log_total)
    mixed_cross = mixed.astype(jnp.bfloat16).reshape(rows, width)
    after_cross = after_self + matmul(mixed_cross, wide_cross_output)
    normed_value, factor_three = rms_norm(after_cross, gain_three)
    normed_hidden = normed_value.astype(jnp.bfloat16)
    pre_act = matmul(normed_hidden, wide_in)
    activation, gelu_pull = jax.vjp(gelu_tanh, pre_act)
    act_low = activation.astype(jnp.bfloat16)
    hidden_part = matmul(act_low, wide_out)
    result = after_cross + hidden_part
    block_out = result.astype(jnp.bfloat16).reshape(decoder_in.shape)
    psg_count = lax.axis_size("psg")
    row_share = rows // psg_count
    first_row = lax.axis_index("psg") * row_share

    def own(values):
        return lax.dynamic_slice_in_dim(values, first_row, row_share, 0)

    grad_top = cotangent.reshape(rows, width)
    dhidden = outer_cols(grad_top, wide_out)
    dpre = gelu_pull(dhidden)[0].astype(jnp.bfloat16)
    term_out = inner_rows(own(act_low), own(grad_top))
    term_in = inner_rows(own(normed_hidden), own(dpre))
    dnorm_hidden = outer_cols(dpre, wide_in)
    lower, gterm_three = rms_back(after_cross, factor_three, gain_three, dnorm_hidden)
    grad_after_cross = grad_top.astype(jnp.float32) + lower
    dcross = grad_after_cross.astype(jnp.bfloat16)
    term_cross_output = inner_rows(own(mixed_cross), own(dcross))
    dmixed_cross = split_heads(
        outer_cols(dcross, wide_cross_output).astype(jnp.bfloat16), questions
    )
    dots_cross = grad_dots(query_cross, all_keys, all_values, log_total, dmixed_cross)
    query_own, key_pair = cross_back(
        query_cross, key_cross, value_cross, log_total, dots_cross, dmixed_cross, True
    )
    begin = (lax.axis_index("psg") + 1) * length
    span = (psg_count - 1) * length
    other_keys = lax.dynamic_slice_in_dim(jnp.concatenate([all_keys, all_keys], 1), begin, span, 1)
    other_values = lax.dynamic_slice_in_dim(
        jnp.concatenate([all_values, all_values], 1), begin, span, 1
    )
    query_rest = cross_back(
        query_cross, other_keys, other_values, log_total, dots_cross, dmixed_cross, False
    )[0]
    query_grad = query_own + query_rest
    dquery_cross = query_grad.astype(jnp.bfloat16).reshape(rows, width)
    dkey_rows = key_pair[0].reshape(-1, width)
    dvalue_rows = key_pair[1].reshape(-1, width)
    grad_encoded = (
        outer_cols(dkey_rows, wide_cross_key) + outer_cols(dvalue_rows, wide_cross_value)
    ).reshape(encoded.shape)
    term_cross_key = inner_rows(encoder_rows, dkey_rows)
    term_cross_value = inner_rows(encoder_rows, dvalue_rows)
    term_cross_query = inner_rows(own(normed_cross), own(dquery_cross))
    dnorm_cross = outer_cols(dquery_cross, wide_cross_query)
    lower, gterm_two = rms_back(after_self, factor_two, gain_two, dnorm_cross)
    grad_after_self = grad_after_cross + lower
    dself = grad_after_self.astype(jnp.bfloat16)
    term_self_output = inner_rows(own(mixed_self), own(dself))
    dmixed_self = split_heads(outer_cols(dself, wide_self_output).astype(jnp.bfloat16), questions)
    dchance = jnp.einsum(
        "bqhe,bkhe->bhqk", dmixed_self, value_self, preferred_element_type=jnp.float32
    )
    dots_self = jnp.sum(chances_self * dchance, -1, keepdims=True)
    dscore = (chances_self * (dchance - dots_self)).astype(jnp.bfloat16)
    scale = query_self.shape[-1] ** (-0.5)
    dquery_self = (
        (
            jnp.einsum("bhqk,bkhe->bqhe", dscore, key_self, preferred_element_type=jnp.float32)
            * scale
        )
        .astype(jnp.bfloat16)
        .reshape(rows, width)
    )
    dkey_self = (
        (
            jnp.einsum("bhqk,bqhe->bkhe", dscore, query_self, preferred_element_type=jnp.float32)
            * scale
        )
        .astype(jnp.bfloat16)
        .reshape(rows, width)
    )
    dvalue_self = (
        jnp.einsum("bhqk,bqhe->bkhe", chances_low, dmixed_self, preferred_element_type=jnp.float32)
        .astype(jnp.bfloat16)
        .reshape(rows, width)
    )
    dnorm_self = (
        outer_cols(dquery_self, wide_self_query)
        + outer_cols(dkey_self, wide_self_key)
        + outer_cols(dvalue_self, wide_self_value)
    )
    normed_own = own(normed_self)
    term_self_query = inner_rows(normed_own, own(dquery_self))
    term_self_key = inner_rows(normed_own, own(dkey_self))
    term_self_value = inner_rows(normed_own, own(dvalue_self))
    lower, gterm_one = rms_back(residual_in, factor_one, gain_one, dnorm_self)
    grad_decoder = grad_after_self + lower
    row_hot = jnp.repeat(onehot, tokens, 0)
    term_table = lax.dot_general(
        own(row_hot), own(grad_decoder), (((0,), (0,)), ((), ())), precision=lax.Precision.HIGHEST
    )
    sums = (
        lax.psum_scatter(term_table, ("psg", "batch"), scatter_dimension=1, tiled=True),
        lax.psum_scatter(
            jnp.sum(own(gterm_one), 0), ("psg", "batch"), scatter_dimension=0, tiled=True
        ),
        lax.psum_scatter(term_self_query, ("psg", "batch"), scatter_dimension=0, tiled=True),
        lax.psum_scatter(term_self_key, ("psg", "batch"), scatter_dimension=0, tiled=True),
        lax.psum_scatter(term_self_value, ("psg", "batch"), scatter_dimension=0, tiled=True),
        lax.psum_scatter(term_self_output, ("psg", "batch"), scatter_dimension=0, tiled=True),
        lax.psum_scatter(
            jnp.sum(own(gterm_two), 0), ("psg", "batch"), scatter_dimension=0, tiled=True
        ),
        lax.psum_scatter(term_cross_query, ("psg", "batch"), scatter_dimension=0, tiled=True),
        lax.psum_scatter(term_cross_key, ("psg", "batch"), scatter_dimension=0, tiled=True),
        lax.psum_scatter(term_cross_value, ("psg", "batch"), scatter_dimension=0, tiled=True),
        lax.psum_scatter(term_cross_output, ("psg", "batch"), scatter_dimension=0, tiled=True),
        lax.psum_scatter(
            jnp.sum(own(gterm_three), 0), ("psg", "batch"), scatter_dimension=0, tiled=True
        ),
    )
    hidden_pair = (
        lax.psum_scatter(
            term_in.astype(jnp.bfloat16), "psg", scatter_dimension=1, tiled=True
        ).astype(jnp.float32),
        lax.psum_scatter(
            term_out.astype(jnp.bfloat16), "psg", scatter_dimension=0, tiled=True
        ).astype(jnp.float32),
    )
    hidden_grads = (
        lax.psum_scatter(hidden_pair[0], "batch", scatter_dimension=0, tiled=True),
        lax.psum_scatter(hidden_pair[1], "batch", scatter_dimension=1, tiled=True),
    )
    return (
        block_out,
        grad_decoder.reshape(decoder_in.shape),
        grad_encoded,
        sums[0],
        sums[1],
        sums[2],
        sums[3],
        sums[4],
        sums[5],
        sums[6],
        sums[7],
        sums[8],
        sums[9],
        sums[10],
        sums[11],
        hidden_grads[0],
        hidden_grads[1],
    )


def local(psg, batch, *arrays):
    decoder_in, gain = arrays[0], arrays[5]
    if regular(gain.shape[0], psg, batch, decoder_in.shape[1], decoder_in.shape[2]) and decoder_in.shape[0] == 1:
        return fused(psg, batch, *arrays)
    return general(*arrays)


def solution(mesh):
    line, spread = P("batch", None, None), P("batch", "psg", None)
    flat, rows = P(("psg", "batch")), P(("psg", "batch"), None)
    table, wide, tall = P(None, ("psg", "batch")), P("batch", "psg"), P("psg", "batch")
    return jax.shard_map(
        functools.partial(local, mesh.shape["psg"], mesh.shape["batch"]),
        mesh=mesh,
        in_specs=(line, spread, line, P("batch"), table) + ((flat,) + (rows,) * 4) * 2 + (flat, wide, tall),
        out_specs=(line, line, spread, table) + ((flat,) + (rows,) * 4) * 2 + (flat, wide, tall),
        check_vma=False,
    )
```
